128 devices in a mesh: seq: 16 (over y, z_hi, core), batch: 8 (over z_lo, x).
Axes of the slice: x: 4, y: 4, z: 4 (z_hi: 2, z_lo: 2; z = z_hi * 2 + z_lo), core: 2. Of those that a mesh axis runs over, the one named last changes fastest.
Arguments:
- tokens: bfloat16 [8, 4096, 768], P('batch', 'seq'), may hold values from -6 to 6
- cotangent: bfloat16 [8, 4096, 768], P('batch', 'seq'), may hold values from -6 to 6
- ln1_gain: float32 [768], replicated, may hold values from 0.1 to 1.9
- ln1_shift: float32 [768], replicated, may hold values from -3 to 3
- w_qkv: bfloat16 [768, 2304], replicated, may hold values from -0.3125 to 0.3125
- b_query: float32 [768], replicated, may hold values from -3 to 3
- b_value: float32 [768], replicated, may hold values from -3 to 3
- w_out: bfloat16 [768, 768], replicated, may hold values from -0.875 to 0.875
- b_out: float32 [768], replicated, may hold values from -3 to 3
- ln2_gain: float32 [768], replicated, may hold values from 0.1 to 1.9
- ln2_shift: float32 [768], replicated, may hold values from -3 to 3
- w_up: bfloat16 [768, 3072], replicated, may hold values from -0.21875 to 0.21875
- b_up: float32 [3072], replicated, may hold values from -3 to 3
- w_down: bfloat16 [3072, 768], replicated, may hold values from -0.109375 to 0.109375
- b_down: float32 [768], replicated, may hold values from -3 to 3
Outputs:
- output: bfloat16 [8, 4096, 768], P('batch', 'seq')
- grad_tokens: float32 [8, 4096, 768], P('batch', 'seq')
- grad_ln1_gain: float32 [768], replicated
- grad_ln1_shift: float32 [768], replicated
- grad_w_qkv: float32 [768, 2304], replicated
- grad_b_query: float32 [768], replicated
- grad_b_value: float32 [768], replicated
- grad_w_out: float32 [768, 768], replicated
- grad_b_out: float32 [768], replicated
- grad_ln2_gain: float32 [768], replicated
- grad_ln2_shift: float32 [768], replicated
- grad_w_up: float32 [768, 3072], replicated
- grad_b_up: float32 [3072], replicated
- grad_w_down: float32 [3072, 768], replicated
- grad_b_down: float32 [768], replicated
The draws below stay inside these ranges and needn't reach their ends.
All inputs are finite; a program needn't handle non-finite values.
Results may differ from the reference program's by a relative error of at most 0.019.
Values may be sent and summed in bfloat16 or wider, within the bound.
No kernel may reach another device: no remote copies, remote signals or barrier semaphores. Data moves between devices by JAX's collectives and lax.ppermute only.
A program may use at most 192 MiB of HBM per device.

```python
import math
import jax
import jax.numpy as jnp
from jax import lax

D = 768
H = 12
HD = 64
FF = 3072
LENGTH = 4096
SEQS = 8


def levels(rng, shape, shards, least, high):
    level, own = 1.0, jax.random.fold_in(rng, 6)
    for position, blocks in shards:
        heights = jnp.exp(jax.random.uniform(jax.random.fold_in(own, position), (blocks,), jnp.float32, least / len(shards), high / len(shards)))
        level = level * jnp.repeat(heights, shape[position] // blocks).reshape([-1 if axis == position else 1 for axis in range(len(shape))])
    return level


def centred(key, shape, scale, bound, pieces=(), kind=jnp.bfloat16):
    loudness = levels(key, shape, pieces, -0.22, 0.18) if pieces else 1.0
    result = jax.random.normal(key, shape, jnp.float32) * scale * loudness
    return jnp.minimum(jnp.maximum(result, -bound), bound).astype(kind)


def setup_inputs(seed: int = 0) -> dict:
    key_of = jax.random.split(jax.random.key(seed), 16)
    return {
        "tokens": centred(key_of[0], (SEQS, LENGTH, D), 1.0, 6.0, ((0, 8), (1, 16))),
        "cotangent": centred(key_of[1], (SEQS, LENGTH, D), 1.0, 6.0, ((0, 8), (1, 16))),
        "ln1_gain": jnp.clip(1.0 + 0.18 * jax.random.normal(key_of[2], (D,), jnp.float32), 0.1, 1.9),
        "ln1_shift": centred(key_of[3], (D,), 0.5, 3.0, (), jnp.float32),
        "w_qkv": centred(key_of[4], (D, 3 * D), (D // 2) ** -0.5, 0.3125),
        "b_query": centred(key_of[5], (D,), 0.5, 3.0, (), jnp.float32),
        "b_value": centred(key_of[6], (D,), 0.5, 3.0, (), jnp.float32),
        "w_out": centred(key_of[7], (D, D), (D // 16) ** -0.5, 0.875),
        "b_out": centred(key_of[8], (D,), 0.5, 3.0, (), jnp.float32),
        "ln2_gain": jnp.clip(1.0 + 0.18 * jax.random.normal(key_of[9], (D,), jnp.float32), 0.1, 1.9),
        "ln2_shift": centred(key_of[10], (D,), 0.5, 3.0, (), jnp.float32),
        "w_up": centred(key_of[11], (D, FF), D ** -0.5, 0.21875),
        "b_up": centred(key_of[12], (FF,), 0.5, 3.0, (), jnp.float32),
        "w_down": centred(key_of[13], (FF, D), FF ** -0.5, 0.109375),
        "b_down": centred(key_of[14], (D,), 0.5, 3.0, (), jnp.float32),
    }


@jax.custom_vjp
def low(v):
    return lax.optimization_barrier(v.astype(jnp.bfloat16)).astype(jnp.float32)

@jax.custom_vjp
def low_back(v):
    return v

def low_keep(v):
    return (low(v), None)

def low_pass(kept, grad):
    return (grad,)

def back_keep(v):
    return (v, None)

def back_low(kept, grad):
    return (low(grad),)
low.defvjp(low_keep, low_pass)
low_back.defvjp(back_keep, back_low)

def layer_norm(values, gain, shift):
    center = values - lax.optimization_barrier(jnp.mean(values, axis=-1, keepdims=True))
    spread = lax.optimization_barrier(jnp.mean(center * center, axis=-1, keepdims=True))
    return center * lax.rsqrt(spread + 1e-05) * gain + shift

def product(left, right):
    return jnp.dot(left, right, precision=lax.Precision.HIGHEST)

def attention(queries, keys, values):
    block = math.gcd(LENGTH, 512)
    count = LENGTH // block
    positions = jnp.arange(LENGTH, dtype=jnp.int32)

    @jax.checkpoint
    def one_block(args):
        query_block, first = args
        scores = jnp.einsum('qhd,khd->hqk', query_block, keys, precision=lax.Precision.HIGHEST) * 0.125
        scores = low_back(scores)
        query_pos = first + jnp.arange(block, dtype=jnp.int32)
        allowed = positions[None, :] <= query_pos[:, None]
        scores = jnp.where(allowed[None], scores, -1e+30)
        weights = jax.nn.softmax(scores, axis=-1)
        return jnp.einsum('hqk,khd->qhd', low(weights), values, precision=lax.Precision.HIGHEST)
    starts = jnp.arange(count, dtype=jnp.int32) * block
    outputs = lax.map(one_block, (queries.reshape(count, block, H, HD), starts))
    return outputs.reshape(LENGTH, H * HD)

def sequence_forward(params, row):
    gain_one, shift_one, w_qkv, b_query, b_value, w_out, b_out, gain_two, shift_two, w_up, b_up, w_down, b_down = params
    hidden_one = low(layer_norm(row, gain_one, shift_one))
    bias_full = jnp.concatenate([b_query, jnp.zeros((D,), jnp.float32), b_value])
    projected = low(low_back(product(hidden_one, w_qkv) + bias_full))
    queries = projected[:, :D].reshape(LENGTH, H, HD)
    keys = projected[:, D:2 * D].reshape(LENGTH, H, HD)
    values = projected[:, 2 * D:].reshape(LENGTH, H, HD)
    attended = low(low_back(attention(queries, keys, values)))
    branch = low_back(product(attended, w_out) + b_out)
    middle = row + branch
    hidden_two = low(layer_norm(middle, gain_two, shift_two))
    inner = low_back(product(hidden_two, w_up) + b_up)
    activated = low(jax.nn.gelu(inner, approximate=True))
    return middle + product(activated, w_down) + b_down

def reference(tokens, cotangent, ln1_gain, ln1_shift, w_qkv, b_query, b_value, w_out, b_out, ln2_gain, ln2_shift, w_up, b_up, w_down, b_down):
    params = tuple((p.astype(jnp.float32) for p in (ln1_gain, ln1_shift, w_qkv, b_query, b_value, w_out, b_out, ln2_gain, ln2_shift, w_up, b_up, w_down, b_down)))
    inputs = tokens.astype(jnp.float32)
    seeds = cotangent.astype(jnp.float32)

    def whole(params, inputs):
        return lax.map(lambda row: sequence_forward(params, row), inputs)
    outputs, pullback = jax.vjp(whole, params, inputs)
    grads, grad_inputs = pullback(seeds)
    g_gain_one, g_shift_one, g_qkv, g_query, g_value, g_out, g_bout, g_gain_two, g_shift_two, g_up, g_bup, g_down, g_bdown = grads
    return (outputs.astype(jnp.bfloat16), grad_inputs, g_gain_one, g_shift_one, g_qkv, g_query, g_value, g_out, g_bout, g_gain_two, g_shift_two, g_up, g_bup, g_down, g_bdown)
```

```python
import jax
import jax.numpy as jnp
from jax import lax
from jax.experimental import pallas as pl
from jax.experimental.pallas import tpu as pltpu
from jax.sharding import PartitionSpec as P

H = 12
HD = 64
LOG2E = 1.4426950408889634
BF = jnp.bfloat16
F32 = jnp.float32


def shift_pairs(axis, step):
    pairs = []
    for s in range(16):
        for b in range(8):
            y, z, c, x = s // 4, (s // 2 % 2) * 2 + b // 4, s % 2, b % 4
            if axis == "y":
                y = (y + step) % 4
            elif axis == "z":
                z = (z + step) % 4
            elif axis == "x":
                x = (x + step) % 4
            else:
                c = c ^ step
            source = (y * 4 + (z // 2) * 2 + c) * 8 + (z % 2) * 4 + x
            pairs.append((source, s * 8 + b))
    return pairs


def fetch(array, axis, step):
    return lax.ppermute(array, ("seq", "batch"), shift_pairs(axis, step))


def reduce_scatter(array, axis, index):
    count = array.shape[0]
    total = lax.dynamic_index_in_dim(array, index, 0, keepdims=False).astype(F32)
    for step in range(1, count):
        target = lax.rem(index + step, count)
        piece = lax.dynamic_index_in_dim(array, target, 0, keepdims=False)
        total = total + fetch(piece, axis, count - step).astype(F32)
    return total.astype(array.dtype)


def all_gather(array, axis, index, count):
    pieces = [array] + [fetch(array, axis, step) for step in range(1, count)]
    return roll_slots(pieces, index)


def roll_slots(pieces, index):
    count = len(pieces)
    stacked = jnp.stack(pieces + pieces[:-1])
    return lax.dynamic_slice_in_dim(stacked, lax.rem(count - index, count), count, 0)


def sum_all(vector):
    vector = vector + fetch(vector, "c", 1)
    for axis in ("y", "z", "x"):
        vector = (vector + fetch(vector, axis, 2)) + (fetch(vector, axis, 1) + fetch(vector, axis, 3))
    return vector


def nt(left, right):
    return lax.dot_general(left, right, (((1,), (1,)), ((), ())), preferred_element_type=F32)


def fwd_kernel(slot_of, block_of, q_ref, kv_ref, kvt_ref, o_ref, o32_ref, lse_ref, m_ref, l_ref, acc_ref):
    me = pl.program_id(0)
    count = block_of[me]
    m_ref[...] = jnp.full(m_ref.shape, -1e30, F32)
    l_ref[...] = jnp.zeros(l_ref.shape, F32)
    acc_ref[...] = jnp.zeros(acc_ref.shape, F32)

    def step(slot, masked):
        for h in range(3):
            q = q_ref[0, :, h * HD : (h + 1) * HD]
            k = kv_ref[slot, :, h * 128 : h * 128 + HD]
            s = nt(k, q) * LOG2E
            if masked:
                keys = lax.broadcasted_iota(jnp.int32, s.shape, 0)
                queries = lax.broadcasted_iota(jnp.int32, s.shape, 1)
                s = jnp.where(keys <= queries, s, -1e30)
            old = m_ref[h]
            new = jnp.maximum(old, jnp.max(s, axis=0, keepdims=True))
            p = jnp.exp2(s - new)
            factor = jnp.exp2(old - new)
            m_ref[h] = new
            l_ref[h] = l_ref[h] * factor + jnp.sum(p, axis=0, keepdims=True)
            vt = kvt_ref[slot, h * 128 + HD : (h + 1) * 128, :]
            acc_ref[h] = acc_ref[h] * factor + jnp.dot(vt, p.astype(BF), preferred_element_type=F32)

    step(me * 4, True)

    def body(b, carry):
        step(slot_of[b], False)
        return carry

    lax.fori_loop(0, count, body, 0)
    for h in range(3):
        o = (acc_ref[h] / l_ref[h]).T
        o32_ref[0, :, h * HD : (h + 1) * HD] = o
        o_ref[0, :, h * HD : (h + 1) * HD] = o.astype(BF)
        lse_ref[0, h : h + 1, :] = m_ref[h] + jnp.log2(l_ref[h])


def bwd_kernel(slot_of, block_of, q_ref, do_ref, o32_ref, lse_ref, kv_ref, kvt_ref, dq_ref, dkv_ref, qdo_ref, delta_ref, dqt_ref):
    me = pl.program_id(0)
    count = block_of[me]

    @pl.when(me == 0)
    def _():
        dkv_ref[...] = jnp.zeros(dkv_ref.shape, F32)

    zero = jnp.zeros((256, HD), BF)
    for h in range(3):
        do = do_ref[0, :, h * HD : (h + 1) * HD]
        qdo_ref[h, :256, :] = jnp.concatenate([q_ref[0, :, h * HD : (h + 1) * HD], zero], axis=1)
        qdo_ref[h, 256:, :] = jnp.concatenate([zero, do], axis=1)
        prod = do.astype(F32) * o32_ref[0, :, h * HD : (h + 1) * HD]
        delta_ref[h] = jnp.sum(prod.T, axis=0, keepdims=True)
    dqt_ref[...] = jnp.zeros(dqt_ref.shape, F32)

    def step(slot, masked):
        for h in range(3):
            qdo = qdo_ref[h]
            both = nt(kv_ref[slot, :, h * 128 : (h + 1) * 128], qdo)
            s = both[:, :256] * LOG2E - lse_ref[0, h : h + 1, :]
            p = jnp.exp2(s)
            if masked:
                keys = lax.broadcasted_iota(jnp.int32, s.shape, 0)
                queries = lax.broadcasted_iota(jnp.int32, s.shape, 1)
                p = jnp.where(keys <= queries, p, 0.0)
            ds = (p * (both[:, 256:] - delta_ref[h])).astype(BF)
            w = jnp.concatenate([ds, p.astype(BF)], axis=1)
            dkv_ref[slot, :, h * 128 : (h + 1) * 128] += jnp.dot(w, qdo, preferred_element_type=F32)
            kt = kvt_ref[slot, h * 128 : h * 128 + HD, :]
            dqt_ref[h] += jnp.dot(kt, ds, preferred_element_type=F32)

    step(me * 4, True)

    def body(b, carry):
        step(slot_of[b], False)
        return carry

    lax.fori_loop(0, count, body, 0)
    for h in range(3):
        dq_ref[0, :, h * HD : (h + 1) * HD] = (dqt_ref[h].T * 0.125).astype(BF)


def whole(shape):
    return pl.BlockSpec(shape, lambda i, *_: (0,) * len(shape))


def of_slot(shape):
    return pl.BlockSpec((1,) + shape, lambda i, *_: (i,) + (0,) * len(shape))


def attend(slot_of, block_of, q, kv, kvt):
    return pl.pallas_call(
        fwd_kernel,
        grid_spec=pltpu.PrefetchScalarGridSpec(
            num_scalar_prefetch=2,
            grid=(4,),
            in_specs=[of_slot((256, 192)), whole((16, 256, 384)), whole((16, 384, 256))],
            out_specs=[of_slot((256, 192)), of_slot((256, 192)), of_slot((3, 256))],
            scratch_shapes=[
                pltpu.VMEM((3, 1, 256), F32),
                pltpu.VMEM((3, 1, 256), F32),
                pltpu.VMEM((3, HD, 256), F32),
            ],
        ),
        out_shape=[
            jax.ShapeDtypeStruct((4, 256, 192), BF),
            jax.ShapeDtypeStruct((4, 256, 192), F32),
            jax.ShapeDtypeStruct((4, 3, 256), F32),
        ],
        compiler_params=pltpu.CompilerParams(vmem_limit_bytes=48 * 2**20),
        name="attend",
    )(slot_of, block_of, q, kv, kvt)


def attend_back(slot_of, block_of, q, do, o32, lse, kv, kvt):
    return pl.pallas_call(
        bwd_kernel,
        grid_spec=pltpu.PrefetchScalarGridSpec(
            num_scalar_prefetch=2,
            grid=(4,),
            in_specs=[
                of_slot((256, 192)),
                of_slot((256, 192)),
                of_slot((256, 192)),
                of_slot((3, 256)),
                whole((16, 256, 384)),
                whole((16, 384, 256)),
            ],
            out_specs=[of_slot((256, 192)), whole((16, 256, 384))],
            scratch_shapes=[
                pltpu.VMEM((3, 512, 128), BF),
                pltpu.VMEM((3, 1, 256), F32),
                pltpu.VMEM((3, HD, 256), F32),
            ],
        ),
        out_shape=[
            jax.ShapeDtypeStruct((4, 256, 192), BF),
            jax.ShapeDtypeStruct((16, 256, 384), F32),
        ],
        compiler_params=pltpu.CompilerParams(vmem_limit_bytes=56 * 2**20),
        name="attend_back",
    )(slot_of, block_of, q, do, o32, lse, kv, kvt)


def layer_norm(values, gain, shift):
    center = values - jnp.mean(values, axis=-1, keepdims=True)
    spread = jnp.mean(center * center, axis=-1, keepdims=True)
    return center * lax.rsqrt(spread + 1e-05) * gain + shift


def shards(
    tokens,
    cotangent,
    ln1_gain,
    ln1_shift,
    w_qkv,
    b_query,
    b_value,
    w_out,
    b_out,
    ln2_gain,
    ln2_shift,
    w_up,
    b_up,
    w_down,
    b_down,
):
    seq, batch = lax.axis_index("seq"), lax.axis_index("batch")
    y, zh, c = seq // 4, lax.rem(seq // 2, 2), lax.rem(seq, 2)
    z, x = zh * 2 + batch // 4, lax.rem(batch, 4)

    inputs = tokens[0].astype(F32)
    normed_one, back_one = jax.vjp(layer_norm, inputs, ln1_gain, ln1_shift)
    h1 = normed_one.astype(BF)

    held = {(0, 0): h1}
    for dy in (1, 2, 3):
        held[dy, 0] = fetch(h1, "y", dy)
    held[0, 1] = fetch(h1, "z", 2)
    held[2, 1] = fetch(held[0, 1], "y", 2)
    for dy in (1, 3):
        held[dy, 1] = fetch(held[dy, 0], "z", 2)
    order = [(dy, dz) for dy in range(4) for dz in range(2)]
    mine = jnp.stack([held[p] for p in order])
    other = fetch(mine, "c", 1)
    h1_all = jnp.stack([mine, other], axis=1).reshape(16, 256, 768)

    dy, dz, dc = jnp.meshgrid(jnp.arange(4), jnp.arange(2), jnp.arange(2), indexing="ij")
    blocks = (lax.rem(y + dy, 4) * 4 + (zh ^ dz) * 2 + (c ^ dc)).reshape(16).astype(jnp.int32)
    slot_of = jnp.zeros((16,), jnp.int32).at[blocks].set(jnp.arange(16, dtype=jnp.int32))
    block_of = blocks[::4]

    w_group = lax.dynamic_slice_in_dim(w_qkv.reshape(768, 3, 768), y * 192, 192, 2)
    bq_group = lax.dynamic_slice_in_dim(b_query, y * 192, 192, 0)
    bv_group = lax.dynamic_slice_in_dim(b_value, y * 192, 192, 0)
    w_kv = jnp.stack([w_group[:, 1].reshape(768, 3, HD), w_group[:, 2].reshape(768, 3, HD)], axis=2).reshape(768, 384)
    b_kv = jnp.stack([jnp.zeros((3, HD), F32), bv_group.reshape(3, HD)], axis=1).reshape(384)
    kv = (jnp.einsum("btf,fc->btc", h1_all, w_kv, preferred_element_type=F32) + b_kv).astype(BF)
    kvt = jnp.swapaxes(kv, 1, 2)
    h1_query = h1_all[::4]
    q = jnp.einsum("btf,fc->btc", h1_query, w_group[:, 0], preferred_element_type=F32) + bq_group
    q = q.astype(BF) * jnp.asarray(0.125, BF)

    o, o32, lse = attend(slot_of, block_of, q, kv, kvt)

    heads = [o[0]] + [fetch(o[4 - e], "y", e) for e in (1, 2, 3)]
    attended = roll_slots(heads, y).transpose(1, 0, 2).reshape(256, 768)

    middle = inputs + jnp.dot(attended, w_out, preferred_element_type=F32) + b_out
    normed_two, back_two = jax.vjp(layer_norm, middle, ln2_gain, ln2_shift)
    h2 = normed_two.astype(BF)
    inner = jnp.dot(h2, w_up, preferred_element_type=F32) + b_up
    activated, back_gelu = jax.vjp(lambda value: jax.nn.gelu(value, approximate=True), inner)
    g = activated.astype(BF)
    result = middle + jnp.dot(g, w_down, preferred_element_type=F32) + b_down
    dy_low = cotangent[0]
    seed = dy_low.astype(F32)
    grad_b_down = jnp.sum(seed, axis=0)
    grad_act = jnp.dot(dy_low, w_down.T, preferred_element_type=F32)
    du = back_gelu(grad_act)[0].astype(BF)
    grad_b_up = jnp.sum(du.astype(F32), axis=0)
    grad_h2 = jnp.dot(du, w_up.T, preferred_element_type=F32)
    grad_mid_norm, grad_gain_two, grad_shift_two = back_two(grad_h2)
    grad_middle = seed + grad_mid_norm
    da = grad_middle.astype(BF)
    grad_b_out = jnp.sum(da.astype(F32), axis=0)
    do = jnp.dot(da, w_out.T, preferred_element_type=F32).astype(BF)

    do_groups = do.reshape(256, 4, 192).transpose(1, 0, 2)
    do_mine = [lax.dynamic_index_in_dim(do_groups, y, 0, keepdims=False)]
    for e in (1, 2, 3):
        piece = lax.dynamic_index_in_dim(do_groups, lax.rem(y + 4 - e, 4), 0, keepdims=False)
        do_mine.append(fetch(piece, "y", e))
    do_mine = jnp.stack(do_mine)

    def halves(array):
        parts = array.reshape(256, 2, -1)
        own = lax.dynamic_index_in_dim(parts, c, 1, keepdims=False)
        return jnp.concatenate([own, fetch(lax.dynamic_index_in_dim(parts, 1 - c, 1, keepdims=False), "c", 1)])

    def pair(array):
        return jnp.concatenate([array, fetch(array, "c", 1)])

    def tn(left, right):
        return lax.dot_general(left, right, (((0,), (0,)), ((), ())), preferred_element_type=F32)

    gw_down = tn(halves(g), pair(dy_low)).astype(BF)
    gw_up = tn(halves(du), pair(h2)).astype(BF)
    gw_out = tn(halves(attended), pair(da)).astype(BF)

    places = {"x": x, "y": y, "z": z}

    def sum_weights(array, axes):
        shape = array.shape
        for axis in axes:
            array = reduce_scatter(array.reshape(4, -1, 768), axis, places[axis])
        for axis in reversed(axes):
            array = all_gather(array, axis, places[axis], 4).reshape(-1, 768)
        return array

    def join_cores(array):
        return all_gather(array, "c", c, 2).reshape(-1, 768)

    gw_down = join_cores(sum_weights(gw_down, ("x", "y", "z"))).astype(F32)
    gw_up = join_cores(sum_weights(gw_up, ("z", "x", "y"))).T.astype(F32)
    gw_out = join_cores(sum_weights(gw_out, ("y", "x", "z"))).astype(F32)

    dq, dkv32 = attend_back(slot_of, block_of, q, do_mine, o32, lse, kv, kvt)
    dkv = dkv32.astype(BF)

    gq = tn(dq.reshape(1024, 192), h1_query.reshape(1024, 768))
    gkv = tn(dkv.reshape(4096, 384), h1_all.reshape(4096, 768))
    gkv = gkv.reshape(3, 2, HD, 768)
    gw = jnp.concatenate([gq, gkv[:, 0].reshape(192, 768), gkv[:, 1].reshape(192, 768)]).astype(BF)
    gw = reduce_scatter(gw.reshape(2, 288, 768), "c", c)
    gw = reduce_scatter(gw.reshape(4, 72, 768), "x", x)
    gw = reduce_scatter(jnp.pad(gw, ((0, 24), (0, 0))).reshape(4, 24, 768), "z", z)
    gw = all_gather(gw, "z", z, 4).reshape(96, 768)[:72]
    gw = all_gather(gw, "x", x, 4).reshape(288, 768)
    gw = all_gather(gw, "c", c, 2).reshape(576, 768)
    gw = all_gather(gw, "y", y, 4).reshape(4, 3, 192, 768)
    gw_qkv = gw.transpose(1, 0, 2, 3).reshape(2304, 768).T.astype(F32)

    parts = dkv.reshape(4, 2, 2, 256, 384)
    parts = parts[:, :, 0].astype(F32) + fetch(parts[:, :, 1], "c", 1).astype(F32)
    parts = parts.astype(BF)
    parts = parts[:, 0].astype(F32) + fetch(parts[:, 1], "z", 2).astype(F32)
    parts = parts.astype(BF)
    parts = jnp.concatenate([dq, parts], axis=2)
    groups = [parts[0]] + [fetch(parts[4 - e], "y", e) for e in (1, 2, 3)]
    groups = roll_slots(groups, y)
    dq_rows = groups[:, :, :192].transpose(1, 0, 2).reshape(256, 768)
    dkv_rows = groups[:, :, 192:].reshape(4, 256, 3, 2, HD).transpose(1, 3, 0, 2, 4).reshape(256, 2, 768)
    dk_rows = dkv_rows[:, 0]
    dv_rows = dkv_rows[:, 1]
    dqkv = jnp.concatenate([dq_rows, dk_rows, dv_rows], axis=1)
    grad_b_query = jnp.sum(dq_rows.astype(F32), axis=0)
    grad_b_value = jnp.sum(dv_rows.astype(F32), axis=0)
    grad_h1 = jnp.dot(dqkv, w_qkv.T, preferred_element_type=F32)
    grad_in_norm, grad_gain_one, grad_shift_one = back_one(grad_h1)
    grad_inputs = grad_middle + grad_in_norm

    small = jnp.stack([grad_gain_one, grad_shift_one, grad_b_query, grad_b_value, grad_b_out, grad_gain_two, grad_shift_two, grad_b_down])
    small = jnp.concatenate([small, grad_b_up.reshape(4, 768)])
    small = sum_all(small)
    return (
        result.astype(BF)[None],
        grad_inputs[None],
        small[0],
        small[1],
        gw_qkv,
        small[2],
        small[3],
        gw_out,
        small[4],
        small[5],
        small[6],
        gw_up,
        small[8:12].reshape(3072),
        gw_down,
        small[7],
    )


def solution(mesh):
    split = P("batch", "seq", None)
    return jax.shard_map(
        shards,
        mesh=mesh,
        in_specs=(split, split) + (P(),) * 13,
        out_specs=(split, split) + (P(),) * 13,
        check_vma=False,
    )
```

```python
import jax
import jax.numpy as jnp
from jax import lax
from jax.experimental import pallas as pl
from jax.experimental.pallas import tpu as pltpu
from jax.sharding import PartitionSpec as P

HD = 64
LOG2E = 1.4426950408889634
BF = jnp.bfloat16
F32 = jnp.float32
MIB = 2**20
COST = pl.CostEstimate(flops=1000, bytes_accessed=1000, transcendentals=0)


def nt(left, right):
    return lax.dot_general(left, right, (((1,), (1,)), ((), ())), preferred_element_type=F32)


def tn(left, right):
    return lax.dot_general(left, right, (((0,), (0,)), ((), ())), preferred_element_type=F32)


def whole(shape):
    return pl.BlockSpec(shape, lambda i, *_: (0,) * len(shape))


def of_slot(shape):
    return pl.BlockSpec((1,) + shape, lambda i, *_: (i,) + (0,) * len(shape))


def causal(scores, other):
    keys = lax.broadcasted_iota(jnp.int32, scores.shape, 0)
    queries = lax.broadcasted_iota(jnp.int32, scores.shape, 1)
    return jnp.where(keys <= queries, scores, other)


def query_y(place):
    return lax.rem(place[0] + pl.program_id(0), 4)


def slot(place, y):
    return lax.rem(y + 4 - place[0], 4)


def softmax_step(q_ref, m_ref, l_ref, acc_ref, blocks, masks):
    scores = []
    for h in range(3):
        q = q_ref[0, :, h * HD : (h + 1) * HD]
        row = [nt(block[:, h * 128 : h * 128 + HD], q) * LOG2E for block in blocks]
        scores.append([mask(s, -1e30) if mask else s for s, mask in zip(row, masks)])
    probs = []
    for h in range(3):
        old = m_ref[0, h : h + 1, :]
        new = old
        for s in scores[h]:
            new = jnp.maximum(new, jnp.max(s, axis=0, keepdims=True))
        factor = jnp.exp2(old - new)
        m_ref[0, h : h + 1, :] = new
        row = [jnp.exp2(s - new) for s in scores[h]]
        l_ref[0, h : h + 1, :] = l_ref[0, h : h + 1, :] * factor + sum(jnp.sum(p, axis=0, keepdims=True) for p in row)
        probs.append((row, factor))
    for h in range(3):
        row, factor = probs[h]
        acc = acc_ref[0, h] * factor
        for block, p in zip(blocks, row):
            acc = acc + tn(block[:, h * 128 + HD : (h + 1) * 128], p.astype(BF))
        acc_ref[0, h] = acc


def attend_near_kernel(place, q_ref, kv0_ref, kv1_ref, m_ref, l_ref, acc_ref):
    own = pl.program_id(0)
    m_ref[...] = jnp.full(m_ref.shape, -1e30, F32)
    l_ref[...] = jnp.zeros(l_ref.shape, F32)
    acc_ref[...] = jnp.zeros(acc_ref.shape, F32)

    def beside(scores, other):
        return jnp.where(place[2] == 1, scores, other)

    softmax_step(q_ref, m_ref, l_ref, acc_ref, [kv0_ref[own], kv1_ref[own]], [causal, beside])

    def body(y, carry):
        at = slot(place, y)
        softmax_step(q_ref, m_ref, l_ref, acc_ref, [kv0_ref[at], kv1_ref[at]], [None, None])
        return carry

    lax.fori_loop(0, query_y(place), body, 0)


def attend_far_kernel(place, q_ref, kv0_ref, kv1_ref, m_in, l_in, acc_in, o_ref, o32_ref, lse_ref, m_ref, l_ref, acc_ref):
    m_ref[...] = m_in[...]
    l_ref[...] = l_in[...]
    acc_ref[...] = acc_in[...]

    def body(y, carry):
        at = slot(place, y)
        softmax_step(q_ref, m_ref, l_ref, acc_ref, [kv0_ref[at], kv1_ref[at]], [None, None])
        return carry

    lax.fori_loop(0, query_y(place) + place[1], body, 0)
    for h in range(3):
        o = (acc_ref[0, h] / l_ref[0, h : h + 1, :]).T
        o32_ref[0, :, h * HD : (h + 1) * HD] = o
        o_ref[0, :, h * HD : (h + 1) * HD] = o.astype(BF)
    lse_ref[...] = m_ref[...] + jnp.log2(l_ref[...])


def attend(place, q, near, far_of):
    stats = [of_slot((3, 256)), of_slot((3, 256)), of_slot((3, HD, 256))]
    stat_shapes = [
        jax.ShapeDtypeStruct((4, 3, 256), F32),
        jax.ShapeDtypeStruct((4, 3, 256), F32),
        jax.ShapeDtypeStruct((4, 3, HD, 256), F32),
    ]
    keys = [whole((4, 256, 384)), whole((4, 256, 384))]
    state = pl.pallas_call(
        attend_near_kernel,
        grid_spec=pltpu.PrefetchScalarGridSpec(
            num_scalar_prefetch=1, grid=(4,), in_specs=[of_slot((256, 192))] + keys, out_specs=stats
        ),
        out_shape=stat_shapes,
        compiler_params=pltpu.CompilerParams(vmem_limit_bytes=32 * MIB),
        cost_estimate=COST,
        name="attend_near",
    )(place, q, *near)
    state, far = far_of(state)
    return pl.pallas_call(
        attend_far_kernel,
        grid_spec=pltpu.PrefetchScalarGridSpec(
            num_scalar_prefetch=1,
            grid=(4,),
            in_specs=[of_slot((256, 192))] + keys + stats,
            out_specs=[of_slot((256, 192)), of_slot((256, 192)), of_slot((3, 256))],
            scratch_shapes=[pltpu.VMEM((1, 3, 256), F32), pltpu.VMEM((1, 3, 256), F32), pltpu.VMEM((1, 3, HD, 256), F32)],
        ),
        out_shape=[
            jax.ShapeDtypeStruct((4, 256, 192), BF),
            jax.ShapeDtypeStruct((4, 256, 192), F32),
            jax.ShapeDtypeStruct((4, 3, 256), F32),
        ],
        compiler_params=pltpu.CompilerParams(vmem_limit_bytes=32 * MIB),
        cost_estimate=COST,
        name="attend_far",
    )(place, q, *far, *state)


def grad_step(lse_ref, qdo_ref, delta_ref, dqt_ref, sums, blocks, at, masks):
    both = {}
    for h in range(3):
        for i, block in enumerate(blocks):
            both[h, i] = nt(block[:, h * 128 : (h + 1) * 128], qdo_ref[h])
    weights = {}
    for h in range(3):
        for i, mask in enumerate(masks):
            p = jnp.exp2(both[h, i][:, :256] * LOG2E - lse_ref[0, h : h + 1, :])
            if mask:
                p = mask(p, 0.0)
            ds = (p * (both[h, i][:, 256:] - delta_ref[h])).astype(BF)
            weights[h, i] = (ds, p.astype(BF))
    for h in range(3):
        dqt = dqt_ref[h]
        for i, block in enumerate(blocks):
            ds, p = weights[h, i]
            sums[i][at, :, h * 128 : (h + 1) * 128] += jnp.dot(
                jnp.concatenate([ds, p], axis=1), qdo_ref[h], preferred_element_type=F32
            )
            dqt = dqt + tn(block[:, h * 128 : h * 128 + HD], ds)
        dqt_ref[h] = dqt


def grad_start(q_ref, do_refs, delta_of, qdo_ref, delta_ref, sums):
    @pl.when(pl.program_id(0) == 0)
    def _():
        for total in sums:
            total[...] = jnp.zeros(total.shape, F32)

    zero = jnp.zeros((256, HD), BF)
    for i, do_ref in enumerate(do_refs):
        @pl.when(pl.program_id(0) == i)
        def _():
            for h in range(3):
                do = do_ref[:, h * HD : (h + 1) * HD]
                qdo_ref[h, :256, :] = jnp.concatenate([q_ref[0, :, h * HD : (h + 1) * HD], zero], axis=1)
                qdo_ref[h, 256:, :] = jnp.concatenate([zero, do], axis=1)
                delta_ref[h] = delta_of(h, do)


def grad_end(sums, outs):
    @pl.when(pl.program_id(0) == 3)
    def _():
        for total, out in zip(sums, outs):
            out[...] = total[...].astype(BF)


def grad_far_kernel(place, q_ref, do0, do1, do2, do3, o32_ref, lse_ref, kv0_ref, kv1_ref, delta_out, dqt_out, g0_ref, g1_ref, qdo_ref, delta_ref, dqt_ref, sum0_ref, sum1_ref):
    sums = [sum0_ref, sum1_ref]

    def delta_of(h, do):
        prod = do.astype(F32) * o32_ref[0, :, h * HD : (h + 1) * HD]
        return jnp.sum(prod.T, axis=0, keepdims=True)

    grad_start(q_ref, (do0, do1, do2, do3), delta_of, qdo_ref, delta_ref, sums)
    dqt_ref[...] = jnp.zeros(dqt_ref.shape, F32)

    def body(y, carry):
        at = slot(place, y)
        grad_step(lse_ref, qdo_ref, delta_ref, dqt_ref, sums, [kv0_ref[at], kv1_ref[at]], at, [None, None])
        return carry

    lax.fori_loop(0, query_y(place) + place[1], body, 0)
    for h in range(3):
        delta_out[0, h : h + 1, :] = delta_ref[h]
        dqt_out[0, h] = dqt_ref[h]
    grad_end(sums, [g0_ref, g1_ref])


def grad_near_kernel(place, q_ref, do0, do1, do2, do3, lse_ref, kv0_ref, kv1_ref, delta_in, dqt_in, dq_ref, g0_ref, g1_ref, qdo_ref, delta_ref, dqt_ref, sum0_ref, sum1_ref):
    own = pl.program_id(0)
    sums = [sum0_ref, sum1_ref]
    grad_start(q_ref, (do0, do1, do2, do3), lambda h, do: delta_in[0, h : h + 1, :], qdo_ref, delta_ref, sums)
    dqt_ref[...] = dqt_in[0]

    def beside(probs, other):
        return jnp.where(place[2] == 1, probs, other)

    grad_step(lse_ref, qdo_ref, delta_ref, dqt_ref, sums, [kv0_ref[own], kv1_ref[own]], own, [causal, beside])

    def body(y, carry):
        at = slot(place, y)
        grad_step(lse_ref, qdo_ref, delta_ref, dqt_ref, sums, [kv0_ref[at], kv1_ref[at]], at, [None, None])
        return carry

    lax.fori_loop(0, query_y(place), body, 0)
    for h in range(3):
        dq_ref[0, :, h * HD : (h + 1) * HD] = (dqt_ref[h].T * 0.125).astype(BF)
    grad_end(sums, [g0_ref, g1_ref])


GRAD_SCRATCH = [
    pltpu.VMEM((3, 512, 128), BF),
    pltpu.VMEM((3, 1, 256), F32),
    pltpu.VMEM((3, HD, 256), F32),
    pltpu.VMEM((4, 256, 384), F32),
    pltpu.VMEM((4, 256, 384), F32),
]


def attend_back_far(place, q, do, o32, lse, far):
    keys = [whole((4, 256, 384)), whole((4, 256, 384))]
    return pl.pallas_call(
        grad_far_kernel,
        grid_spec=pltpu.PrefetchScalarGridSpec(
            num_scalar_prefetch=1,
            grid=(4,),
            in_specs=[of_slot((256, 192))] + [whole((256, 192))] * 4 + [of_slot((256, 192)), of_slot((3, 256))] + keys,
            out_specs=[of_slot((3, 256)), of_slot((3, HD, 256))] + keys,
            scratch_shapes=GRAD_SCRATCH,
        ),
        out_shape=[
            jax.ShapeDtypeStruct((4, 3, 256), F32),
            jax.ShapeDtypeStruct((4, 3, HD, 256), F32),
            jax.ShapeDtypeStruct((4, 256, 384), BF),
            jax.ShapeDtypeStruct((4, 256, 384), BF),
        ],
        compiler_params=pltpu.CompilerParams(vmem_limit_bytes=40 * MIB),
        cost_estimate=COST,
        name="attend_back_far",
    )(place, q, *do, o32, lse, *far)


def attend_back_near(place, q, do, lse, near, delta, dqt):
    keys = [whole((4, 256, 384)), whole((4, 256, 384))]
    return pl.pallas_call(
        grad_near_kernel,
        grid_spec=pltpu.PrefetchScalarGridSpec(
            num_scalar_prefetch=1,
            grid=(4,),
            in_specs=[of_slot((256, 192))] + [whole((256, 192))] * 4 + [of_slot((3, 256))] + keys + [of_slot((3, 256)), of_slot((3, HD, 256))],
            out_specs=[of_slot((256, 192))] + keys,
            scratch_shapes=GRAD_SCRATCH,
        ),
        out_shape=[
            jax.ShapeDtypeStruct((4, 256, 192), BF),
            jax.ShapeDtypeStruct((4, 256, 384), BF),
            jax.ShapeDtypeStruct((4, 256, 384), BF),
        ],
        compiler_params=pltpu.CompilerParams(vmem_limit_bytes=40 * MIB),
        cost_estimate=COST,
        name="attend_back_near",
    )(place, q, *do, lse, *near, delta, dqt)


def prep_kernel(place, x0_ref, x1_ref, x2_ref, x3_ref, x4_ref, w_ref, bias_ref, gain_ref, shift_ref, xhat_ref, q_ref, kv_ref, far_ref):
    for i, x_ref in enumerate((x4_ref, x0_ref, x1_ref, x2_ref, x3_ref)):
        @pl.when(pl.program_id(0) == i)
        def _():
            x = x_ref[...].astype(F32)
            center = x - jnp.mean(x, axis=-1, keepdims=True)
            spread = jnp.mean(center * center, axis=-1, keepdims=True)
            xhat = center * lax.rsqrt(spread + 1e-05)
            h1 = (xhat * gain_ref[...] + shift_ref[...]).astype(BF)
            qkv = jnp.dot(h1, w_ref[0], preferred_element_type=F32) + bias_ref[0]
            if i == 0:
                far_ref[...] = qkv[:, 192:].astype(BF)
            else:
                xhat_ref[0] = xhat.astype(BF)
                q_ref[0] = qkv[:, :192].astype(BF) * jnp.asarray(0.125, BF)
                kv_ref[0] = qkv[:, 192:].astype(BF)


def prep(place, blocks, w_groups, bias_groups, gain, shift):
    def after(shape):
        return pl.BlockSpec((1,) + shape, lambda i, *_: (jnp.maximum(i - 1, 0),) + (0,) * len(shape))

    return pl.pallas_call(
        prep_kernel,
        grid_spec=pltpu.PrefetchScalarGridSpec(
            num_scalar_prefetch=1,
            grid=(5,),
            in_specs=[whole((256, 768))] * 5
            + [
                pl.BlockSpec((1, 768, 576), lambda i, place: (place[0], 0, 0)),
                pl.BlockSpec((1, 1, 576), lambda i, place: (place[0], 0, 0)),
                whole((1, 768)),
                whole((1, 768)),
            ],
            out_specs=[after((256, 768)), after((256, 192)), after((256, 384)), whole((256, 384))],
        ),
        out_shape=[
            jax.ShapeDtypeStruct((4, 256, 768), BF),
            jax.ShapeDtypeStruct((4, 256, 192), BF),
            jax.ShapeDtypeStruct((4, 256, 384), BF),
            jax.ShapeDtypeStruct((256, 384), BF),
        ],
        compiler_params=pltpu.CompilerParams(vmem_limit_bytes=32 * MIB),
        cost_estimate=COST,
        name="prep",
    )(place, *blocks, w_groups, bias_groups, gain.reshape(1, 768), shift.reshape(1, 768))


FIRST = ("x", "y")
SECOND = ("y", "z")
REST = ("z", "x")
LAST = ("x", "z")


def shift_pairs(axes, step, pairwise=False):
    pairs = []
    for s in range(16):
        for b in range(8):
            at = {"y": s // 4, "z": (s // 2 % 2) * 2 + b // 4, "c": s % 2, "x": b % 4}
            axis = axes[at["c"]]
            at[axis] = at[axis] ^ step if pairwise else (at[axis] + step) % (2 if axis == "c" else 4)
            source = (at["y"] * 4 + (at["z"] // 2) * 2 + at["c"]) * 8 + (at["z"] % 2) * 4 + at["x"]
            pairs.append((source, s * 8 + b))
    return pairs


def fetch(array, axes, step):
    if isinstance(axes, str):
        axes = (axes, axes)
    return lax.ppermute(array, ("seq", "batch"), shift_pairs(axes, step))


def fetch_all(array, axes):
    return [fetch(array, axes, step) for step in (1, 2, 3)]


def roll_slots(pieces, index):
    count = len(pieces)
    stacked = jnp.stack(pieces + pieces[:-1])
    return lax.dynamic_slice_in_dim(stacked, lax.rem(count - index, count), count, 0)


def halve(array, axis, index):
    for step in (2, 1):
        parts = array.reshape(2, -1, *array.shape[1:])
        side = lax.rem(index // step, 2)
        kept = lax.dynamic_index_in_dim(parts, side, 0, keepdims=False)
        other = fetch_pair(lax.dynamic_index_in_dim(parts, 1 - side, 0, keepdims=False), axis, step)
        array = (kept.astype(F32) + other.astype(F32)).astype(array.dtype)
    return array


def gather_two(array, axes):
    pair = jnp.stack([array, fetch_pair(array, axes, 1)])
    return jnp.concatenate([pair, fetch_pair(pair, axes, 2)])


def sum_pairs(array, axes):
    for step in (2, 1):
        array = (array.astype(F32) + fetch_pair(array, axes, step).astype(F32)).astype(array.dtype)
    return array


def fetch_pair(array, axes, step):
    if isinstance(axes, str):
        axes = (axes, axes)
    return lax.ppermute(array, ("seq", "batch"), shift_pairs(axes, step, True))


def reduce_scatter(array, axes, index):
    total = lax.dynamic_index_in_dim(array, index, 0, keepdims=False).astype(F32)
    for step in (1, 2, 3):
        piece = lax.dynamic_index_in_dim(array, lax.rem(index + step, 4), 0, keepdims=False)
        total = total + fetch(piece, axes, 4 - step).astype(F32)
    return total.astype(array.dtype)


def all_gather(array, axes, index):
    return roll_slots([array] + fetch_all(array, axes), index)


def feed_kernel(place, a0, a1, a2, a3, x_ref, dy_ref, w_out_ref, w_up_ref, w_down_ref, b_out_ref, gain_ref, shift_ref, b_up_ref, b_down_ref, result_ref, mid_grad_ref, d0, d1, d2, d3, g_ref, du_ref, h2_ref, da_ref, at_ref, send_ref, rows_ref, mid_ref, turned_ref, sum_ref, grad_ref):
    step = pl.program_id(0)
    core = place[2]

    @pl.when(step == 0)
    def _():
        for e, ref in enumerate((a0, a1, a2, a3)):
            turned_ref[:, e * 192 : (e + 1) * 192] = ref[...]
            for group in range(4):
                @pl.when(lax.rem(place[0] + e, 4) == group)
                def _():
                    at = group % 2 * 192

                    @pl.when(core == group // 2)
                    def _():
                        at_ref[:, at : at + 192] = ref[...]

                    @pl.when(core != group // 2)
                    def _():
                        send_ref[:, 4608 + at : 4800 + at] = ref[...]

        mid = x_ref[...].astype(F32) + jnp.dot(turned_ref[...], w_out_ref[...], preferred_element_type=F32) + b_out_ref[...]
        mid_ref[...] = mid
        center = mid - jnp.mean(mid, axis=-1, keepdims=True)
        xhat = center * lax.rsqrt(jnp.mean(center * center, axis=-1, keepdims=True) + 1e-05)
        h2 = (xhat * gain_ref[...] + shift_ref[...]).astype(BF)
        h2_ref[...] = h2
        send_ref[:, 3072:3840] = h2
        rows_ref[...] = jnp.zeros(rows_ref.shape, F32)
        rows_ref[3:4, :] = jnp.sum(dy_ref[...].astype(F32), axis=0, keepdims=True)

    u = jnp.dot(h2_ref[...], w_up_ref[...], preferred_element_type=F32) + b_up_ref[...]
    grad_act = nt(dy_ref[...], w_down_ref[...])
    scale = 0.7978845608028654
    square = u * u
    t = jnp.tanh(scale * u * (1.0 + 0.044715 * square))
    half = 0.5 + 0.5 * t
    g = (u * half).astype(BF)
    slope = half + 0.5 * u * (1.0 - t * t) * scale * (1.0 + 3 * 0.044715 * square)
    du = (grad_act * slope).astype(BF)
    out = jnp.dot(g, w_down_ref[...], preferred_element_type=F32)
    back = nt(du, w_up_ref[...])
    total = jnp.sum(du.astype(F32), axis=0, keepdims=True)
    for j in range(4):
        @pl.when(step == j)
        def _():
            rows_ref[6 + j : 7 + j, :] = total
            sum_ref[...] = out if j == 0 else sum_ref[...] + out
            grad_ref[...] = back if j == 0 else grad_ref[...] + back
            at = j % 2 * 768

            @pl.when(core == j // 2)
            def _():
                g_ref[:, at : at + 768] = g
                du_ref[:, at : at + 768] = du

            @pl.when(core != j // 2)
            def _():
                send_ref[:, at : at + 768] = g
                send_ref[:, 1536 + at : 2304 + at] = du

    @pl.when(step == 3)
    def _():
        mid = mid_ref[...]
        result_ref[...] = (mid + sum_ref[...] + b_down_ref[...]).astype(BF)
        center = mid - jnp.mean(mid, axis=-1, keepdims=True)
        norm = lax.rsqrt(jnp.mean(center * center, axis=-1, keepdims=True) + 1e-05)
        xhat = center * norm
        dh2 = grad_ref[...]
        rows_ref[4:5, :] = jnp.sum(dh2 * xhat, axis=0, keepdims=True)
        rows_ref[5:6, :] = jnp.sum(dh2, axis=0, keepdims=True)
        grad = dh2 * gain_ref[...]
        inner = grad - jnp.mean(grad, axis=-1, keepdims=True) - xhat * jnp.mean(grad * xhat, axis=-1, keepdims=True)
        mid_grad = dy_ref[...].astype(F32) + norm * inner
        mid_grad_ref[...] = mid_grad
        da = mid_grad.astype(BF)
        da_ref[...] = da
        send_ref[:, 3840:4608] = da
        rows_ref[2:3, :] = jnp.sum(da.astype(F32), axis=0, keepdims=True)
        do = nt(da, w_out_ref[...]).astype(BF)
        for e, ref in enumerate((d0, d1, d2, d3)):
            ref[...] = do[:, e * 192 : (e + 1) * 192]


def feed(place, heads, x, dy, w_out, w_up, w_down, b_out, gain, shift, b_up, b_down):
    tile = whole((256, 768))
    row = whole((1, 768))
    part = whole((256, 192))
    return pl.pallas_call(
        feed_kernel,
        grid_spec=pltpu.PrefetchScalarGridSpec(
            num_scalar_prefetch=1,
            grid=(4,),
            in_specs=[part] * 4
            + [
                tile,
                tile,
                whole((768, 768)),
                pl.BlockSpec((768, 768), lambda i, place: (0, i)),
                pl.BlockSpec((768, 768), lambda i, place: (i, 0)),
                row,
                row,
                row,
                pl.BlockSpec((1, 768), lambda i, place: (0, i)),
                row,
            ],
            out_specs=[tile, tile]
            + [part] * 4
            + [whole((256, 1536)), whole((256, 1536)), tile, tile, whole((256, 384)), whole((256, 4992)), whole((64, 768))],
            scratch_shapes=[
                pltpu.VMEM((256, 768), F32),
                pltpu.VMEM((256, 768), BF),
                pltpu.VMEM((256, 768), F32),
                pltpu.VMEM((256, 768), F32),
            ],
        ),
        out_shape=[
            jax.ShapeDtypeStruct((256, 768), BF),
            jax.ShapeDtypeStruct((256, 768), F32),
        ]
        + [jax.ShapeDtypeStruct((256, 192), BF)] * 4
        + [jax.ShapeDtypeStruct((256, width), BF) for width in (1536, 1536, 768, 768, 384, 4992)]
        + [jax.ShapeDtypeStruct((64, 768), F32)],
        compiler_params=pltpu.CompilerParams(vmem_limit_bytes=40 * MIB),
        cost_estimate=COST,
        name="feed",
    )(
        place,
        *heads,
        x,
        dy,
        w_out,
        w_up,
        w_down,
        b_out.reshape(1, 768),
        gain.reshape(1, 768),
        shift.reshape(1, 768),
        b_up.reshape(1, 3072),
        b_down.reshape(1, 768),
    )


def weights_kernel(info, g, dy, du, h2, at, da, g2, dy2, du2, h22, at2, da2, b0, b1, b2, b3, out_scr):
    a1 = pl.program_id(0)

    @pl.when(a1 == 0)
    def _():
        out_scr[...] = tn(at[...], da[...]) + tn(at2[...], da2[...])

    down = (tn(g[...], dy[...]) + tn(g2[...], dy2[...])).astype(BF)
    up = (tn(h2[...], du[...]) + tn(h22[...], du2[...])).astype(BF)
    zero = jnp.zeros((8, 768), F32)
    for a2 in range(4):
        rest = out_scr[pl.ds(pl.multiple_of(a1 * 96 + a2 * 24, 8), 24), :]
        rest = jnp.concatenate([rest, zero], axis=0).astype(BF)
        slot_at = lax.rem(jnp.where(info[0] == 0, a1, a2) + 4 - info[1], 4)
        at_second = jnp.where(info[0] == 0, a2, a1)
        for i, ref in enumerate((b0, b1, b2, b3)):
            @pl.when(slot_at == i)
            def _():
                ref[at_second, 0:96, :] = down[a2 * 96 : (a2 + 1) * 96]
                ref[at_second, 96:192, :] = up[a2 * 96 : (a2 + 1) * 96]
                ref[at_second, 192:224, :] = rest


def weights(info, g, dy, du, h2, at, da, received, dy_received):
    def cols(width, index):
        return pl.BlockSpec((256, width), lambda i, info: (0, index(i, info)))

    full = whole((256, 768))
    return pl.pallas_call(
        weights_kernel,
        grid_spec=pltpu.PrefetchScalarGridSpec(
            num_scalar_prefetch=1,
            grid=(4,),
            in_specs=[
                cols(384, lambda i, info: i),
                full,
                cols(768, lambda i, info: i // 2),
                cols(384, lambda i, info: i % 2),
                whole((256, 384)),
                full,
                cols(384, lambda i, info: i),
                full,
                cols(768, lambda i, info: 2 + i // 2),
                cols(384, lambda i, info: 8 + i % 2),
                cols(384, lambda i, info: 12),
                cols(768, lambda i, info: 5),
            ],
            out_specs=[whole((4, 224, 768))] * 4,
            scratch_shapes=[pltpu.VMEM((384, 768), F32)],
        ),
        out_shape=[jax.ShapeDtypeStruct((4, 224, 768), BF)] * 4,
        compiler_params=pltpu.CompilerParams(vmem_limit_bytes=40 * MIB),
        cost_estimate=COST,
        name="weights",
    )(info, g, dy, du, h2, at, da, received, dy_received, received, received, received, received)


def add_kernel(info, p0, p1, p2, p3, *outs):
    total = p0[0].astype(F32) + p1[0].astype(F32) + p2[0].astype(F32) + p3[0].astype(F32)
    for i, out in enumerate(outs):
        @pl.when(pl.program_id(0) == i)
        def _():
            out[...] = total.astype(BF)


def add_pieces(info, pieces):
    spec = pl.BlockSpec((1, 224, 768), lambda i, info: (lax.rem(info[2] + i, 4), 0, 0))
    return pl.pallas_call(
        add_kernel,
        grid_spec=pltpu.PrefetchScalarGridSpec(
            num_scalar_prefetch=1, grid=(4,), in_specs=[spec] * 4, out_specs=[whole((224, 768))] * 4
        ),
        out_shape=[jax.ShapeDtypeStruct((224, 768), BF)] * 4,
        compiler_params=pltpu.CompilerParams(vmem_limit_bytes=24 * MIB),
        cost_estimate=COST,
        name="add_pieces",
    )(info, *pieces)


def place_kernel(info, p0, p1, p2, p3, *refs):
    down, up, out = refs[-3:]
    for i, piece in enumerate((p0, p1, p2, p3)):
        @pl.when(pl.program_id(0) == i)
        def _():
            for r2 in range(4):
                a2 = lax.rem(info[2] + r2, 4)
                rows = piece[r2].astype(F32)
                at = pl.multiple_of(a2 * 96, 96)
                down[pl.ds(at, 96), :] = rows[0:96]
                up[pl.ds(at, 96), :] = rows[96:192]
                out[pl.ds(pl.multiple_of(a2 * 24, 8), 24), :] = rows[192:216]


def place_weights(info, pieces, others=()):
    def by_rows(r1, info):
        return (info[0] * 4 + lax.rem(info[1] + r1, 4), 0)

    def by_columns(r1, info):
        a1 = lax.rem(info[1] + r1, 4)
        return (lax.rem(a1, 2), info[0] * 2 + a1 // 2)

    return pl.pallas_call(
        place_kernel,
        grid_spec=pltpu.PrefetchScalarGridSpec(
            num_scalar_prefetch=1,
            grid=(4,),
            in_specs=[whole((4, 224, 768))] * 4 + [pl.BlockSpec(memory_space=pl.ANY)] * len(others),
            out_specs=[pl.BlockSpec((384, 768), by_rows), pl.BlockSpec((384, 768), by_columns), pl.BlockSpec((96, 768), by_rows)],
        ),
        out_shape=[
            jax.ShapeDtypeStruct((3072, 768), F32),
            jax.ShapeDtypeStruct((768, 3072), F32),
            jax.ShapeDtypeStruct((768, 768), F32),
        ],
        input_output_aliases={5 + i: i for i in range(len(others))},
        compiler_params=pltpu.CompilerParams(vmem_limit_bytes=32 * MIB),
        cost_estimate=COST,
        name="place_weights",
    )(info, *pieces, *others)


def moment_kernel(place, xhat_ref, dq_ref, near0_ref, near1_ref, far_ref, w_ref, gain_ref, shift_ref, rows_ref, p0, p1, p2, p3, give_ref, keep_ref, dqkv_ref):
    step = pl.program_id(0)

    @pl.when(step == 0)
    def _():
        for i, piece in enumerate((p0, p1, p2, p3)):
            dkv = near0_ref[i].astype(F32) + near1_ref[i].astype(F32) + far_ref[i].astype(F32)
            piece[:, :192] = dq_ref[i]
            piece[:, 192:] = dkv.astype(BF)
            dqkv_ref[i * 256 : (i + 1) * 256, :] = piece[...]

    dqkv = dqkv_ref[...]
    moment = tn(xhat_ref[...], dqkv)
    total = jnp.sum(dqkv.astype(F32), axis=0, keepdims=True)
    w = w_ref[0].astype(F32)
    gain = jnp.sum(w * moment, axis=1, keepdims=True)
    shift = jnp.sum(w * total, axis=1, keepdims=True)
    gw = (gain_ref[...] * moment + shift_ref[...] * total).astype(BF)
    lane = lax.broadcasted_iota(jnp.int32, (384, 64), 1)
    here = lax.rem(place[2] + 1 + step, 2)
    ends = jnp.concatenate([total[:, 384:], jnp.zeros((1, 192), F32)], axis=1)
    total_here = jnp.where(here == 0, total[:, :384], ends)
    row = lax.broadcasted_iota(jnp.int32, (64, 384), 0)
    vectors = jnp.where(row == 10, total_here, rows_ref[...]).T
    vectors = jnp.where(lane == 0, gain, jnp.where(lane == 1, shift, vectors)).astype(BF)

    def put(ref):
        ref[:, :576] = gw
        ref[:, 576:] = vectors

    @pl.when(step == 0)
    def _():
        put(give_ref)

    @pl.when(step == 1)
    def _():
        put(keep_ref)


def moments(place, xhat, dq, near0, near1, far, w_groups, gain, shift, rows):
    def half(i, place):
        return lax.rem(place[2] + 1 + i, 2)

    return pl.pallas_call(
        moment_kernel,
        grid_spec=pltpu.PrefetchScalarGridSpec(
            num_scalar_prefetch=1,
            grid=(2,),
            in_specs=[
                pl.BlockSpec((1024, 384), lambda i, place: (0, half(i, place))),
                whole((4, 256, 192)),
                whole((4, 256, 384)),
                whole((4, 256, 384)),
                whole((4, 256, 384)),
                pl.BlockSpec((1, 384, 576), lambda i, place: (place[0], half(i, place), 0)),
                pl.BlockSpec((384, 1), lambda i, place: (half(i, place), 0)),
                pl.BlockSpec((384, 1), lambda i, place: (half(i, place), 0)),
                pl.BlockSpec((64, 384), lambda i, place: (0, half(i, place))),
            ],
            out_specs=[whole((256, 576))] * 4 + [whole((384, 640))] * 2,
            scratch_shapes=[pltpu.VMEM((1024, 576), BF)],
        ),
        out_shape=[jax.ShapeDtypeStruct((256, 576), BF)] * 4 + [jax.ShapeDtypeStruct((384, 640), BF)] * 2,
        compiler_params=pltpu.CompilerParams(vmem_limit_bytes=40 * MIB),
        cost_estimate=COST,
        name="moments",
    )(place, xhat.reshape(1024, 768), dq, near0, near1, far, w_groups, gain.reshape(768, 1), shift.reshape(768, 1), rows)


def regroup_kernel(w_ref, out_ref):
    for group in range(4):
        @pl.when(pl.program_id(0) == group)
        def _():
            at = group * 192
            out_ref[0, :, :192] = w_ref[:, at : at + 192]
            for h in range(3):
                for t in range(2):
                    to = 192 + h * 128 + t * HD
                    first = 768 * (t + 1) + at + h * HD
                    out_ref[0, :, to : to + HD] = w_ref[:, first : first + HD]


def regroup(w):
    return pl.pallas_call(
        regroup_kernel,
        grid=(4,),
        in_specs=[pl.BlockSpec((768, 2304), lambda i: (0, 0))],
        out_specs=pl.BlockSpec((1, 768, 576), lambda i: (i, 0, 0)),
        out_shape=jax.ShapeDtypeStruct((4, 768, 576), BF),
        compiler_params=pltpu.CompilerParams(vmem_limit_bytes=24 * MIB),
        cost_estimate=COST,
        name="regroup",
    )(w)


def finish_kernel(place, p0, p1, p2, p3, w_ref, x_ref, gain_ref, mid_ref, out_ref, acc_ref):
    e = pl.program_id(0)
    for i, piece in enumerate((p0, p1, p2, p3)):
        @pl.when(e == i)
        def _():
            part = nt(piece[...], w_ref[0])
            acc_ref[...] = part if i == 0 else acc_ref[...] + part

    @pl.when(e == 3)
    def _():
        x = x_ref[...].astype(F32)
        center = x - jnp.mean(x, axis=-1, keepdims=True)
        scale = lax.rsqrt(jnp.mean(center * center, axis=-1, keepdims=True) + 1e-05)
        xhat = center * scale
        grad = acc_ref[...] * gain_ref[...]
        inner = grad - jnp.mean(grad, axis=-1, keepdims=True) - xhat * jnp.mean(grad * xhat, axis=-1, keepdims=True)
        out_ref[...] = mid_ref[...] + scale * inner


def finish(place, pieces, w_groups, x, gain, middle):
    return pl.pallas_call(
        finish_kernel,
        grid_spec=pltpu.PrefetchScalarGridSpec(
            num_scalar_prefetch=1,
            grid=(4,),
            in_specs=[whole((256, 576))] * 4
            + [
                pl.BlockSpec((1, 768, 576), lambda i, place: (lax.rem(place[0] + i, 4), 0, 0)),
                whole((256, 768)),
                whole((1, 768)),
                whole((256, 768)),
            ],
            out_specs=whole((256, 768)),
            scratch_shapes=[pltpu.VMEM((256, 768), F32)],
        ),
        out_shape=jax.ShapeDtypeStruct((256, 768), F32),
        compiler_params=pltpu.CompilerParams(vmem_limit_bytes=24 * MIB),
        cost_estimate=COST,
        name="finish",
    )(place, *pieces, w_groups, x, gain.reshape(1, 768), middle)


def join_kernel(place, own_ref, other_ref, out_ref, cols_ref):
    core = lax.rem(place[2] + pl.program_id(0), 2)
    for o, ref in enumerate((own_ref, other_ref)):
        @pl.when(pl.program_id(0) == o)
        def _():
            for group in range(4):
                by_y = lax.rem(group + 4 - place[0], 4)
                for part in range(4):
                    by_x = lax.rem(part + 4 - place[3], 4)
                    second = jnp.where(core == 0, part ^ place[3], group ^ place[0])
                    rows = ref[jnp.where(core == 0, by_y, by_x), second].astype(F32)
                    to = slice(part * 96, (part + 1) * 96)
                    at = group * 192
                    out_ref[to, at : at + 192] = rows[:, :192]
                    for h in range(3):
                        for t in range(2):
                            first = 192 + h * 128 + t * HD
                            column = 768 * (t + 1) + at + h * HD
                            out_ref[to, column : column + HD] = rows[:, first : first + HD]
                    cols_ref[group, to, :] = rows[:, 512:640]


def join_qkv(place, own, other):
    return pl.pallas_call(
        join_kernel,
        grid_spec=pltpu.PrefetchScalarGridSpec(
            num_scalar_prefetch=1,
            grid=(2,),
            in_specs=[whole((4, 4, 96, 640))] * 2,
            out_specs=[
                pl.BlockSpec((384, 2304), lambda o, place: (lax.rem(place[2] + o, 2), 0)),
                pl.BlockSpec((4, 384, 128), lambda o, place: (0, lax.rem(place[2] + o, 2), 0)),
            ],
        ),
        out_shape=[jax.ShapeDtypeStruct((768, 2304), F32), jax.ShapeDtypeStruct((4, 768, 128), F32)],
        compiler_params=pltpu.CompilerParams(vmem_limit_bytes=40 * MIB),
        cost_estimate=COST,
        name="join_qkv",
    )(place, own, other)


def region(always, work, *operands):
    shapes = jax.eval_shape(work, *operands)
    empty = [jnp.zeros(shape.shape, shape.dtype) for shape in shapes]
    return lax.cond(always, lambda *args: list(work(*args)), lambda *args: empty, *operands)


def layer_norm(values, gain, shift):
    center = values - jnp.mean(values, axis=-1, keepdims=True)
    spread = jnp.mean(center * center, axis=-1, keepdims=True)
    return center * lax.rsqrt(spread + 1e-05) * gain + shift


def shards(
    tokens,
    cotangent,
    ln1_gain,
    ln1_shift,
    w_qkv,
    b_query,
    b_value,
    w_out,
    b_out,
    ln2_gain,
    ln2_shift,
    w_up,
    b_up,
    w_down,
    b_down,
):
    seq, batch = lax.axis_index("seq"), lax.axis_index("batch")
    y, zh, c = seq // 4, lax.rem(seq // 2, 2), lax.rem(seq, 2)
    z, x = zh * 2 + batch // 4, lax.rem(batch, 4)
    always = seq + batch >= 0
    place = jnp.stack([y, zh, c, x]).astype(jnp.int32)
    info = jnp.stack([c, jnp.where(c == 0, x, y), jnp.where(c == 0, y, z)]).astype(jnp.int32)
    own_chunks = jnp.stack([c, jnp.where(c == 0, x, z), y]).astype(jnp.int32)
    other_chunks = jnp.stack([1 - c, jnp.where(c == 0, z, x), y]).astype(jnp.int32)

    tokens = tokens[0]
    dy_low = cotangent[0]
    columns = [tokens] + fetch_all(tokens, "y") + [fetch(tokens, "z", 2)]
    dy_other = fetch(dy_low, "c", 1)

    def by_group(array):
        parts = array.reshape(1, 3, 4, 3, HD)
        query = parts[:, 0].transpose(1, 0, 2, 3).reshape(4, 1, 192)
        keys = parts[:, 1:].transpose(2, 0, 3, 1, 4).reshape(4, 1, 384)
        return jnp.concatenate([query, keys], axis=2)

    w_groups = regroup(w_qkv)
    bias_groups = by_group(jnp.concatenate([b_query, jnp.zeros_like(b_query), b_value]))
    w_out_turned = lax.dynamic_slice_in_dim(jnp.concatenate([w_out, w_out]), y * 192, 768, 0)

    xhat, q, kv, far_first = prep(place, columns, w_groups, bias_groups, ln1_gain, ln1_shift)
    far_rest = fetch(kv[1:], "z", 2)
    near = (kv, fetch(kv, "c", 1))
    far = []

    def far_of(state):
        rest, *state = lax.optimization_barrier((far_rest, *state))
        keys = jnp.concatenate([far_first[None], rest])
        far.extend([keys, fetch(keys, "c", 1)])
        return state, far

    o, o32, lse = attend(place, q, near, far_of)

    heads = [o[0]] + [fetch(o[4 - e], "y", e) for e in (1, 2, 3)]
    fed = feed(place, heads, tokens, dy_low, w_out_turned, w_up, w_down, b_out, ln2_gain, ln2_shift, b_up, b_down)
    result, grad_middle, *do, g, du, h2, da, attended, send, vectors = fed

    do_mine = [do[0]] + [fetch(do[4 - e], "y", e) for e in (1, 2, 3)]
    received = fetch(send, "c", 1)
    pieces = weights(info, g, dy_low, du, h2, attended, da, received, dy_other)

    def back(*do_mine):
        delta, dqt, far0, far1 = attend_back_far(place, q, do_mine, o32, lse, far)
        far_sum = (far0.astype(F32) + fetch(far1, "c", 1).astype(F32)).astype(BF)
        far_sum, dqt = lax.optimization_barrier((far_sum, dqt))
        far_received = fetch(far_sum, "z", 2)
        return far_received, *attend_back_near(place, q, do_mine, lse, near, delta, dqt)

    def scatter_beside(pieces, *do_mine):
        return *[fetch(pieces[d], FIRST, 4 - d) for d in (1, 2, 3)], *region(always, back, *do_mine)

    *received, far_received, dq, near0, near1 = region(always, scatter_beside, pieces, *do_mine)
    pieces = [pieces[0]] + received
    def finish_keys(near0, near1, dq, far_received):
        near_received = fetch(near1, "c", 1)
        return moments(place, xhat, dq, near0, near_received, far_received, w_groups, ln1_gain, ln1_shift, vectors)

    def scatter_again(pieces, *operands):
        pieces = add_pieces(info, pieces)
        return pieces[0], *[fetch(pieces[d], SECOND, 4 - d) for d in (1, 2, 3)], *region(always, finish_keys, *operands)

    *pieces, dqkv0, dqkv1, dqkv2, dqkv3, given, gw = region(always, scatter_again, pieces, near0, near1, dq, far_received)
    dqkv = (dqkv0, dqkv1, dqkv2, dqkv3)

    def sum_rest(pieces, given, gw):
        chunk = (sum(p.astype(F32) for p in pieces)).astype(BF)
        gw = (gw.astype(F32) + fetch(given, "c", 1).astype(F32)).astype(BF)
        return sum_pairs(chunk, REST), halve(gw, "x", x)

    def rows_beside(dqkv, *operands):
        return *[fetch(dqkv[4 - e], "y", e) for e in (1, 2, 3)], *region(always, sum_rest, *operands)

    *parts, chunk, gw = region(always, rows_beside, dqkv, pieces, given, gw)

    def finish_rows(gw, *parts):
        gw = sum_pairs(gw, "z")
        grad_inputs = finish(place, parts, w_groups, tokens, ln1_gain, grad_middle)
        return gather_two(gw, FIRST), grad_inputs

    def gather_beside(chunk, *operands):
        return *fetch_all(chunk, "y"), *region(always, finish_rows, *operands)

    *others, gw, grad_inputs = region(always, gather_beside, chunk, gw, dqkv[0], *parts)
    chunk = jnp.stack([chunk] + others)

    def gather_keys(gw):
        return jnp.stack([gw] + fetch_all(gw, ("y", "x")))

    def gather_sides(chunk, gw):
        return fetch(chunk, LAST, 1), fetch(chunk, LAST, 3), region(always, lambda gw: (gather_keys(gw),), gw)[0]

    side1, side3, gw = region(always, gather_sides, chunk, gw)

    def join(gw):
        return join_qkv(place, gw, fetch(gw, "c", 1))

    def gather_far(side1, side3, gw):
        return fetch(side1[:2], LAST, 1), fetch(side3[2:], LAST, 3), *region(always, join, gw)

    low, high, gw_qkv, columns = region(always, gather_far, side1, side3, gw)
    mine = [chunk, side1, jnp.concatenate([low, high]), side3]
    other = [fetch(part, "c", 1) for part in mine]
    placed = place_weights(own_chunks, mine)
    gw_down, gw_up, gw_out = place_weights(other_chunks, other, placed)
    sums = jnp.sum(columns[:, :, 64:74], axis=0)
    totals = columns[:, :576, 74]
    return (
        result[None],
        grad_inputs[None],
        sums[:, 0],
        sums[:, 1],
        gw_qkv,
        totals[:, :192].reshape(768),
        totals[:, 192:].reshape(4, 3, 2, HD)[:, :, 1].reshape(768),
        gw_out,
        sums[:, 2],
        sums[:, 4],
        sums[:, 5],
        gw_up,
        sums[:, 6:10].T.reshape(3072),
        gw_down,
        sums[:, 3],
    )


def solution(mesh):
    split = P("batch", "seq", None)
    return jax.shard_map(
        shards,
        mesh=mesh,
        in_specs=(split, split) + (P(),) * 13,
        out_specs=(split, split) + (P(),) * 13,
        check_vma=False,
    )
```

```python
import functools

import jax
import jax.numpy as jnp
from jax import lax
from jax.experimental import pallas as pl
from jax.experimental.pallas import tpu as pltpu
from jax.sharding import PartitionSpec as P

HD = 64
LOG2E = 1.4426950408889634
BF = jnp.bfloat16
F32 = jnp.float32
MIB = 2**20
COST = pl.CostEstimate(flops=1000, bytes_accessed=1000, transcendentals=0)


def nt(left, right):
    return lax.dot_general(left, right, (((1,), (1,)), ((), ())), preferred_element_type=F32)


def tn(left, right):
    return lax.dot_general(left, right, (((0,), (0,)), ((), ())), preferred_element_type=F32)


def whole(shape):
    return pl.BlockSpec(shape, lambda i, *_: (0,) * len(shape))


def of_slot(shape):
    return pl.BlockSpec((1,) + shape, lambda i, *_: (i,) + (0,) * len(shape))


def causal(scores, other):
    keys = lax.broadcasted_iota(jnp.int32, scores.shape, 0)
    queries = lax.broadcasted_iota(jnp.int32, scores.shape, 1)
    return jnp.where(keys <= queries, scores, other)


def query_y(place):
    return lax.rem(place[0] + pl.program_id(0), 4)


def slot(place, y):
    return lax.rem(y + 4 - place[0], 4)


def softmax_step(q_ref, m_ref, l_ref, acc_ref, blocks, masks):
    scores = []
    for h in range(3):
        q = q_ref[0, :, h * HD : (h + 1) * HD]
        row = [nt(block[:, h * 128 : h * 128 + HD], q) * LOG2E for block in blocks]
        scores.append([mask(s, -1e30) if mask else s for s, mask in zip(row, masks)])
    probs = []
    for h in range(3):
        old = m_ref[0, h : h + 1, :]
        new = old
        for s in scores[h]:
            new = jnp.maximum(new, jnp.max(s, axis=0, keepdims=True))
        factor = jnp.exp2(old - new)
        m_ref[0, h : h + 1, :] = new
        row = [jnp.exp2(s - new) for s in scores[h]]
        l_ref[0, h : h + 1, :] = l_ref[0, h : h + 1, :] * factor + sum(jnp.sum(p, axis=0, keepdims=True) for p in row)
        probs.append((row, factor))
    for h in range(3):
        row, factor = probs[h]
        acc = acc_ref[0, h] * factor
        for block, p in zip(blocks, row):
            acc = acc + tn(block[:, h * 128 + HD : (h + 1) * 128], p.astype(BF))
        acc_ref[0, h] = acc


def attend_near_kernel(place, q_ref, kv0_ref, kv1_ref, m_ref, l_ref, acc_ref):
    own = pl.program_id(0)
    m_ref[...] = jnp.full(m_ref.shape, -1e30, F32)
    l_ref[...] = jnp.zeros(l_ref.shape, F32)
    acc_ref[...] = jnp.zeros(acc_ref.shape, F32)

    def beside(scores, other):
        return jnp.where(place[2] == 1, scores, other)

    softmax_step(q_ref, m_ref, l_ref, acc_ref, [kv0_ref[own], kv1_ref[own]], [causal, beside])

    def body(y, carry):
        at = slot(place, y)
        softmax_step(q_ref, m_ref, l_ref, acc_ref, [kv0_ref[at], kv1_ref[at]], [None, None])
        return carry

    lax.fori_loop(0, query_y(place), body, 0)


def attend_far_kernel(place, q_ref, kv0_ref, kv1_ref, m_in, l_in, acc_in, o_ref, o32_ref, lse_ref, m_ref, l_ref, acc_ref):
    m_ref[...] = m_in[...]
    l_ref[...] = l_in[...]
    acc_ref[...] = acc_in[...]

    def body(y, carry):
        at = slot(place, y)
        softmax_step(q_ref, m_ref, l_ref, acc_ref, [kv0_ref[at], kv1_ref[at]], [None, None])
        return carry

    lax.fori_loop(0, query_y(place) + place[1], body, 0)
    for h in range(3):
        o = (acc_ref[0, h] / l_ref[0, h : h + 1, :]).T
        o32_ref[0, :, h * HD : (h + 1) * HD] = o
        o_ref[0, :, h * HD : (h + 1) * HD] = o.astype(BF)
    lse_ref[...] = m_ref[...] + jnp.log2(l_ref[...])


def attend(place, q, near, far_of):
    stats = [of_slot((3, 256)), of_slot((3, 256)), of_slot((3, HD, 256))]
    stat_shapes = [
        jax.ShapeDtypeStruct((4, 3, 256), F32),
        jax.ShapeDtypeStruct((4, 3, 256), F32),
        jax.ShapeDtypeStruct((4, 3, HD, 256), F32),
    ]
    keys = [whole((4, 256, 384)), whole((4, 256, 384))]
    state = pl.pallas_call(
        attend_near_kernel,
        grid_spec=pltpu.PrefetchScalarGridSpec(
            num_scalar_prefetch=1, grid=(4,), in_specs=[of_slot((256, 192))] + keys, out_specs=stats
        ),
        out_shape=stat_shapes,
        compiler_params=pltpu.CompilerParams(vmem_limit_bytes=32 * MIB),
        cost_estimate=COST,
        name="attend_near",
    )(place, q, *near)
    state, far = far_of(state)
    return pl.pallas_call(
        attend_far_kernel,
        grid_spec=pltpu.PrefetchScalarGridSpec(
            num_scalar_prefetch=1,
            grid=(4,),
            in_specs=[of_slot((256, 192))] + keys + stats,
            out_specs=[of_slot((256, 192)), of_slot((256, 192)), of_slot((3, 256))],
            scratch_shapes=[pltpu.VMEM((1, 3, 256), F32), pltpu.VMEM((1, 3, 256), F32), pltpu.VMEM((1, 3, HD, 256), F32)],
        ),
        out_shape=[
            jax.ShapeDtypeStruct((4, 256, 192), BF),
            jax.ShapeDtypeStruct((4, 256, 192), F32),
            jax.ShapeDtypeStruct((4, 3, 256), F32),
        ],
        compiler_params=pltpu.CompilerParams(vmem_limit_bytes=32 * MIB),
        cost_estimate=COST,
        name="attend_far",
    )(place, q, *far, *state)


def grad_step(lse_ref, qdo_ref, delta_ref, dqt_ref, sums, blocks, at, masks):
    both = {}
    for h in range(3):
        for i, block in enumerate(blocks):
            both[h, i] = nt(block[:, h * 128 : (h + 1) * 128], qdo_ref[h])
    weights = {}
    for h in range(3):
        for i, mask in enumerate(masks):
            p = jnp.exp2(both[h, i][:, :256] * LOG2E - lse_ref[0, h : h + 1, :])
            if mask:
                p = mask(p, 0.0)
            ds = (p * (both[h, i][:, 256:] - delta_ref[h])).astype(BF)
            weights[h, i] = (ds, p.astype(BF))
    for h in range(3):
        dqt = dqt_ref[h]
        for i, block in enumerate(blocks):
            ds, p = weights[h, i]
            sums[i][at, :, h * 128 : (h + 1) * 128] += jnp.dot(
                jnp.concatenate([ds, p], axis=1), qdo_ref[h], preferred_element_type=F32
            )
            dqt = dqt + tn(block[:, h * 128 : h * 128 + HD], ds)
        dqt_ref[h] = dqt


def grad_start(q_ref, do_refs, delta_of, qdo_ref, delta_ref, sums):
    @pl.when(pl.program_id(0) == 0)
    def _():
        for total in sums:
            total[...] = jnp.zeros(total.shape, F32)

    zero = jnp.zeros((256, HD), BF)
    for i, do_ref in enumerate(do_refs):
        @pl.when(pl.program_id(0) == i)
        def _():
            for h in range(3):
                do = do_ref[:, h * HD : (h + 1) * HD]
                qdo_ref[h, :256, :] = jnp.concatenate([q_ref[0, :, h * HD : (h + 1) * HD], zero], axis=1)
                qdo_ref[h, 256:, :] = jnp.concatenate([zero, do], axis=1)
                delta_ref[h] = delta_of(h, do)


def grad_end(sums, outs):
    @pl.when(pl.program_id(0) == 3)
    def _():
        for total, out in zip(sums, outs):
            out[...] = total[...].astype(BF)


def grad_far_kernel(place, q_ref, do0, do1, do2, do3, o32_ref, lse_ref, kv0_ref, kv1_ref, delta_out, dqt_out, g0_ref, g1_ref, qdo_ref, delta_ref, dqt_ref, sum0_ref, sum1_ref):
    sums = [sum0_ref, sum1_ref]

    def delta_of(h, do):
        prod = do.astype(F32) * o32_ref[0, :, h * HD : (h + 1) * HD]
        return jnp.sum(prod.T, axis=0, keepdims=True)

    grad_start(q_ref, (do0, do1, do2, do3), delta_of, qdo_ref, delta_ref, sums)
    dqt_ref[...] = jnp.zeros(dqt_ref.shape, F32)

    def body(y, carry):
        at = slot(place, y)
        grad_step(lse_ref, qdo_ref, delta_ref, dqt_ref, sums, [kv0_ref[at], kv1_ref[at]], at, [None, None])
        return carry

    lax.fori_loop(0, query_y(place) + place[1], body, 0)
    for h in range(3):
        delta_out[0, h : h + 1, :] = delta_ref[h]
        dqt_out[0, h] = dqt_ref[h]
    grad_end(sums, [g0_ref, g1_ref])


def grad_near_kernel(place, q_ref, do0, do1, do2, do3, lse_ref, kv0_ref, kv1_ref, delta_in, dqt_in, dq_ref, g0_ref, g1_ref, qdo_ref, delta_ref, dqt_ref, sum0_ref, sum1_ref):
    own = pl.program_id(0)
    sums = [sum0_ref, sum1_ref]
    grad_start(q_ref, (do0, do1, do2, do3), lambda h, do: delta_in[0, h : h + 1, :], qdo_ref, delta_ref, sums)
    dqt_ref[...] = dqt_in[0]

    def beside(probs, other):
        return jnp.where(place[2] == 1, probs, other)

    grad_step(lse_ref, qdo_ref, delta_ref, dqt_ref, sums, [kv0_ref[own], kv1_ref[own]], own, [causal, beside])

    def body(y, carry):
        at = slot(place, y)
        grad_step(lse_ref, qdo_ref, delta_ref, dqt_ref, sums, [kv0_ref[at], kv1_ref[at]], at, [None, None])
        return carry

    lax.fori_loop(0, query_y(place), body, 0)
    for h in range(3):
        dq_ref[0, :, h * HD : (h + 1) * HD] = (dqt_ref[h].T * 0.125).astype(BF)
    grad_end(sums, [g0_ref, g1_ref])


GRAD_SCRATCH = [
    pltpu.VMEM((3, 512, 128), BF),
    pltpu.VMEM((3, 1, 256), F32),
    pltpu.VMEM((3, HD, 256), F32),
    pltpu.VMEM((4, 256, 384), F32),
    pltpu.VMEM((4, 256, 384), F32),
]


def attend_back_far(place, q, do, o32, lse, far):
    keys = [whole((4, 256, 384)), whole((4, 256, 384))]
    return pl.pallas_call(
        grad_far_kernel,
        grid_spec=pltpu.PrefetchScalarGridSpec(
            num_scalar_prefetch=1,
            grid=(4,),
            in_specs=[of_slot((256, 192))] + [whole((256, 192))] * 4 + [of_slot((256, 192)), of_slot((3, 256))] + keys,
            out_specs=[of_slot((3, 256)), of_slot((3, HD, 256))] + keys,
            scratch_shapes=GRAD_SCRATCH,
        ),
        out_shape=[
            jax.ShapeDtypeStruct((4, 3, 256), F32),
            jax.ShapeDtypeStruct((4, 3, HD, 256), F32),
            jax.ShapeDtypeStruct((4, 256, 384), BF),
            jax.ShapeDtypeStruct((4, 256, 384), BF),
        ],
        compiler_params=pltpu.CompilerParams(vmem_limit_bytes=40 * MIB),
        cost_estimate=COST,
        name="attend_back_far",
    )(place, q, *do, o32, lse, *far)


def attend_back_near(place, q, do, lse, near, delta, dqt):
    keys = [whole((4, 256, 384)), whole((4, 256, 384))]
    return pl.pallas_call(
        grad_near_kernel,
        grid_spec=pltpu.PrefetchScalarGridSpec(
            num_scalar_prefetch=1,
            grid=(4,),
            in_specs=[of_slot((256, 192))] + [whole((256, 192))] * 4 + [of_slot((3, 256))] + keys + [of_slot((3, 256)), of_slot((3, HD, 256))],
            out_specs=[of_slot((256, 192))] + keys,
            scratch_shapes=GRAD_SCRATCH,
        ),
        out_shape=[
            jax.ShapeDtypeStruct((4, 256, 192), BF),
            jax.ShapeDtypeStruct((4, 256, 384), BF),
            jax.ShapeDtypeStruct((4, 256, 384), BF),
        ],
        compiler_params=pltpu.CompilerParams(vmem_limit_bytes=40 * MIB),
        cost_estimate=COST,
        name="attend_back_near",
    )(place, q, *do, lse, *near, delta, dqt)


def prep_kernel(place, x0_ref, x1_ref, x2_ref, x3_ref, x4_ref, w_ref, bias_ref, gain_ref, shift_ref, xhat_ref, q_ref, kv_ref, far_ref):
    for i, x_ref in enumerate((x4_ref, x0_ref, x1_ref, x2_ref, x3_ref)):
        @pl.when(pl.program_id(0) == i)
        def _():
            x = x_ref[...].astype(F32)
            center = x - jnp.mean(x, axis=-1, keepdims=True)
            spread = jnp.mean(center * center, axis=-1, keepdims=True)
            xhat = center * lax.rsqrt(spread + 1e-05)
            h1 = (xhat * gain_ref[...] + shift_ref[...]).astype(BF)
            qkv = jnp.dot(h1, w_ref[0], preferred_element_type=F32) + bias_ref[0]
            if i == 0:
                far_ref[...] = qkv[:, 192:].astype(BF)
            else:
                xhat_ref[0] = xhat.astype(BF)
                q_ref[0] = qkv[:, :192].astype(BF) * jnp.asarray(0.125, BF)
                kv_ref[0] = qkv[:, 192:].astype(BF)


def prep(place, blocks, w_groups, bias_groups, gain, shift):
    def after(shape):
        return pl.BlockSpec((1,) + shape, lambda i, *_: (jnp.maximum(i - 1, 0),) + (0,) * len(shape))

    return pl.pallas_call(
        prep_kernel,
        grid_spec=pltpu.PrefetchScalarGridSpec(
            num_scalar_prefetch=1,
            grid=(5,),
            in_specs=[whole((256, 768))] * 5
            + [
                pl.BlockSpec((1, 768, 576), lambda i, place: (place[0], 0, 0)),
                pl.BlockSpec((1, 1, 576), lambda i, place: (place[0], 0, 0)),
                whole((1, 768)),
                whole((1, 768)),
            ],
            out_specs=[after((256, 768)), after((256, 192)), after((256, 384)), whole((256, 384))],
        ),
        out_shape=[
            jax.ShapeDtypeStruct((4, 256, 768), BF),
            jax.ShapeDtypeStruct((4, 256, 192), BF),
            jax.ShapeDtypeStruct((4, 256, 384), BF),
            jax.ShapeDtypeStruct((256, 384), BF),
        ],
        compiler_params=pltpu.CompilerParams(vmem_limit_bytes=32 * MIB),
        cost_estimate=COST,
        name="prep",
    )(place, *blocks, w_groups, bias_groups, gain.reshape(1, 768), shift.reshape(1, 768))


FIRST = ("x", "y")
SECOND = ("y", "z")
REST = ("z", "x")
KEYS = ("x", "z")


def shift_pairs(axes, step, pairwise=False):
    pairs = []
    for s in range(16):
        for b in range(8):
            at = {"y": s // 4, "z": (s // 2 % 2) * 2 + b // 4, "c": s % 2, "x": b % 4}
            axis = axes[at["c"]]
            at[axis] = at[axis] ^ step if pairwise else (at[axis] + step) % (2 if axis == "c" else 4)
            source = (at["y"] * 4 + (at["z"] // 2) * 2 + at["c"]) * 8 + (at["z"] % 2) * 4 + at["x"]
            pairs.append((source, s * 8 + b))
    return pairs


def fetch(array, axes, step):
    if isinstance(axes, str):
        axes = (axes, axes)
    return lax.ppermute(array, ("seq", "batch"), shift_pairs(axes, step))


def fetch_all(array, axes):
    return [fetch(array, axes, step) for step in (1, 2, 3)]


def roll_slots(pieces, index):
    count = len(pieces)
    stacked = jnp.stack(pieces + pieces[:-1])
    return lax.dynamic_slice_in_dim(stacked, lax.rem(count - index, count), count, 0)


def sum_pairs(array, axes):
    for step in (2, 1):
        array = (array.astype(F32) + fetch_pair(array, axes, step).astype(F32)).astype(array.dtype)
    return array


def halve(array, axes, index):
    for step in (2, 1):
        parts = array.reshape(2, -1, *array.shape[1:])
        side = lax.rem(index // step, 2)
        kept = lax.dynamic_index_in_dim(parts, side, 0, keepdims=False)
        other = fetch_pair(lax.dynamic_index_in_dim(parts, 1 - side, 0, keepdims=False), axes, step)
        array = (kept.astype(F32) + other.astype(F32)).astype(array.dtype)
    return array


def fetch_sides(array, axes):
    return fetch(array, axes, 1), fetch(array, axes, 3)


def fetch_halves(side1, side3, axes):
    half = side1.shape[0] // 2
    return fetch(side1[:half], axes, 1), fetch(side3[half:], axes, 3)


def fetch_pair(array, axes, step):
    if isinstance(axes, str):
        axes = (axes, axes)
    return lax.ppermute(array, ("seq", "batch"), shift_pairs(axes, step, True))


def all_gather(array, axes, index):
    return roll_slots([array] + fetch_all(array, axes), index)


def feed_kernel(place, a0, a1, a2, a3, x_ref, dy_ref, w_out_ref, w_up_ref, w_down_ref, b_out_ref, gain_ref, shift_ref, b_up_ref, b_down_ref, result_ref, mid_grad_ref, d0, d1, d2, d3, g_ref, du_ref, h2_ref, da_ref, at_ref, send_ref, rows_ref, mid_ref, turned_ref, sum_ref, grad_ref):
    step = pl.program_id(0)
    core = place[2]

    @pl.when(step == 0)
    def _():
        for e, ref in enumerate((a0, a1, a2, a3)):
            turned_ref[:, e * 192 : (e + 1) * 192] = ref[...]
            for group in range(4):
                @pl.when(lax.rem(place[0] + e, 4) == group)
                def _():
                    at = group % 2 * 192

                    @pl.when(core == group // 2)
                    def _():
                        at_ref[:, at : at + 192] = ref[...]

                    @pl.when(core != group // 2)
                    def _():
                        send_ref[:, 4608 + at : 4800 + at] = ref[...]

        mid = x_ref[...].astype(F32) + jnp.dot(turned_ref[...], w_out_ref[...], preferred_element_type=F32) + b_out_ref[...]
        mid_ref[...] = mid
        center = mid - jnp.mean(mid, axis=-1, keepdims=True)
        xhat = center * lax.rsqrt(jnp.mean(center * center, axis=-1, keepdims=True) + 1e-05)
        h2 = (xhat * gain_ref[...] + shift_ref[...]).astype(BF)
        h2_ref[...] = h2
        send_ref[:, 3072:3840] = h2
        rows_ref[...] = jnp.zeros(rows_ref.shape, F32)
        rows_ref[3:4, :] = jnp.sum(dy_ref[...].astype(F32), axis=0, keepdims=True)

    u = jnp.dot(h2_ref[...], w_up_ref[...], preferred_element_type=F32) + b_up_ref[...]
    grad_act = nt(dy_ref[...], w_down_ref[...])
    scale = 0.7978845608028654
    square = u * u
    t = jnp.tanh(scale * u * (1.0 + 0.044715 * square))
    half = 0.5 + 0.5 * t
    g = (u * half).astype(BF)
    slope = half + 0.5 * u * (1.0 - t * t) * scale * (1.0 + 3 * 0.044715 * square)
    du = (grad_act * slope).astype(BF)
    out = jnp.dot(g, w_down_ref[...], preferred_element_type=F32)
    back = nt(du, w_up_ref[...])
    total = jnp.sum(du.astype(F32), axis=0, keepdims=True)
    for j in range(4):
        @pl.when(step == j)
        def _():
            rows_ref[6 + j : 7 + j, :] = total
            sum_ref[...] = out if j == 0 else sum_ref[...] + out
            grad_ref[...] = back if j == 0 else grad_ref[...] + back
            at = j % 2 * 768

            @pl.when(core == j // 2)
            def _():
                g_ref[:, at : at + 768] = g
                du_ref[:, at : at + 768] = du

            @pl.when(core != j // 2)
            def _():
                send_ref[:, at : at + 768] = g
                send_ref[:, 1536 + at : 2304 + at] = du

    @pl.when(step == 3)
    def _():
        mid = mid_ref[...]
        result_ref[...] = (mid + sum_ref[...] + b_down_ref[...]).astype(BF)
        center = mid - jnp.mean(mid, axis=-1, keepdims=True)
        norm = lax.rsqrt(jnp.mean(center * center, axis=-1, keepdims=True) + 1e-05)
        xhat = center * norm
        dh2 = grad_ref[...]
        rows_ref[4:5, :] = jnp.sum(dh2 * xhat, axis=0, keepdims=True)
        rows_ref[5:6, :] = jnp.sum(dh2, axis=0, keepdims=True)
        grad = dh2 * gain_ref[...]
        inner = grad - jnp.mean(grad, axis=-1, keepdims=True) - xhat * jnp.mean(grad * xhat, axis=-1, keepdims=True)
        mid_grad = dy_ref[...].astype(F32) + norm * inner
        mid_grad_ref[...] = mid_grad
        da = mid_grad.astype(BF)
        da_ref[...] = da
        send_ref[:, 3840:4608] = da
        rows_ref[2:3, :] = jnp.sum(da.astype(F32), axis=0, keepdims=True)
        do = nt(da, w_out_ref[...]).astype(BF)
        for e, ref in enumerate((d0, d1, d2, d3)):
            ref[...] = do[:, e * 192 : (e + 1) * 192]


def feed(place, heads, x, dy, w_out, w_up, w_down, b_out, gain, shift, b_up, b_down):
    tile = whole((256, 768))
    row = whole((1, 768))
    part = whole((256, 192))
    return pl.pallas_call(
        feed_kernel,
        grid_spec=pltpu.PrefetchScalarGridSpec(
            num_scalar_prefetch=1,
            grid=(4,),
            in_specs=[part] * 4
            + [
                tile,
                tile,
                whole((768, 768)),
                pl.BlockSpec((768, 768), lambda i, place: (0, i)),
                pl.BlockSpec((768, 768), lambda i, place: (i, 0)),
                row,
                row,
                row,
                pl.BlockSpec((1, 768), lambda i, place: (0, i)),
                row,
            ],
            out_specs=[tile, tile]
            + [part] * 4
            + [whole((256, 1536)), whole((256, 1536)), tile, tile, whole((256, 384)), whole((256, 4992)), whole((64, 768))],
            scratch_shapes=[
                pltpu.VMEM((256, 768), F32),
                pltpu.VMEM((256, 768), BF),
                pltpu.VMEM((256, 768), F32),
                pltpu.VMEM((256, 768), F32),
            ],
        ),
        out_shape=[
            jax.ShapeDtypeStruct((256, 768), BF),
            jax.ShapeDtypeStruct((256, 768), F32),
        ]
        + [jax.ShapeDtypeStruct((256, 192), BF)] * 4
        + [jax.ShapeDtypeStruct((256, width), BF) for width in (1536, 1536, 768, 768, 384, 4992)]
        + [jax.ShapeDtypeStruct((64, 768), F32)],
        compiler_params=pltpu.CompilerParams(vmem_limit_bytes=60 * MIB),
        cost_estimate=COST,
        name="feed",
    )(
        place,
        *heads,
        x,
        dy,
        w_out,
        w_up,
        w_down,
        b_out.reshape(1, 768),
        gain.reshape(1, 768),
        shift.reshape(1, 768),
        b_up.reshape(1, 3072),
        b_down.reshape(1, 768),
    )


def weights_kernel(info, g, dy, du, h2, at, da, g2, dy2, du2, h22, at2, da2, b0, b1, b2, b3, out_scr):
    a1 = pl.program_id(0)

    @pl.when(a1 == 0)
    def _():
        out_scr[...] = tn(at[...], da[...]) + tn(at2[...], da2[...])

    down = (tn(g[...], dy[...]) + tn(g2[...], dy2[...])).astype(BF)
    up = (tn(h2[...], du[...]) + tn(h22[...], du2[...])).astype(BF)
    zero = jnp.zeros((8, 768), F32)
    slot_at = lax.rem(a1 + 4 - info[1], 4)
    for i, ref in enumerate((b0, b1, b2, b3)):
        @pl.when(slot_at == i)
        def _():
            for a2 in range(4):
                ref[a2, 0:96, :] = down[a2 * 96 : (a2 + 1) * 96]
                ref[a2, 96:192, :] = up[a2 * 96 : (a2 + 1) * 96]
                rest = out_scr[pl.ds(pl.multiple_of(a1 * 96 + a2 * 24, 8), 24), :]
                ref[a2, 192:224, :] = jnp.concatenate([rest, zero], axis=0).astype(BF)


def weights(info, g, dy, du, h2, at, da, received, dy_received):
    def cols(width, index):
        return pl.BlockSpec((256, width), lambda i, info: (0, index(i, info)))

    full = whole((256, 768))
    return pl.pallas_call(
        weights_kernel,
        grid_spec=pltpu.PrefetchScalarGridSpec(
            num_scalar_prefetch=1,
            grid=(4,),
            in_specs=[
                cols(384, lambda i, info: i),
                full,
                cols(768, lambda i, info: i // 2),
                cols(384, lambda i, info: i % 2),
                whole((256, 384)),
                full,
                cols(384, lambda i, info: i),
                full,
                cols(768, lambda i, info: 2 + i // 2),
                cols(384, lambda i, info: 8 + i % 2),
                cols(384, lambda i, info: 12),
                cols(768, lambda i, info: 5),
            ],
            out_specs=[whole((4, 224, 768))] * 4,
            scratch_shapes=[pltpu.VMEM((384, 768), F32)],
        ),
        out_shape=[jax.ShapeDtypeStruct((4, 224, 768), BF)] * 4,
        compiler_params=pltpu.CompilerParams(vmem_limit_bytes=60 * MIB),
        cost_estimate=COST,
        name="weights",
    )(info, g, dy, du, h2, at, da, received, dy_received, received, received, received, received)


def add_kernel(info, p0, p1, p2, p3, *outs):
    total = p0[0].astype(F32) + p1[0].astype(F32) + p2[0].astype(F32) + p3[0].astype(F32)
    for i, out in enumerate(outs):
        @pl.when(pl.program_id(0) == i)
        def _():
            out[...] = total.astype(BF)


def add_pieces(info, pieces):
    spec = pl.BlockSpec((1, 224, 768), lambda i, info: (lax.rem(info[2] + i, 4), 0, 0))
    return pl.pallas_call(
        add_kernel,
        grid_spec=pltpu.PrefetchScalarGridSpec(
            num_scalar_prefetch=1, grid=(4,), in_specs=[spec] * 4, out_specs=[whole((224, 768))] * 4
        ),
        out_shape=[jax.ShapeDtypeStruct((224, 768), BF)] * 4,
        compiler_params=pltpu.CompilerParams(vmem_limit_bytes=24 * MIB),
        cost_estimate=COST,
        name="add_pieces",
    )(info, *pieces)


def place_kernel(counts, info, *refs):
    down, up, out = refs[-3:]
    for i, count in enumerate(counts):
        @pl.when(pl.program_id(0) == i)
        def _():
            base = sum(counts[:i])
            for r2 in range(4):
                a2 = lax.rem(info[2] + r2, 4)
                rows = refs[base + r2 * count // 4][r2 % (4 // count)].astype(F32)
                at = pl.multiple_of(a2 * 96, 96)
                down[pl.ds(at, 96), :] = rows[0:96]
                up[pl.ds(at, 96), :] = rows[96:192]
                out[pl.ds(pl.multiple_of(a2 * 24, 8), 24), :] = rows[192:216]


def place_weights(info, slots, pieces, others=()):
    arrays = [array for piece in pieces for array in piece]

    def first(i, info):
        slot_at = slots[0]
        for j, other in enumerate(slots):
            slot_at = jnp.where(i == j, other, slot_at)
        return lax.rem(info[1] + slot_at, 4)

    def by_rows(i, info):
        return (info[0] * 4 + first(i, info), 0)

    def by_columns(i, info):
        return (lax.rem(first(i, info), 2), info[0] * 2 + first(i, info) // 2)

    return pl.pallas_call(
        functools.partial(place_kernel, [len(piece) for piece in pieces]),
        grid_spec=pltpu.PrefetchScalarGridSpec(
            num_scalar_prefetch=1,
            grid=(len(pieces),),
            in_specs=[whole(array.shape) for array in arrays] + [pl.BlockSpec(memory_space=pl.ANY)] * len(others),
            out_specs=[pl.BlockSpec((384, 768), by_rows), pl.BlockSpec((384, 768), by_columns), pl.BlockSpec((96, 768), by_rows)],
        ),
        out_shape=[
            jax.ShapeDtypeStruct((3072, 768), F32),
            jax.ShapeDtypeStruct((768, 3072), F32),
            jax.ShapeDtypeStruct((768, 768), F32),
        ],
        input_output_aliases={1 + len(arrays) + i: i for i in range(len(others))},
        compiler_params=pltpu.CompilerParams(vmem_limit_bytes=32 * MIB),
        cost_estimate=COST,
        name="place_weights",
    )(info, *arrays, *others)


def moment_kernel(place, xhat_ref, dq_ref, near0_ref, near1_ref, far_ref, w_ref, gain_ref, shift_ref, rows_ref, p0, p1, p2, p3, give_ref, keep_ref, dqkv_ref):
    step = pl.program_id(0)

    @pl.when(step == 0)
    def _():
        for i, piece in enumerate((p0, p1, p2, p3)):
            dkv = near0_ref[i].astype(F32) + near1_ref[i].astype(F32) + far_ref[i].astype(F32)
            piece[:, :192] = dq_ref[i]
            piece[:, 192:] = dkv.astype(BF)
            dqkv_ref[i * 256 : (i + 1) * 256, :] = piece[...]

    dqkv = dqkv_ref[...]
    moment = tn(xhat_ref[...], dqkv)
    total = jnp.sum(dqkv.astype(F32), axis=0, keepdims=True)
    w = w_ref[0].astype(F32)
    gain = jnp.sum(w * moment, axis=1, keepdims=True)
    shift = jnp.sum(w * total, axis=1, keepdims=True)
    gw = (gain_ref[...] * moment + shift_ref[...] * total).astype(BF)
    lane = lax.broadcasted_iota(jnp.int32, (384, 64), 1)
    here = lax.rem(place[2] + 1 + step, 2)
    ends = jnp.concatenate([total[:, 384:], jnp.zeros((1, 192), F32)], axis=1)
    total_here = jnp.where(here == 0, total[:, :384], ends)
    row = lax.broadcasted_iota(jnp.int32, (64, 384), 0)
    vectors = jnp.where(row == 10, total_here, rows_ref[...]).T
    vectors = jnp.where(lane == 0, gain, jnp.where(lane == 1, shift, vectors)).astype(BF)

    def put(ref):
        ref[:, :576] = gw
        ref[:, 576:640] = vectors

    @pl.when(step == 0)
    def _():
        put(give_ref)

    @pl.when(step == 1)
    def _():
        put(keep_ref)


def moments(place, xhat, dq, near0, near1, far, w_groups, gain, shift, rows):
    def half(i, place):
        return lax.rem(place[2] + 1 + i, 2)

    return pl.pallas_call(
        moment_kernel,
        grid_spec=pltpu.PrefetchScalarGridSpec(
            num_scalar_prefetch=1,
            grid=(2,),
            in_specs=[
                pl.BlockSpec((1024, 384), lambda i, place: (0, half(i, place))),
                whole((4, 256, 192)),
                whole((4, 256, 384)),
                whole((4, 256, 384)),
                whole((4, 256, 384)),
                pl.BlockSpec((1, 384, 576), lambda i, place: (place[0], half(i, place), 0)),
                pl.BlockSpec((384, 1), lambda i, place: (half(i, place), 0)),
                pl.BlockSpec((384, 1), lambda i, place: (half(i, place), 0)),
                pl.BlockSpec((64, 384), lambda i, place: (0, half(i, place))),
            ],
            out_specs=[whole((256, 576))] * 4 + [whole((384, 640))] * 2,
            scratch_shapes=[pltpu.VMEM((1024, 576), BF)],
        ),
        out_shape=[jax.ShapeDtypeStruct((256, 576), BF)] * 4 + [jax.ShapeDtypeStruct((384, 640), BF)] * 2,
        compiler_params=pltpu.CompilerParams(vmem_limit_bytes=40 * MIB),
        cost_estimate=COST,
        name="moments",
    )(place, xhat.reshape(1024, 768), dq, near0, near1, far, w_groups, gain.reshape(768, 1), shift.reshape(768, 1), rows)


def regroup_kernel(w_ref, out_ref):
    for group in range(4):
        @pl.when(pl.program_id(0) == group)
        def _():
            at = group * 192
            out_ref[0, :, :192] = w_ref[:, at : at + 192]
            for h in range(3):
                for t in range(2):
                    to = 192 + h * 128 + t * HD
                    first = 768 * (t + 1) + at + h * HD
                    out_ref[0, :, to : to + HD] = w_ref[:, first : first + HD]


def regroup(w):
    return pl.pallas_call(
        regroup_kernel,
        grid=(4,),
        in_specs=[pl.BlockSpec((768, 2304), lambda i: (0, 0))],
        out_specs=pl.BlockSpec((1, 768, 576), lambda i: (i, 0, 0)),
        out_shape=jax.ShapeDtypeStruct((4, 768, 576), BF),
        compiler_params=pltpu.CompilerParams(vmem_limit_bytes=24 * MIB),
        cost_estimate=COST,
        name="regroup",
    )(w)


def finish_kernel(place, p0, p1, p2, p3, w_ref, x_ref, gain_ref, mid_ref, out_ref, acc_ref):
    e = pl.program_id(0)
    for i, piece in enumerate((p0, p1, p2, p3)):
        @pl.when(e == i)
        def _():
            part = nt(piece[...], w_ref[0])
            acc_ref[...] = part if i == 0 else acc_ref[...] + part

    @pl.when(e == 3)
    def _():
        x = x_ref[...].astype(F32)
        center = x - jnp.mean(x, axis=-1, keepdims=True)
        scale = lax.rsqrt(jnp.mean(center * center, axis=-1, keepdims=True) + 1e-05)
        xhat = center * scale
        grad = acc_ref[...] * gain_ref[...]
        inner = grad - jnp.mean(grad, axis=-1, keepdims=True) - xhat * jnp.mean(grad * xhat, axis=-1, keepdims=True)
        out_ref[...] = mid_ref[...] + scale * inner


def finish(place, pieces, w_groups, x, gain, middle):
    return pl.pallas_call(
        finish_kernel,
        grid_spec=pltpu.PrefetchScalarGridSpec(
            num_scalar_prefetch=1,
            grid=(4,),
            in_specs=[whole((256, 576))] * 4
            + [
                pl.BlockSpec((1, 768, 576), lambda i, place: (lax.rem(place[0] + i, 4), 0, 0)),
                whole((256, 768)),
                whole((1, 768)),
                whole((256, 768)),
            ],
            out_specs=whole((256, 768)),
            scratch_shapes=[pltpu.VMEM((256, 768), F32)],
        ),
        out_shape=jax.ShapeDtypeStruct((256, 768), F32),
        compiler_params=pltpu.CompilerParams(vmem_limit_bytes=24 * MIB),
        cost_estimate=COST,
        name="finish",
    )(place, *pieces, w_groups, x, gain.reshape(1, 768), middle)


def join_kernel(own, other, *refs):
    pieces, (out_ref, rows_ref) = refs[:8], refs[8:]
    for o, info in enumerate((own, other)):
        @pl.when(pl.program_id(0) == o)
        def _():
            def put(rows, part, group):
                to = pl.ds(pl.multiple_of(part * 96, 96), 96)
                rows = rows.astype(F32)
                out_ref[to, group * 192 : (group + 1) * 192] = rows[:, :192]
                for h in range(3):
                    for t in range(2):
                        start = 192 + h * 128 + t * HD
                        column = 768 * (t + 1) + group * 192 + h * HD
                        out_ref[to, column : column + HD] = rows[:, start : start + HD]
                rows_ref[group, to, :] = rows[:, 512:640]

            for r1 in range(4):
                piece = pieces[o * 4 + r1]
                first = lax.rem(info[1] + r1, 4)

                @pl.when(info[0] == 0)
                def _():
                    for group in range(4):
                        put(piece[lax.rem(group + 4 - info[2], 4)], first, group)

                for group in range(4):
                    @pl.when(jnp.logical_and(info[0] == 1, first == group))
                    def _():
                        for r2 in range(4):
                            put(piece[r2], lax.rem(info[2] + r2, 4), group)


def join_qkv(own, other, pieces, others):
    piece = pl.BlockSpec((4, 96, 640), lambda o, own, other: (0, 0, 0))
    return pl.pallas_call(
        join_kernel,
        grid_spec=pltpu.PrefetchScalarGridSpec(
            num_scalar_prefetch=2,
            grid=(2,),
            in_specs=[piece] * 8,
            out_specs=[
                pl.BlockSpec((384, 2304), lambda o, own, other: (lax.rem(own[0] + o, 2), 0)),
                pl.BlockSpec((4, 384, 128), lambda o, own, other: (0, lax.rem(own[0] + o, 2), 0)),
            ],
        ),
        out_shape=[jax.ShapeDtypeStruct((768, 2304), F32), jax.ShapeDtypeStruct((4, 768, 128), F32)],
        compiler_params=pltpu.CompilerParams(vmem_limit_bytes=40 * MIB),
        cost_estimate=COST,
        name="join_qkv",
    )(own, other, *pieces, *others)


def region(always, work, *operands):
    shapes = jax.eval_shape(work, *operands)
    empty = jax.tree.map(lambda shape: jnp.zeros(shape.shape, shape.dtype), shapes)
    return lax.cond(always, work, lambda *args: empty, *operands)


def layer_norm(values, gain, shift):
    center = values - jnp.mean(values, axis=-1, keepdims=True)
    spread = jnp.mean(center * center, axis=-1, keepdims=True)
    return center * lax.rsqrt(spread + 1e-05) * gain + shift


def shards(
    tokens,
    cotangent,
    ln1_gain,
    ln1_shift,
    w_qkv,
    b_query,
    b_value,
    w_out,
    b_out,
    ln2_gain,
    ln2_shift,
    w_up,
    b_up,
    w_down,
    b_down,
):
    seq, batch = lax.axis_index("seq"), lax.axis_index("batch")
    y, zh, c = seq // 4, lax.rem(seq // 2, 2), lax.rem(seq, 2)
    z, x = zh * 2 + batch // 4, lax.rem(batch, 4)
    always = seq + batch >= 0
    place = jnp.stack([y, zh, c, x]).astype(jnp.int32)
    info = jnp.stack([c, jnp.where(c == 0, x, y), jnp.where(c == 0, y, z)]).astype(jnp.int32)
    other_info = jnp.stack([1 - c, jnp.where(c == 0, y, x), jnp.where(c == 0, z, y)]).astype(jnp.int32)

    tokens = tokens[0]
    dy_low = cotangent[0]
    columns = [tokens] + fetch_all(tokens, "y") + [fetch(tokens, "z", 2)]
    dy_other = fetch(dy_low, "c", 1)

    def by_group(array):
        parts = array.reshape(1, 3, 4, 3, HD)
        query = parts[:, 0].transpose(1, 0, 2, 3).reshape(4, 1, 192)
        keys = parts[:, 1:].transpose(2, 0, 3, 1, 4).reshape(4, 1, 384)
        return jnp.concatenate([query, keys], axis=2)

    w_groups = regroup(w_qkv)
    bias_groups = by_group(jnp.concatenate([b_query, jnp.zeros_like(b_query), b_value]))
    w_out_turned = lax.dynamic_slice_in_dim(jnp.concatenate([w_out, w_out]), y * 192, 768, 0)

    xhat, q, kv, far_first = prep(place, columns, w_groups, bias_groups, ln1_gain, ln1_shift)
    far_rest = fetch(kv[1:], "z", 2)
    near = (kv, fetch(kv, "c", 1))
    far = []

    def far_of(state):
        rest, *state = lax.optimization_barrier((far_rest, *state))
        keys = jnp.concatenate([far_first[None], rest])
        far.extend([keys, fetch(keys, "c", 1)])
        return state, far

    o, o32, lse = attend(place, q, near, far_of)

    heads = [o[0]] + [fetch(o[4 - e], "y", e) for e in (1, 2, 3)]
    fed = feed(place, heads, tokens, dy_low, w_out_turned, w_up, w_down, b_out, ln2_gain, ln2_shift, b_up, b_down)
    result, grad_middle, *do, g, du, h2, da, attended, send, vectors = fed

    do_mine = [do[0]] + [fetch(do[4 - e], "y", e) for e in (1, 2, 3)]
    received = fetch(send, "c", 1)
    pieces = weights(info, g, dy_low, du, h2, attended, da, received, dy_other)

    def back_far(*do_mine):
        delta, dqt, far0, far1 = attend_back_far(place, q, do_mine, o32, lse, far)
        return delta, dqt, (far0.astype(F32) + fetch(far1, "c", 1).astype(F32)).astype(BF)

    def back_near(delta, dqt, *do_mine):
        dq, near0, near1 = attend_back_near(place, q, do_mine, lse, near, delta, dqt)
        return dq, near0, fetch(near1, "c", 1)

    def scatter_beside(pieces, *do_mine):
        received = [fetch(pieces[d], FIRST, 4 - d) for d in (1, 2, 3)]
        delta, dqt, far_sum = region(always, back_far, *do_mine)
        far_received = fetch(far_sum, "z", 2)
        dq, near0, near1 = region(always, back_near, delta, dqt, *do_mine)
        dq, *received = lax.optimization_barrier((dq, *received))
        pieces = add_pieces(info, [pieces[0]] + received)
        moved = [fetch(pieces[d], SECOND, 4 - d) for d in (1, 2, 3)]
        moved = moments(place, xhat, dq, near0, near1, far_received, w_groups, ln1_gain, ln1_shift, vectors), pieces[0], moved
        return moved

    (dqkv0, dqkv1, dqkv2, dqkv3, given, gw), own, received = region(always, scatter_beside, pieces, *do_mine)
    pieces = [own] + received

    def sum_rest(pieces, given, gw):
        chunk = sum(p.astype(F32) for p in pieces).astype(BF)
        gw = (gw.astype(F32) + fetch(given, "c", 1).astype(F32)).astype(BF)
        return sum_pairs(chunk, REST), halve(gw, KEYS, jnp.where(c == 0, x, z))

    def rows_beside(dqkv1, dqkv2, dqkv3, *operands):
        rows = fetch(dqkv3, "y", 1), fetch(dqkv2, "y", 2), fetch(dqkv1, "y", 3)
        return *rows, *region(always, sum_rest, *operands)

    *parts, chunk, gw = region(always, rows_beside, dqkv1, dqkv2, dqkv3, pieces, given, gw)

    def sum_keys(gw):
        return (sum_pairs(gw, REST),)

    def gather_second(chunk, gw):
        return jnp.stack([chunk] + fetch_all(chunk, SECOND)), *region(always, sum_keys, gw)

    chunk, gw = region(always, gather_second, chunk, gw)

    def finish_keys_rows(gw, *parts):
        gw = jnp.stack([gw] + fetch_all(gw, SECOND))
        return gw, finish(place, parts, w_groups, tokens, ln1_gain, grad_middle)

    def gather_sides(chunk, *operands):
        return *fetch_sides(chunk, FIRST), *region(always, finish_keys_rows, *operands)

    side1, side3, gw, grad_inputs = region(always, gather_sides, chunk, gw, dqkv0, *parts)

    def place_near(*near):
        return place_weights(info, (0, 1, 3), [(piece,) for piece in near])

    def gather_far(*near):
        return *fetch_halves(near[1], near[2], FIRST), *[fetch(piece, "c", 1) for piece in near], *region(always, place_near, *near)

    low, high, other0, other1, other3, *placed = region(always, gather_far, chunk, side1, side3)

    def place_more(low, high, placed, *others):
        placed = place_weights(other_info, (0, 1, 3), [(piece,) for piece in others], placed)
        return place_weights(info, (2,), [(low, high)], placed)

    def gather_keys(gw, low, high, *operands):
        far = fetch(low, "c", 1), fetch(high, "c", 1)
        return *fetch_all(gw, FIRST), *far, *region(always, place_more, low, high, *operands)

    key1, key2, key3, *far, gw_down, gw_up, gw_out = region(always, gather_keys, gw, low, high, placed, other0, other1, other3)
    keys = (gw, key1, key2, key3)
    gw_qkv, columns = join_qkv(info, other_info, keys, [fetch(piece, "c", 1) for piece in keys])
    gw_down, gw_up, gw_out = place_weights(other_info, (2,), [far], (gw_down, gw_up, gw_out))
    sums = jnp.sum(columns[:, :, 64:74], axis=0)
    totals = columns[:, :576, 74]
    return (
        result[None],
        grad_inputs[None],
        sums[:, 0],
        sums[:, 1],
        gw_qkv,
        totals[:, :192].reshape(768),
        totals[:, 192:].reshape(4, 3, 2, HD)[:, :, 1].reshape(768),
        gw_out,
        sums[:, 2],
        sums[:, 4],
        sums[:, 5],
        gw_up,
        sums[:, 6:10].T.reshape(3072),
        gw_down,
        sums[:, 3],
    )


def solution(mesh):
    split = P("batch", "seq", None)
    return jax.shard_map(
        shards,
        mesh=mesh,
        in_specs=(split, split) + (P(),) * 13,
        out_specs=(split, split) + (P(),) * 13,
        check_vma=False,
    )
```

```python
import functools

import jax
import jax.numpy as jnp
from jax import lax
from jax.experimental import pallas as pl
from jax.experimental.pallas import tpu as pltpu
from jax.sharding import PartitionSpec as P

HD = 64
LOG2E = 1.4426950408889634
BF = jnp.bfloat16
F32 = jnp.float32
MIB = 2**20
COST = pl.CostEstimate(flops=1000, bytes_accessed=1000, transcendentals=0)


def nt(left, right):
    return lax.dot_general(left, right, (((1,), (1,)), ((), ())), preferred_element_type=F32)


def tn(left, right):
    return lax.dot_general(left, right, (((0,), (0,)), ((), ())), preferred_element_type=F32)


def whole(shape):
    return pl.BlockSpec(shape, lambda i, *_: (0,) * len(shape))


def of_slot(shape):
    return pl.BlockSpec((1,) + shape, lambda i, *_: (i,) + (0,) * len(shape))


def causal(scores, other):
    keys = lax.broadcasted_iota(jnp.int32, scores.shape, 0)
    queries = lax.broadcasted_iota(jnp.int32, scores.shape, 1)
    return jnp.where(keys <= queries, scores, other)


def query_y(place):
    return lax.rem(place[0] + pl.program_id(0), 4)


def slot(place, y):
    return lax.rem(y + 4 - place[0], 4)


def softmax_step(q_ref, m_ref, l_ref, acc_ref, blocks, masks):
    scores = []
    for h in range(3):
        q = q_ref[0, :, h * HD : (h + 1) * HD]
        row = [nt(block[:, h * 128 : h * 128 + HD], q) * LOG2E for block in blocks]
        scores.append([mask(s, -1e30) if mask else s for s, mask in zip(row, masks)])
    probs = []
    for h in range(3):
        old = m_ref[0, h : h + 1, :]
        new = old
        for s in scores[h]:
            new = jnp.maximum(new, jnp.max(s, axis=0, keepdims=True))
        factor = jnp.exp2(old - new)
        m_ref[0, h : h + 1, :] = new
        row = [jnp.exp2(s - new) for s in scores[h]]
        l_ref[0, h : h + 1, :] = l_ref[0, h : h + 1, :] * factor + sum(jnp.sum(p, axis=0, keepdims=True) for p in row)
        probs.append((row, factor))
    for h in range(3):
        row, factor = probs[h]
        acc = acc_ref[0, h] * factor
        for block, p in zip(blocks, row):
            acc = acc + tn(block[:, h * 128 + HD : (h + 1) * 128], p.astype(BF))
        acc_ref[0, h] = acc


def attend_near_kernel(place, q_ref, kv0_ref, kv1_ref, first0_ref, first1_ref, m_ref, l_ref, acc_ref):
    own = pl.program_id(0)
    m_ref[...] = jnp.full(m_ref.shape, -1e30, F32)
    l_ref[...] = jnp.zeros(l_ref.shape, F32)
    acc_ref[...] = jnp.zeros(acc_ref.shape, F32)

    def beside(scores, other):
        return jnp.where(place[2] == 1, scores, other)

    softmax_step(q_ref, m_ref, l_ref, acc_ref, [kv0_ref[own], kv1_ref[own]], [causal, beside])

    @pl.when(place[0] < query_y(place) + place[1])
    def _():
        softmax_step(q_ref, m_ref, l_ref, acc_ref, [first0_ref[...], first1_ref[...]], [None, None])

    def body(y, carry):
        at = slot(place, y)
        softmax_step(q_ref, m_ref, l_ref, acc_ref, [kv0_ref[at], kv1_ref[at]], [None, None])
        return carry

    lax.fori_loop(0, query_y(place), body, 0)


def attend_far_kernel(place, q_ref, kv0_ref, kv1_ref, m_in, l_in, acc_in, o_ref, o32_ref, lse_ref, m_ref, l_ref, acc_ref):
    m_ref[...] = m_in[...]
    l_ref[...] = l_in[...]
    acc_ref[...] = acc_in[...]

    def body(y, carry):
        @pl.when(y != place[0])
        def _():
            at = slot(place, y) - 1
            softmax_step(q_ref, m_ref, l_ref, acc_ref, [kv0_ref[at], kv1_ref[at]], [None, None])

        return carry

    lax.fori_loop(0, query_y(place) + place[1], body, 0)
    for h in range(3):
        o = (acc_ref[0, h] / l_ref[0, h : h + 1, :]).T
        o32_ref[0, :, h * HD : (h + 1) * HD] = o
        o_ref[0, :, h * HD : (h + 1) * HD] = o.astype(BF)
    lse_ref[...] = m_ref[...] + jnp.log2(l_ref[...])


def attend(place, q, near, far_of):
    stats = [of_slot((3, 256)), of_slot((3, 256)), of_slot((3, HD, 256))]
    stat_shapes = [
        jax.ShapeDtypeStruct((4, 3, 256), F32),
        jax.ShapeDtypeStruct((4, 3, 256), F32),
        jax.ShapeDtypeStruct((4, 3, HD, 256), F32),
    ]
    keys = [whole((4, 256, 384)), whole((4, 256, 384)), whole((256, 384)), whole((256, 384))]
    far_keys = [whole((3, 256, 384)), whole((3, 256, 384))]
    state = pl.pallas_call(
        attend_near_kernel,
        grid_spec=pltpu.PrefetchScalarGridSpec(
            num_scalar_prefetch=1, grid=(4,), in_specs=[of_slot((256, 192))] + keys, out_specs=stats
        ),
        out_shape=stat_shapes,
        compiler_params=pltpu.CompilerParams(vmem_limit_bytes=32 * MIB),
        cost_estimate=COST,
        name="attend_near",
    )(place, q, *near)
    state, far = far_of(state)
    return pl.pallas_call(
        attend_far_kernel,
        grid_spec=pltpu.PrefetchScalarGridSpec(
            num_scalar_prefetch=1,
            grid=(4,),
            in_specs=[of_slot((256, 192))] + far_keys + stats,
            out_specs=[of_slot((256, 192)), of_slot((256, 192)), of_slot((3, 256))],
            scratch_shapes=[pltpu.VMEM((1, 3, 256), F32), pltpu.VMEM((1, 3, 256), F32), pltpu.VMEM((1, 3, HD, 256), F32)],
        ),
        out_shape=[
            jax.ShapeDtypeStruct((4, 256, 192), BF),
            jax.ShapeDtypeStruct((4, 256, 192), F32),
            jax.ShapeDtypeStruct((4, 3, 256), F32),
        ],
        compiler_params=pltpu.CompilerParams(vmem_limit_bytes=32 * MIB),
        cost_estimate=COST,
        name="attend_far",
    )(place, q, *far, *state)


def grad_step(lse_ref, qdo_ref, delta_ref, dqt_ref, sums, blocks, at, masks):
    both = {}
    for h in range(3):
        for i, block in enumerate(blocks):
            both[h, i] = nt(block[:, h * 128 : (h + 1) * 128], qdo_ref[h])
    weights = {}
    for h in range(3):
        for i, mask in enumerate(masks):
            p = jnp.exp2(both[h, i][:, :256] * LOG2E - lse_ref[0, h : h + 1, :])
            if mask:
                p = mask(p, 0.0)
            ds = (p * (both[h, i][:, 256:] - delta_ref[h])).astype(BF)
            weights[h, i] = (ds, p.astype(BF))
    for h in range(3):
        dqt = dqt_ref[h]
        for i, block in enumerate(blocks):
            ds, p = weights[h, i]
            sums[i][at, :, h * 128 : (h + 1) * 128] += jnp.dot(
                jnp.concatenate([ds, p], axis=1), qdo_ref[h], preferred_element_type=F32
            )
            dqt = dqt + tn(block[:, h * 128 : h * 128 + HD], ds)
        dqt_ref[h] = dqt


def grad_start(q_ref, do_refs, delta_of, qdo_ref, delta_ref, sums):
    @pl.when(pl.program_id(0) == 0)
    def _():
        for total in sums:
            total[...] = jnp.zeros(total.shape, F32)

    zero = jnp.zeros((256, HD), BF)
    for i, do_ref in enumerate(do_refs):
        @pl.when(pl.program_id(0) == i)
        def _():
            for h in range(3):
                do = do_ref[:, h * HD : (h + 1) * HD]
                qdo_ref[h, :256, :] = jnp.concatenate([q_ref[0, :, h * HD : (h + 1) * HD], zero], axis=1)
                qdo_ref[h, 256:, :] = jnp.concatenate([zero, do], axis=1)
                delta_ref[h] = delta_of(h, do)


def grad_end(sums, outs):
    @pl.when(pl.program_id(0) == 3)
    def _():
        for total, out in zip(sums, outs):
            out[...] = total[...].astype(BF)


def grad_far_kernel(place, q_ref, do0, do1, do2, do3, o32_ref, lse_ref, first0_ref, first1_ref, kv0_ref, kv1_ref, delta_out, dqt_out, g0_ref, g1_ref, qdo_ref, delta_ref, dqt_ref, sum0_ref, sum1_ref):
    sums = [sum0_ref, sum1_ref]

    def delta_of(h, do):
        prod = do.astype(F32) * o32_ref[0, :, h * HD : (h + 1) * HD]
        return jnp.sum(prod.T, axis=0, keepdims=True)

    grad_start(q_ref, (do0, do1, do2, do3), delta_of, qdo_ref, delta_ref, sums)
    dqt_ref[...] = jnp.zeros(dqt_ref.shape, F32)

    @pl.when(place[0] < query_y(place) + place[1])
    def _():
        grad_step(lse_ref, qdo_ref, delta_ref, dqt_ref, sums, [first0_ref[...], first1_ref[...]], 0, [None, None])

    def body(y, carry):
        @pl.when(y != place[0])
        def _():
            at = slot(place, y)
            grad_step(lse_ref, qdo_ref, delta_ref, dqt_ref, sums, [kv0_ref[at - 1], kv1_ref[at - 1]], at, [None, None])

        return carry

    lax.fori_loop(0, query_y(place) + place[1], body, 0)
    for h in range(3):
        delta_out[0, h : h + 1, :] = delta_ref[h]
        dqt_out[0, h] = dqt_ref[h]
    grad_end(sums, [g0_ref, g1_ref])


def grad_near_kernel(place, q_ref, do0, do1, do2, do3, lse_ref, kv0_ref, kv1_ref, delta_in, dqt_in, dq_ref, g0_ref, g1_ref, qdo_ref, delta_ref, dqt_ref, sum0_ref, sum1_ref):
    own = pl.program_id(0)
    sums = [sum0_ref, sum1_ref]
    grad_start(q_ref, (do0, do1, do2, do3), lambda h, do: delta_in[0, h : h + 1, :], qdo_ref, delta_ref, sums)
    dqt_ref[...] = dqt_in[0]

    def beside(probs, other):
        return jnp.where(place[2] == 1, probs, other)

    grad_step(lse_ref, qdo_ref, delta_ref, dqt_ref, sums, [kv0_ref[own], kv1_ref[own]], own, [causal, beside])

    def body(y, carry):
        at = slot(place, y)
        grad_step(lse_ref, qdo_ref, delta_ref, dqt_ref, sums, [kv0_ref[at], kv1_ref[at]], at, [None, None])
        return carry

    lax.fori_loop(0, query_y(place), body, 0)
    for h in range(3):
        dq_ref[0, :, h * HD : (h + 1) * HD] = (dqt_ref[h].T * 0.125).astype(BF)
    grad_end(sums, [g0_ref, g1_ref])


GRAD_SCRATCH = [
    pltpu.VMEM((3, 512, 128), BF),
    pltpu.VMEM((3, 1, 256), F32),
    pltpu.VMEM((3, HD, 256), F32),
    pltpu.VMEM((4, 256, 384), F32),
    pltpu.VMEM((4, 256, 384), F32),
]


def attend_back_far(place, q, do, o32, lse, far):
    keys = [whole((4, 256, 384)), whole((4, 256, 384))]
    return pl.pallas_call(
        grad_far_kernel,
        grid_spec=pltpu.PrefetchScalarGridSpec(
            num_scalar_prefetch=1,
            grid=(4,),
            in_specs=[of_slot((256, 192))] + [whole((256, 192))] * 4 + [of_slot((256, 192)), of_slot((3, 256))] + [whole((256, 384))] * 2 + [whole((3, 256, 384))] * 2,
            out_specs=[of_slot((3, 256)), of_slot((3, HD, 256))] + keys,
            scratch_shapes=GRAD_SCRATCH,
        ),
        out_shape=[
            jax.ShapeDtypeStruct((4, 3, 256), F32),
            jax.ShapeDtypeStruct((4, 3, HD, 256), F32),
            jax.ShapeDtypeStruct((4, 256, 384), BF),
            jax.ShapeDtypeStruct((4, 256, 384), BF),
        ],
        compiler_params=pltpu.CompilerParams(vmem_limit_bytes=40 * MIB),
        cost_estimate=COST,
        name="attend_back_far",
    )(place, q, *do, o32, lse, *far)


def attend_back_near(place, q, do, lse, near, delta, dqt):
    keys = [whole((4, 256, 384)), whole((4, 256, 384))]
    return pl.pallas_call(
        grad_near_kernel,
        grid_spec=pltpu.PrefetchScalarGridSpec(
            num_scalar_prefetch=1,
            grid=(4,),
            in_specs=[of_slot((256, 192))] + [whole((256, 192))] * 4 + [of_slot((3, 256))] + keys + [of_slot((3, 256)), of_slot((3, HD, 256))],
            out_specs=[of_slot((256, 192))] + keys,
            scratch_shapes=GRAD_SCRATCH,
        ),
        out_shape=[
            jax.ShapeDtypeStruct((4, 256, 192), BF),
            jax.ShapeDtypeStruct((4, 256, 384), BF),
            jax.ShapeDtypeStruct((4, 256, 384), BF),
        ],
        compiler_params=pltpu.CompilerParams(vmem_limit_bytes=40 * MIB),
        cost_estimate=COST,
        name="attend_back_near",
    )(place, q, *do, lse, *near, delta, dqt)


def prep_kernel(place, x0_ref, x1_ref, x2_ref, x3_ref, x4_ref, w_ref, bias_ref, gain_ref, shift_ref, xhat_ref, q_ref, kv_ref, far_ref):
    for i, x_ref in enumerate((x4_ref, x0_ref, x1_ref, x2_ref, x3_ref)):
        @pl.when(pl.program_id(0) == i)
        def _():
            x = x_ref[...].astype(F32)
            center = x - jnp.mean(x, axis=-1, keepdims=True)
            spread = jnp.mean(center * center, axis=-1, keepdims=True)
            xhat = center * lax.rsqrt(spread + 1e-05)
            h1 = (xhat * gain_ref[...] + shift_ref[...]).astype(BF)
            qkv = jnp.dot(h1, w_ref[0], preferred_element_type=F32) + bias_ref[0]
            if i == 0:
                far_ref[...] = qkv[:, 192:].astype(BF)
            else:
                xhat_ref[0] = xhat.astype(BF)
                q_ref[0] = qkv[:, :192].astype(BF) * jnp.asarray(0.125, BF)
                kv_ref[0] = qkv[:, 192:].astype(BF)


def prep(place, blocks, w_groups, bias_groups, gain, shift):
    def after(shape):
        return pl.BlockSpec((1,) + shape, lambda i, *_: (jnp.maximum(i - 1, 0),) + (0,) * len(shape))

    return pl.pallas_call(
        prep_kernel,
        grid_spec=pltpu.PrefetchScalarGridSpec(
            num_scalar_prefetch=1,
            grid=(5,),
            in_specs=[whole((256, 768))] * 5
            + [
                pl.BlockSpec((1, 768, 576), lambda i, place: (place[0], 0, 0)),
                pl.BlockSpec((1, 1, 576), lambda i, place: (place[0], 0, 0)),
                whole((1, 768)),
                whole((1, 768)),
            ],
            out_specs=[after((256, 768)), after((256, 192)), after((256, 384)), whole((256, 384))],
        ),
        out_shape=[
            jax.ShapeDtypeStruct((4, 256, 768), BF),
            jax.ShapeDtypeStruct((4, 256, 192), BF),
            jax.ShapeDtypeStruct((4, 256, 384), BF),
            jax.ShapeDtypeStruct((256, 384), BF),
        ],
        compiler_params=pltpu.CompilerParams(vmem_limit_bytes=32 * MIB),
        cost_estimate=COST,
        name="prep",
    )(place, *blocks, w_groups, bias_groups, gain.reshape(1, 768), shift.reshape(1, 768))


FIRST = ("x", "y")
SECOND = ("y", "z")
REST = ("z", "x")
KEYS = ("x", "z")


def shift_pairs(axes, step, pairwise=False):
    pairs = []
    for s in range(16):
        for b in range(8):
            at = {"y": s // 4, "z": (s // 2 % 2) * 2 + b // 4, "c": s % 2, "x": b % 4}
            axis = axes[at["c"]]
            at[axis] = at[axis] ^ step if pairwise else (at[axis] + step) % (2 if axis == "c" else 4)
            source = (at["y"] * 4 + (at["z"] // 2) * 2 + at["c"]) * 8 + (at["z"] % 2) * 4 + at["x"]
            pairs.append((source, s * 8 + b))
    return pairs


def fetch(array, axes, step):
    if isinstance(axes, str):
        axes = (axes, axes)
    return lax.ppermute(array, ("seq", "batch"), shift_pairs(axes, step))


def fetch_all(array, axes):
    return [fetch(array, axes, step) for step in (1, 2, 3)]


def roll_slots(pieces, index):
    count = len(pieces)
    stacked = jnp.stack(pieces + pieces[:-1])
    return lax.dynamic_slice_in_dim(stacked, lax.rem(count - index, count), count, 0)


def sum_pairs(array, axes):
    for step in (2, 1):
        array = (array.astype(F32) + fetch_pair(array, axes, step).astype(F32)).astype(array.dtype)
    return array


def halve(array, axes, index):
    for step in (2, 1):
        parts = array.reshape(2, -1, *array.shape[1:])
        side = lax.rem(index // step, 2)
        kept = lax.dynamic_index_in_dim(parts, side, 0, keepdims=False)
        other = fetch_pair(lax.dynamic_index_in_dim(parts, 1 - side, 0, keepdims=False), axes, step)
        array = (kept.astype(F32) + other.astype(F32)).astype(array.dtype)
    return array


def fetch_sides(array, axes):
    return fetch(array, axes, 1), fetch(array, axes, 3)


def fetch_halves(side1, side3, axes):
    half = side1.shape[0] // 2
    return fetch(side1[:half], axes, 1), fetch(side3[half:], axes, 3)


def fetch_pair(array, axes, step):
    if isinstance(axes, str):
        axes = (axes, axes)
    return lax.ppermute(array, ("seq", "batch"), shift_pairs(axes, step, True))


def all_gather(array, axes, index):
    return roll_slots([array] + fetch_all(array, axes), index)


def feed_kernel(place, a0, a1, a2, a3, x_ref, dy_ref, w_out_ref, w_up_hbm, w_down_hbm, b_out_ref, gain_ref, shift_ref, b_up_ref, b_down_ref, result_ref, mid_grad_ref, d0, d1, d2, d3, g_ref, du_ref, h2_ref, da_ref, at_ref, send_ref, rows_ref, turned_ref, up_ref, down_ref, hidden, send_scr, up_sem, down_sem, own_sem, send_sem):
    core = place[2]
    copies = []
    for j in range(2):
        part = pl.ds(j * 1536, 1536)
        copies.append(pltpu.make_async_copy(w_up_hbm.at[:, part], up_ref.at[j], up_sem.at[j]))
        copies.append(pltpu.make_async_copy(w_down_hbm.at[part, :], down_ref.at[j], down_sem.at[j]))
    for copy in copies:
        copy.start()
    own, sent = [], []
    for k, ref in enumerate((g_ref, du_ref)):
        own.append(pltpu.make_async_copy(hidden.at[core, k], ref, own_sem.at[k]))
        sent.append(pltpu.make_async_copy(hidden.at[1 - core, k], send_ref.at[:, pl.ds(k * 1536, 1536)], send_sem.at[k]))
    sent.append(pltpu.make_async_copy(send_scr, send_ref.at[:, pl.ds(3072, 1920)], send_sem.at[2]))

    for e, ref in enumerate((a0, a1, a2, a3)):
        turned_ref[:, e * 192 : (e + 1) * 192] = ref[...]
        for group in range(4):
            @pl.when(lax.rem(place[0] + e, 4) == group)
            def _():
                at = group % 2 * 192

                @pl.when(core == group // 2)
                def _():
                    at_ref[:, at : at + 192] = ref[...]

                @pl.when(core != group // 2)
                def _():
                    send_scr[:, 1536 + at : 1728 + at] = ref[...]

    dy = dy_ref[...]
    mid = x_ref[...].astype(F32) + jnp.dot(turned_ref[...], w_out_ref[...], preferred_element_type=F32) + b_out_ref[...]
    center = mid - jnp.mean(mid, axis=-1, keepdims=True)
    norm = lax.rsqrt(jnp.mean(center * center, axis=-1, keepdims=True) + 1e-05)
    xhat = center * norm
    h2 = (xhat * gain_ref[...] + shift_ref[...]).astype(BF)
    h2_ref[...] = h2
    send_scr[:, 0:768] = h2
    rows_ref[...] = jnp.zeros(rows_ref.shape, F32)
    rows_ref[3:4, :] = jnp.sum(dy.astype(F32), axis=0, keepdims=True)

    out = mid + b_down_ref[...]
    dh2 = jnp.zeros((256, 768), F32)
    scale = 0.7978845608028654
    for j in range(2):
        copies[2 * j].wait()
        copies[2 * j + 1].wait()
        for i in range(2):
            k = 2 * j + i
            at = slice(i * 768, (i + 1) * 768)
            u = jnp.dot(h2, up_ref[j, :, at], preferred_element_type=F32) + b_up_ref[:, k * 768 : (k + 1) * 768]
            grad_act = nt(dy, down_ref[j, at, :])
            square = u * u
            t = jnp.tanh(u * (scale + scale * 0.044715 * square))
            half = 0.5 + 0.5 * t
            g = u * half
            slope = half + g * (1.0 - t) * (scale + 3 * scale * 0.044715 * square)
            g = g.astype(BF)
            du = (grad_act * slope).astype(BF)
            rows_ref[6 + k : 7 + k, :] = jnp.sum(du.astype(F32), axis=0, keepdims=True)
            out = out + jnp.dot(g, down_ref[j, at, :], preferred_element_type=F32)
            dh2 = dh2 + nt(du, up_ref[j, :, at])

            hidden[j, 0, :, at] = g
            hidden[j, 1, :, at] = du

    for copy in own + sent[:2]:
        copy.start()
    result_ref[...] = out.astype(BF)
    rows_ref[4:5, :] = jnp.sum(dh2 * xhat, axis=0, keepdims=True)
    rows_ref[5:6, :] = jnp.sum(dh2, axis=0, keepdims=True)
    grad = dh2 * gain_ref[...]
    inner = grad - jnp.mean(grad, axis=-1, keepdims=True) - xhat * jnp.mean(grad * xhat, axis=-1, keepdims=True)
    mid_grad = dy.astype(F32) + norm * inner
    mid_grad_ref[...] = mid_grad
    da = mid_grad.astype(BF)
    da_ref[...] = da
    send_scr[:, 768:1536] = da
    sent[2].start()
    rows_ref[2:3, :] = jnp.sum(da.astype(F32), axis=0, keepdims=True)
    do = nt(da, w_out_ref[...]).astype(BF)
    for e, ref in enumerate((d0, d1, d2, d3)):
        ref[...] = do[:, e * 192 : (e + 1) * 192]
    for copy in own + sent:
        copy.wait()


def feed(place, heads, x, dy, w_out, w_up, w_down, b_out, gain, shift, b_up, b_down):
    tile = whole((256, 768))
    row = whole((1, 768))
    part = whole((256, 192))
    return pl.pallas_call(
        feed_kernel,
        grid_spec=pltpu.PrefetchScalarGridSpec(
            num_scalar_prefetch=1,
            grid=(1,),
            in_specs=[part] * 4
            + [
                tile,
                tile,
                whole((768, 768)),
                pl.BlockSpec(memory_space=pl.ANY),
                pl.BlockSpec(memory_space=pl.ANY),
                row,
                row,
                row,
                whole((1, 3072)),
                row,
            ],
            out_specs=[tile, tile]
            + [part] * 4
            + [pl.BlockSpec(memory_space=pl.ANY)] * 2
            + [tile, tile, whole((256, 384)), pl.BlockSpec(memory_space=pl.ANY), whole((64, 768))],
            scratch_shapes=[
                pltpu.VMEM((256, 768), BF),
                pltpu.VMEM((2, 768, 1536), BF),
                pltpu.VMEM((2, 1536, 768), BF),
                pltpu.VMEM((2, 2, 256, 1536), BF),
                pltpu.VMEM((256, 1920), BF),
                pltpu.SemaphoreType.DMA((2,)),
                pltpu.SemaphoreType.DMA((2,)),
                pltpu.SemaphoreType.DMA((2,)),
                pltpu.SemaphoreType.DMA((3,)),
            ],
        ),
        out_shape=[
            jax.ShapeDtypeStruct((256, 768), BF),
            jax.ShapeDtypeStruct((256, 768), F32),
        ]
        + [jax.ShapeDtypeStruct((256, 192), BF)] * 4
        + [jax.ShapeDtypeStruct((256, width), BF) for width in (1536, 1536, 768, 768, 384, 4992)]
        + [jax.ShapeDtypeStruct((64, 768), F32)],
        compiler_params=pltpu.CompilerParams(vmem_limit_bytes=60 * MIB),
        cost_estimate=COST,
        name="feed",
    )(
        place,
        *heads,
        x,
        dy,
        w_out,
        w_up,
        w_down,
        b_out.reshape(1, 768),
        gain.reshape(1, 768),
        shift.reshape(1, 768),
        b_up.reshape(1, 3072),
        b_down.reshape(1, 768),
    )


def both(own, other):
    return jnp.concatenate([own, other], axis=0)


def weights_kernel(info, g, dy, du, h2, at, da, received, dy2, b0, b1, b2, b3, out_scr, slot_scr, sem):
    dy_both = both(dy[...], dy2[...])
    out_scr[...] = tn(both(at[...], received[:, 4608:4992]), both(da[...], received[:, 3840:4608]))
    zero = jnp.zeros((8, 768), F32)
    copies = []
    for i, ref in enumerate((b0, b1, b2, b3)):
        a1 = lax.rem(info[1] + i, 4)
        cut = pl.ds(pl.multiple_of(a1 * 384, 384), 384)
        down = tn(both(g[:, cut], received[:, cut]), dy_both).astype(BF)
        first = pl.multiple_of(lax.rem(a1, 2) * 384, 384)
        left = both(h2[:, pl.ds(first, 384)], received[:, pl.ds(pl.multiple_of(3072 + first, 384), 384)])
        second = pl.multiple_of(a1 // 2 * 768, 768)
        right = both(du[:, pl.ds(second, 768)], received[:, pl.ds(pl.multiple_of(1536 + second, 768), 768)])
        up = tn(left, right).astype(BF)
        for a2 in range(4):
            slot_scr[i, a2, 0:96, :] = down[a2 * 96 : (a2 + 1) * 96]
            slot_scr[i, a2, 96:192, :] = up[a2 * 96 : (a2 + 1) * 96]
            rest = out_scr[pl.ds(pl.multiple_of(a1 * 96 + a2 * 24, 8), 24), :]
            slot_scr[i, a2, 192:224, :] = jnp.concatenate([rest, zero], axis=0).astype(BF)
        copies.append(pltpu.make_async_copy(slot_scr.at[i], ref, sem.at[i]))
        copies[-1].start()
    for copy in copies:
        copy.wait()


def weights(info, g, dy, du, h2, at, da, received, dy_received):
    operands = (g, dy, du, h2, at, da, received, dy_received)
    return pl.pallas_call(
        weights_kernel,
        grid_spec=pltpu.PrefetchScalarGridSpec(
            num_scalar_prefetch=1,
            grid=(1,),
            in_specs=[whole(array.shape) for array in operands],
            out_specs=[pl.BlockSpec(memory_space=pl.ANY)] * 4,
            scratch_shapes=[
                pltpu.VMEM((384, 768), F32),
                pltpu.VMEM((4, 4, 224, 768), BF),
                pltpu.SemaphoreType.DMA((4,)),
            ],
        ),
        out_shape=[jax.ShapeDtypeStruct((4, 224, 768), BF)] * 4,
        compiler_params=pltpu.CompilerParams(vmem_limit_bytes=60 * MIB),
        cost_estimate=COST,
        name="weights",
    )(info, *operands)


def add_kernel(info, p0, p1, p2, p3, *outs):
    total = p0[0].astype(F32) + p1[0].astype(F32) + p2[0].astype(F32) + p3[0].astype(F32)
    for i, out in enumerate(outs):
        @pl.when(pl.program_id(0) == i)
        def _():
            out[...] = total.astype(BF)


def add_pieces(info, pieces):
    spec = pl.BlockSpec((1, 224, 768), lambda i, info: (lax.rem(info[2] + i, 4), 0, 0))
    return pl.pallas_call(
        add_kernel,
        grid_spec=pltpu.PrefetchScalarGridSpec(
            num_scalar_prefetch=1, grid=(4,), in_specs=[spec] * 4, out_specs=[whole((224, 768))] * 4
        ),
        out_shape=[jax.ShapeDtypeStruct((224, 768), BF)] * 4,
        compiler_params=pltpu.CompilerParams(vmem_limit_bytes=24 * MIB),
        cost_estimate=COST,
        name="add_pieces",
    )(info, *pieces)


def place_kernel(counts, info, *refs):
    down, up, out = refs[-3:]
    for i, count in enumerate(counts):
        @pl.when(pl.program_id(0) == i)
        def _():
            base = sum(counts[:i])
            for r2 in range(4):
                a2 = lax.rem(info[2] + r2, 4)
                rows = refs[base + r2 * count // 4][r2 % (4 // count)].astype(F32)
                at = pl.multiple_of(a2 * 96, 96)
                down[pl.ds(at, 96), :] = rows[0:96]
                up[pl.ds(at, 96), :] = rows[96:192]
                out[pl.ds(pl.multiple_of(a2 * 24, 8), 24), :] = rows[192:216]


def place_weights(info, slots, pieces, others=()):
    arrays = [array for piece in pieces for array in piece]

    def first(i, info):
        slot_at = slots[0]
        for j, other in enumerate(slots):
            slot_at = jnp.where(i == j, other, slot_at)
        return lax.rem(info[1] + slot_at, 4)

    def by_rows(i, info):
        return (info[0] * 4 + first(i, info), 0)

    def by_columns(i, info):
        return (lax.rem(first(i, info), 2), info[0] * 2 + first(i, info) // 2)

    return pl.pallas_call(
        functools.partial(place_kernel, [len(piece) for piece in pieces]),
        grid_spec=pltpu.PrefetchScalarGridSpec(
            num_scalar_prefetch=1,
            grid=(len(pieces),),
            in_specs=[whole(array.shape) for array in arrays] + [pl.BlockSpec(memory_space=pl.ANY)] * len(others),
            out_specs=[pl.BlockSpec((384, 768), by_rows), pl.BlockSpec((384, 768), by_columns), pl.BlockSpec((96, 768), by_rows)],
        ),
        out_shape=[
            jax.ShapeDtypeStruct((3072, 768), F32),
            jax.ShapeDtypeStruct((768, 3072), F32),
            jax.ShapeDtypeStruct((768, 768), F32),
        ],
        input_output_aliases={1 + len(arrays) + i: i for i in range(len(others))},
        compiler_params=pltpu.CompilerParams(vmem_limit_bytes=32 * MIB),
        cost_estimate=COST,
        name="place_weights",
    )(info, *arrays, *others)


def moment_kernel(place, xhat_ref, dq_ref, near0_ref, near1_ref, far_ref, w_ref, gain_ref, shift_ref, rows_ref, p0, p1, p2, p3, give_ref, keep_ref, dqkv_ref):
    step = pl.program_id(0)

    @pl.when(step == 0)
    def _():
        for i, piece in enumerate((p0, p1, p2, p3)):
            dkv = near0_ref[i].astype(F32) + near1_ref[i].astype(F32) + far_ref[i].astype(F32)
            piece[:, :192] = dq_ref[i]
            piece[:, 192:] = dkv.astype(BF)
            dqkv_ref[i * 256 : (i + 1) * 256, :] = piece[...]

    dqkv = dqkv_ref[...]
    moment = tn(xhat_ref[...], dqkv)
    total = jnp.sum(dqkv.astype(F32), axis=0, keepdims=True)
    w = w_ref[0].astype(F32)
    gain = jnp.sum(w * moment, axis=1, keepdims=True)
    shift = jnp.sum(w * total, axis=1, keepdims=True)
    gw = (gain_ref[...] * moment + shift_ref[...] * total).astype(BF)
    lane = lax.broadcasted_iota(jnp.int32, (384, 64), 1)
    here = lax.rem(place[2] + 1 + step, 2)
    ends = jnp.concatenate([total[:, 384:], jnp.zeros((1, 192), F32)], axis=1)
    total_here = jnp.where(here == 0, total[:, :384], ends)
    row = lax.broadcasted_iota(jnp.int32, (64, 384), 0)
    vectors = jnp.where(row == 10, total_here, rows_ref[...]).T
    vectors = jnp.where(lane == 0, gain, jnp.where(lane == 1, shift, vectors)).astype(BF)

    def put(ref):
        ref[:, :576] = gw
        ref[:, 576:640] = vectors

    @pl.when(step == 0)
    def _():
        put(give_ref)

    @pl.when(step == 1)
    def _():
        put(keep_ref)


def moments(place, xhat, dq, near0, near1, far, w_groups, gain, shift, rows):
    def half(i, place):
        return lax.rem(place[2] + 1 + i, 2)

    return pl.pallas_call(
        moment_kernel,
        grid_spec=pltpu.PrefetchScalarGridSpec(
            num_scalar_prefetch=1,
            grid=(2,),
            in_specs=[
                pl.BlockSpec((1024, 384), lambda i, place: (0, half(i, place))),
                whole((4, 256, 192)),
                whole((4, 256, 384)),
                whole((4, 256, 384)),
                whole((4, 256, 384)),
                pl.BlockSpec((1, 384, 576), lambda i, place: (place[0], half(i, place), 0)),
                pl.BlockSpec((384, 1), lambda i, place: (half(i, place), 0)),
                pl.BlockSpec((384, 1), lambda i, place: (half(i, place), 0)),
                pl.BlockSpec((64, 384), lambda i, place: (0, half(i, place))),
            ],
            out_specs=[whole((256, 576))] * 4 + [whole((384, 640))] * 2,
            scratch_shapes=[pltpu.VMEM((1024, 576), BF)],
        ),
        out_shape=[jax.ShapeDtypeStruct((256, 576), BF)] * 4 + [jax.ShapeDtypeStruct((384, 640), BF)] * 2,
        compiler_params=pltpu.CompilerParams(vmem_limit_bytes=40 * MIB),
        cost_estimate=COST,
        name="moments",
    )(place, xhat.reshape(1024, 768), dq, near0, near1, far, w_groups, gain.reshape(768, 1), shift.reshape(768, 1), rows)


def regroup_kernel(w_ref, out_ref):
    for group in range(4):
        @pl.when(pl.program_id(0) == group)
        def _():
            at = group * 192
            out_ref[0, :, :192] = w_ref[:, at : at + 192]
            for h in range(3):
                for t in range(2):
                    to = 192 + h * 128 + t * HD
                    first = 768 * (t + 1) + at + h * HD
                    out_ref[0, :, to : to + HD] = w_ref[:, first : first + HD]


def regroup(w):
    return pl.pallas_call(
        regroup_kernel,
        grid=(4,),
        in_specs=[pl.BlockSpec((768, 2304), lambda i: (0, 0))],
        out_specs=pl.BlockSpec((1, 768, 576), lambda i: (i, 0, 0)),
        out_shape=jax.ShapeDtypeStruct((4, 768, 576), BF),
        compiler_params=pltpu.CompilerParams(vmem_limit_bytes=24 * MIB),
        cost_estimate=COST,
        name="regroup",
    )(w)


def finish_kernel(place, p0, p1, p2, p3, w_ref, x_ref, gain_ref, mid_ref, out_ref, acc_ref):
    e = pl.program_id(0)
    for i, piece in enumerate((p0, p1, p2, p3)):
        @pl.when(e == i)
        def _():
            part = nt(piece[...], w_ref[0])
            acc_ref[...] = part if i == 0 else acc_ref[...] + part

    @pl.when(e == 3)
    def _():
        x = x_ref[...].astype(F32)
        center = x - jnp.mean(x, axis=-1, keepdims=True)
        scale = lax.rsqrt(jnp.mean(center * center, axis=-1, keepdims=True) + 1e-05)
        xhat = center * scale
        grad = acc_ref[...] * gain_ref[...]
        inner = grad - jnp.mean(grad, axis=-1, keepdims=True) - xhat * jnp.mean(grad * xhat, axis=-1, keepdims=True)
        out_ref[...] = mid_ref[...] + scale * inner


def finish(place, pieces, w_groups, x, gain, middle):
    return pl.pallas_call(
        finish_kernel,
        grid_spec=pltpu.PrefetchScalarGridSpec(
            num_scalar_prefetch=1,
            grid=(4,),
            in_specs=[whole((256, 576))] * 4
            + [
                pl.BlockSpec((1, 768, 576), lambda i, place: (lax.rem(place[0] + i, 4), 0, 0)),
                whole((256, 768)),
                whole((1, 768)),
                whole((256, 768)),
            ],
            out_specs=whole((256, 768)),
            scratch_shapes=[pltpu.VMEM((256, 768), F32)],
        ),
        out_shape=jax.ShapeDtypeStruct((256, 768), F32),
        compiler_params=pltpu.CompilerParams(vmem_limit_bytes=24 * MIB),
        cost_estimate=COST,
        name="finish",
    )(place, *pieces, w_groups, x, gain.reshape(1, 768), middle)


def join_kernel(info, p0, p1, p2, p3, *refs):
    out_ref, rows_ref, cols_ref = refs[-3:]

    def put(rows, part, group):
        to = pl.ds(pl.multiple_of(part * 96, 96), 96)
        rows = rows.astype(F32)
        out_ref[to, group * 192 : (group + 1) * 192] = rows[:, :192]
        for h in range(3):
            for t in range(2):
                start = 192 + h * 128 + t * HD
                column = 768 * (t + 1) + group * 192 + h * HD
                out_ref[to, column : column + HD] = rows[:, start : start + HD]
        cols_ref[group, to, :] = rows[:, 512:640]

    for r1, piece in enumerate((p0, p1, p2, p3)):
        first = lax.rem(info[1] + r1, 4)

        @pl.when(info[0] == 0)
        def _():
            for group in range(4):
                put(piece[lax.rem(group + 4 - info[2], 4)], first, group)

        for group in range(4):
            @pl.when(jnp.logical_and(info[0] == 1, first == group))
            def _():
                for r2 in range(4):
                    put(piece[r2], lax.rem(info[2] + r2, 4), group)

    turned = [cols_ref[group].T for group in range(4)]
    rows_ref[:16, :] = (turned[0] + turned[1] + turned[2] + turned[3])[64:80]
    for group in range(4):
        rows_ref[16 + group : 17 + group, :] = turned[group][74:75]
    rows_ref[20:, :] = jnp.zeros((4, 384), F32)


def join_qkv(info, pieces, others=()):
    return pl.pallas_call(
        join_kernel,
        grid_spec=pltpu.PrefetchScalarGridSpec(
            num_scalar_prefetch=1,
            grid=(1,),
            in_specs=[whole((4, 96, 640))] * 4 + [pl.BlockSpec(memory_space=pl.ANY)] * len(others),
            out_specs=[
                pl.BlockSpec((384, 2304), lambda i, info: (info[0], 0)),
                pl.BlockSpec((24, 384), lambda i, info: (0, info[0])),
            ],
            scratch_shapes=[pltpu.VMEM((4, 384, 128), F32)],
        ),
        out_shape=[jax.ShapeDtypeStruct((768, 2304), F32), jax.ShapeDtypeStruct((24, 768), F32)],
        input_output_aliases={5 + i: i for i in range(len(others))},
        compiler_params=pltpu.CompilerParams(vmem_limit_bytes=40 * MIB),
        cost_estimate=COST,
        name="join_qkv",
    )(info, *pieces, *others)


def region(always, work, *operands):
    shapes = jax.eval_shape(work, *operands)
    empty = jax.tree.map(lambda shape: jnp.zeros(shape.shape, shape.dtype), shapes)
    return lax.cond(always, work, lambda *args: empty, *operands)


def layer_norm(values, gain, shift):
    center = values - jnp.mean(values, axis=-1, keepdims=True)
    spread = jnp.mean(center * center, axis=-1, keepdims=True)
    return center * lax.rsqrt(spread + 1e-05) * gain + shift


def shards(
    tokens,
    cotangent,
    ln1_gain,
    ln1_shift,
    w_qkv,
    b_query,
    b_value,
    w_out,
    b_out,
    ln2_gain,
    ln2_shift,
    w_up,
    b_up,
    w_down,
    b_down,
):
    seq, batch = lax.axis_index("seq"), lax.axis_index("batch")
    y, zh, c = seq // 4, lax.rem(seq // 2, 2), lax.rem(seq, 2)
    z, x = zh * 2 + batch // 4, lax.rem(batch, 4)
    always = seq + batch >= 0
    place = jnp.stack([y, zh, c, x]).astype(jnp.int32)
    info = jnp.stack([c, jnp.where(c == 0, x, y), jnp.where(c == 0, y, z)]).astype(jnp.int32)
    other_info = jnp.stack([1 - c, jnp.where(c == 0, y, x), jnp.where(c == 0, z, y)]).astype(jnp.int32)

    tokens = tokens[0]
    dy_low = cotangent[0]
    columns = [tokens] + fetch_all(tokens, "y") + [fetch(tokens, "z", 2)]
    dy_other = fetch(dy_low, "c", 1)

    def by_group(array):
        parts = array.reshape(1, 3, 4, 3, HD)
        query = parts[:, 0].transpose(1, 0, 2, 3).reshape(4, 1, 192)
        keys = parts[:, 1:].transpose(2, 0, 3, 1, 4).reshape(4, 1, 384)
        return jnp.concatenate([query, keys], axis=2)

    w_groups = regroup(w_qkv)
    bias_groups = by_group(jnp.concatenate([b_query, jnp.zeros_like(b_query), b_value]))
    w_out_turned = lax.dynamic_slice_in_dim(jnp.concatenate([w_out, w_out]), y * 192, 768, 0)

    xhat, q, kv, far_first = prep(place, columns, w_groups, bias_groups, ln1_gain, ln1_shift)
    far_rest = fetch(kv[1:], "z", 2)
    near = (kv, fetch(kv, "c", 1))
    far_near = (far_first, fetch(far_first, "c", 1))
    far = []

    def far_of(state):
        rest, *state = lax.optimization_barrier((far_rest, *state))
        far.extend([*far_near, rest, fetch(rest, "c", 1)])
        return state, far[2:]

    o, o32, lse = attend(place, q, (*near, *far_near), far_of)

    heads = [o[0]] + [fetch(o[4 - e], "y", e) for e in (1, 2, 3)]
    fed = feed(place, heads, tokens, dy_low, w_out_turned, w_up, w_down, b_out, ln2_gain, ln2_shift, b_up, b_down)
    result, grad_middle, *do, g, du, h2, da, attended, send, vectors = fed

    do_mine = [do[0]] + [fetch(do[4 - e], "y", e) for e in (1, 2, 3)]
    received = fetch(send, "c", 1)
    pieces = weights(info, g, dy_low, du, h2, attended, da, received, dy_other)

    def back_far(*do_mine):
        delta, dqt, far0, far1 = attend_back_far(place, q, do_mine, o32, lse, far)
        return delta, dqt, (far0.astype(F32) + fetch(far1, "c", 1).astype(F32)).astype(BF)

    def back_near(delta, dqt, *do_mine):
        dq, near0, near1 = attend_back_near(place, q, do_mine, lse, near, delta, dqt)
        return dq, near0, fetch(near1, "c", 1)

    def scatter_beside(pieces, *do_mine):
        received = [fetch(pieces[d], FIRST, 4 - d) for d in (1, 2, 3)]
        delta, dqt, far_sum = region(always, back_far, *do_mine)
        far_received = fetch(far_sum, "z", 2)
        dq, near0, near1 = region(always, back_near, delta, dqt, *do_mine)
        dq, *received = lax.optimization_barrier((dq, *received))
        pieces = add_pieces(info, [pieces[0]] + received)
        moved = [fetch(pieces[d], SECOND, 4 - d) for d in (1, 2, 3)]
        moved = moments(place, xhat, dq, near0, near1, far_received, w_groups, ln1_gain, ln1_shift, vectors), pieces[0], moved
        return moved

    (dqkv0, dqkv1, dqkv2, dqkv3, given, gw), own, received = region(always, scatter_beside, pieces, *do_mine)
    pieces = [own] + received

    def sum_rest(pieces, given, gw):
        chunk = sum(p.astype(F32) for p in pieces).astype(BF)
        gw = (gw.astype(F32) + fetch(given, "c", 1).astype(F32)).astype(BF)
        return sum_pairs(chunk, REST), halve(gw, KEYS, jnp.where(c == 0, x, z))

    def rows_beside(dqkv1, dqkv2, dqkv3, *operands):
        rows = fetch(dqkv3, "y", 1), fetch(dqkv2, "y", 2), fetch(dqkv1, "y", 3)
        return *rows, *region(always, sum_rest, *operands)

    *parts, chunk, gw = region(always, rows_beside, dqkv1, dqkv2, dqkv3, pieces, given, gw)

    def sum_keys(gw):
        return (sum_pairs(gw, REST),)

    def gather_second(chunk, gw):
        return jnp.stack([chunk] + fetch_all(chunk, SECOND)), *region(always, sum_keys, gw)

    chunk, gw = region(always, gather_second, chunk, gw)

    def finish_keys_rows(gw, *parts):
        gw = jnp.stack([gw] + fetch_all(gw, SECOND))
        return gw, finish(place, parts, w_groups, tokens, ln1_gain, grad_middle)

    def place_first(chunk):
        other = fetch(chunk, "c", 1)
        placed = place_weights(info, (0,), [(chunk,)])
        return place_weights(other_info, (0,), [(other,)], placed)

    def place_after(chunk, *operands):
        gw, grad_inputs = region(always, finish_keys_rows, *operands)
        gw, chunk = lax.optimization_barrier((gw, chunk))
        return gw, grad_inputs, *region(always, place_first, chunk)

    def gather_sides(chunk, *operands):
        return *fetch_sides(chunk, FIRST), *region(always, place_after, chunk, *operands)

    side1, side3, gw, grad_inputs, *placed = region(always, gather_sides, chunk, gw, dqkv0, *parts)

    def place_near(placed, *near):
        return place_weights(info, (1, 3), [(piece,) for piece in near], placed)

    def gather_far(placed, *near):
        others = [fetch(piece, "c", 1) for piece in near]
        return *fetch_halves(*near, FIRST), *others, *region(always, place_near, placed, *near)

    low, high, other1, other3, *placed = region(always, gather_far, placed, side1, side3)

    def place_more(low, high, placed, *others):
        far = fetch(low, "c", 1), fetch(high, "c", 1)
        placed = place_weights(other_info, (1, 3), [(piece,) for piece in others], placed)
        placed = place_weights(info, (2,), [(low, high)], placed)
        return place_weights(other_info, (2,), [far], placed)

    def gather_keys(gw, *operands):
        return *fetch_all(gw, FIRST), *region(always, place_more, *operands)

    key1, key2, key3, gw_down, gw_up, gw_out = region(always, gather_keys, gw, low, high, placed, other1, other3)
    keys = (gw, key1, key2, key3)
    other_keys = [fetch(piece, "c", 1) for piece in keys]
    joined = join_qkv(info, keys)
    gw_qkv, sums = join_qkv(other_info, other_keys, joined)
    return (
        result[None],
        grad_inputs[None],
        sums[0],
        sums[1],
        gw_qkv,
        sums[16:20, :192].reshape(768),
        sums[16:20, 192:576].reshape(4, 3, 2, HD)[:, :, 1].reshape(768),
        gw_out,
        sums[2],
        sums[4],
        sums[5],
        gw_up,
        sums[6:10].reshape(3072),
        gw_down,
        sums[3],
    )


def solution(mesh):
    split = P("batch", "seq", None)
    return jax.shard_map(
        shards,
        mesh=mesh,
        in_specs=(split, split) + (P(),) * 13,
        out_specs=(split, split) + (P(),) * 13,
        check_vma=False,
    )
```

```python
import functools

import jax
import jax.numpy as jnp
from jax import lax
from jax.experimental import pallas as pl
from jax.experimental.pallas import tpu as pltpu
from jax.sharding import PartitionSpec as P

HD = 64
LOG2E = 1.4426950408889634
BF = jnp.bfloat16
F32 = jnp.float32
MIB = 2**20
COST = pl.CostEstimate(flops=1000, bytes_accessed=1000, transcendentals=0)


def nt(left, right):
    return lax.dot_general(left, right, (((1,), (1,)), ((), ())), preferred_element_type=F32)


def tn(left, right):
    return lax.dot_general(left, right, (((0,), (0,)), ((), ())), preferred_element_type=F32)


def whole(shape):
    return pl.BlockSpec(shape, lambda i, *_: (0,) * len(shape))


def of_slot(shape):
    return pl.BlockSpec((1,) + shape, lambda i, *_: (i,) + (0,) * len(shape))


def causal(scores, other):
    keys = lax.broadcasted_iota(jnp.int32, scores.shape, 0)
    queries = lax.broadcasted_iota(jnp.int32, scores.shape, 1)
    return jnp.where(keys <= queries, scores, other)


def query_y(place):
    return lax.rem(place[0] + pl.program_id(0), 4)


def slot(place, y):
    return lax.rem(y + 4 - place[0], 4)


def softmax_step(q_ref, m_ref, l_ref, acc_ref, blocks, masks):
    scores = []
    for h in range(3):
        q = q_ref[0, :, h * HD : (h + 1) * HD]
        row = [nt(block[:, h * 128 : h * 128 + HD], q) * LOG2E for block in blocks]
        scores.append([mask(s, -1e30) if mask else s for s, mask in zip(row, masks)])
    probs = []
    for h in range(3):
        old = m_ref[0, h : h + 1, :]
        new = old
        for s in scores[h]:
            new = jnp.maximum(new, jnp.max(s, axis=0, keepdims=True))
        factor = jnp.exp2(old - new)
        m_ref[0, h : h + 1, :] = new
        row = [jnp.exp2(s - new) for s in scores[h]]
        l_ref[0, h : h + 1, :] = l_ref[0, h : h + 1, :] * factor + sum(jnp.sum(p, axis=0, keepdims=True) for p in row)
        probs.append((row, factor))
    for h in range(3):
        row, factor = probs[h]
        acc = acc_ref[0, h] * factor
        for block, p in zip(blocks, row):
            acc = acc + tn(block[:, h * 128 + HD : (h + 1) * 128], p.astype(BF))
        acc_ref[0, h] = acc


def attend_near_kernel(place, q_ref, kv0_ref, kv1_ref, first0_ref, first1_ref, m_ref, l_ref, acc_ref):
    own = pl.program_id(0)
    m_ref[...] = jnp.full(m_ref.shape, -1e30, F32)
    l_ref[...] = jnp.zeros(l_ref.shape, F32)
    acc_ref[...] = jnp.zeros(acc_ref.shape, F32)

    def beside(scores, other):
        return jnp.where(place[2] == 1, scores, other)

    softmax_step(q_ref, m_ref, l_ref, acc_ref, [kv0_ref[own], kv1_ref[own]], [causal, beside])

    @pl.when(place[0] < query_y(place) + place[1])
    def _():
        softmax_step(q_ref, m_ref, l_ref, acc_ref, [first0_ref[...], first1_ref[...]], [None, None])

    def body(y, carry):
        at = slot(place, y)
        softmax_step(q_ref, m_ref, l_ref, acc_ref, [kv0_ref[at], kv1_ref[at]], [None, None])
        return carry

    lax.fori_loop(0, query_y(place), body, 0)


def attend_far_kernel(place, q_ref, kv0_ref, kv1_ref, m_in, l_in, acc_in, o_ref, o32_ref, lse_ref, m_ref, l_ref, acc_ref):
    m_ref[...] = m_in[...]
    l_ref[...] = l_in[...]
    acc_ref[...] = acc_in[...]

    def body(y, carry):
        @pl.when(y != place[0])
        def _():
            at = slot(place, y) - 1
            softmax_step(q_ref, m_ref, l_ref, acc_ref, [kv0_ref[at], kv1_ref[at]], [None, None])

        return carry

    lax.fori_loop(0, query_y(place) + place[1], body, 0)
    for h in range(3):
        o = (acc_ref[0, h] / l_ref[0, h : h + 1, :]).T
        o32_ref[0, :, h * HD : (h + 1) * HD] = o
        o_ref[0, :, h * HD : (h + 1) * HD] = o.astype(BF)
    lse_ref[...] = m_ref[...] + jnp.log2(l_ref[...])


def attend(place, q, near, far_of):
    stats = [of_slot((3, 256)), of_slot((3, 256)), of_slot((3, HD, 256))]
    stat_shapes = [
        jax.ShapeDtypeStruct((4, 3, 256), F32),
        jax.ShapeDtypeStruct((4, 3, 256), F32),
        jax.ShapeDtypeStruct((4, 3, HD, 256), F32),
    ]
    keys = [whole((4, 256, 384)), whole((4, 256, 384)), whole((256, 384)), whole((256, 384))]
    far_keys = [whole((3, 256, 384)), whole((3, 256, 384))]
    state = pl.pallas_call(
        attend_near_kernel,
        grid_spec=pltpu.PrefetchScalarGridSpec(
            num_scalar_prefetch=1, grid=(4,), in_specs=[of_slot((256, 192))] + keys, out_specs=stats
        ),
        out_shape=stat_shapes,
        compiler_params=pltpu.CompilerParams(vmem_limit_bytes=32 * MIB),
        cost_estimate=COST,
        name="attend_near",
    )(place, q, *near)
    state, far = far_of(state)
    return pl.pallas_call(
        attend_far_kernel,
        grid_spec=pltpu.PrefetchScalarGridSpec(
            num_scalar_prefetch=1,
            grid=(4,),
            in_specs=[of_slot((256, 192))] + far_keys + stats,
            out_specs=[of_slot((256, 192)), of_slot((256, 192)), of_slot((3, 256))],
            scratch_shapes=[pltpu.VMEM((1, 3, 256), F32), pltpu.VMEM((1, 3, 256), F32), pltpu.VMEM((1, 3, HD, 256), F32)],
        ),
        out_shape=[
            jax.ShapeDtypeStruct((4, 256, 192), BF),
            jax.ShapeDtypeStruct((4, 256, 192), F32),
            jax.ShapeDtypeStruct((4, 3, 256), F32),
        ],
        compiler_params=pltpu.CompilerParams(vmem_limit_bytes=32 * MIB),
        cost_estimate=COST,
        name="attend_far",
    )(place, q, *far, *state)


def grad_step(lse_ref, qdo_ref, delta_ref, dqt_ref, sums, blocks, at, masks):
    both = {}
    for h in range(3):
        for i, block in enumerate(blocks):
            both[h, i] = nt(block[:, h * 128 : (h + 1) * 128], qdo_ref[h])
    weights = {}
    for h in range(3):
        for i, mask in enumerate(masks):
            p = jnp.exp2(both[h, i][:, :256] * LOG2E - lse_ref[0, h : h + 1, :])
            if mask:
                p = mask(p, 0.0)
            ds = (p * (both[h, i][:, 256:] - delta_ref[h])).astype(BF)
            weights[h, i] = (ds, p.astype(BF))
    for h in range(3):
        dqt = dqt_ref[h]
        for i, block in enumerate(blocks):
            ds, p = weights[h, i]
            sums[i][at, :, h * 128 : (h + 1) * 128] += jnp.dot(
                jnp.concatenate([ds, p], axis=1), qdo_ref[h], preferred_element_type=F32
            )
            dqt = dqt + tn(block[:, h * 128 : h * 128 + HD], ds)
        dqt_ref[h] = dqt


def grad_start(q_ref, do_refs, delta_of, qdo_ref, delta_ref, sums):
    @pl.when(pl.program_id(0) == 0)
    def _():
        for total in sums:
            total[...] = jnp.zeros(total.shape, F32)

    zero = jnp.zeros((256, HD), BF)
    for i, do_ref in enumerate(do_refs):
        @pl.when(pl.program_id(0) == i)
        def _():
            for h in range(3):
                do = do_ref[:, h * HD : (h + 1) * HD]
                qdo_ref[h, :256, :] = jnp.concatenate([q_ref[0, :, h * HD : (h + 1) * HD], zero], axis=1)
                qdo_ref[h, 256:, :] = jnp.concatenate([zero, do], axis=1)
                delta_ref[h] = delta_of(h, do)


def grad_end(sums, outs):
    @pl.when(pl.program_id(0) == 3)
    def _():
        for total, out in zip(sums, outs):
            out[...] = total[...].astype(BF)


def grad_far_kernel(place, q_ref, do0, do1, do2, do3, o32_ref, lse_ref, first0_ref, first1_ref, kv0_ref, kv1_ref, delta_out, dqt_out, g0_ref, g1_ref, qdo_ref, delta_ref, dqt_ref, sum0_ref, sum1_ref):
    sums = [sum0_ref, sum1_ref]

    def delta_of(h, do):
        prod = do.astype(F32) * o32_ref[0, :, h * HD : (h + 1) * HD]
        return jnp.sum(prod.T, axis=0, keepdims=True)

    grad_start(q_ref, (do0, do1, do2, do3), delta_of, qdo_ref, delta_ref, sums)
    dqt_ref[...] = jnp.zeros(dqt_ref.shape, F32)

    @pl.when(place[0] < query_y(place) + place[1])
    def _():
        grad_step(lse_ref, qdo_ref, delta_ref, dqt_ref, sums, [first0_ref[...], first1_ref[...]], 0, [None, None])

    def body(y, carry):
        @pl.when(y != place[0])
        def _():
            at = slot(place, y)
            grad_step(lse_ref, qdo_ref, delta_ref, dqt_ref, sums, [kv0_ref[at - 1], kv1_ref[at - 1]], at, [None, None])

        return carry

    lax.fori_loop(0, query_y(place) + place[1], body, 0)
    for h in range(3):
        delta_out[0, h : h + 1, :] = delta_ref[h]
        dqt_out[0, h] = dqt_ref[h]
    grad_end(sums, [g0_ref, g1_ref])


def grad_near_kernel(place, q_ref, do0, do1, do2, do3, lse_ref, kv0_ref, kv1_ref, delta_in, dqt_in, dq_ref, g0_ref, g1_ref, qdo_ref, delta_ref, dqt_ref, sum0_ref, sum1_ref):
    own = pl.program_id(0)
    sums = [sum0_ref, sum1_ref]
    grad_start(q_ref, (do0, do1, do2, do3), lambda h, do: delta_in[0, h : h + 1, :], qdo_ref, delta_ref, sums)
    dqt_ref[...] = dqt_in[0]

    def beside(probs, other):
        return jnp.where(place[2] == 1, probs, other)

    grad_step(lse_ref, qdo_ref, delta_ref, dqt_ref, sums, [kv0_ref[own], kv1_ref[own]], own, [causal, beside])

    def body(y, carry):
        at = slot(place, y)
        grad_step(lse_ref, qdo_ref, delta_ref, dqt_ref, sums, [kv0_ref[at], kv1_ref[at]], at, [None, None])
        return carry

    lax.fori_loop(0, query_y(place), body, 0)
    for h in range(3):
        dq_ref[0, :, h * HD : (h + 1) * HD] = (dqt_ref[h].T * 0.125).astype(BF)
    grad_end(sums, [g0_ref, g1_ref])


GRAD_SCRATCH = [
    pltpu.VMEM((3, 512, 128), BF),
    pltpu.VMEM((3, 1, 256), F32),
    pltpu.VMEM((3, HD, 256), F32),
    pltpu.VMEM((4, 256, 384), F32),
    pltpu.VMEM((4, 256, 384), F32),
]


def attend_back_far(place, q, do, o32, lse, far):
    keys = [whole((4, 256, 384)), whole((4, 256, 384))]
    return pl.pallas_call(
        grad_far_kernel,
        grid_spec=pltpu.PrefetchScalarGridSpec(
            num_scalar_prefetch=1,
            grid=(4,),
            in_specs=[of_slot((256, 192))] + [whole((256, 192))] * 4 + [of_slot((256, 192)), of_slot((3, 256))] + [whole((256, 384))] * 2 + [whole((3, 256, 384))] * 2,
            out_specs=[of_slot((3, 256)), of_slot((3, HD, 256))] + keys,
            scratch_shapes=GRAD_SCRATCH,
        ),
        out_shape=[
            jax.ShapeDtypeStruct((4, 3, 256), F32),
            jax.ShapeDtypeStruct((4, 3, HD, 256), F32),
            jax.ShapeDtypeStruct((4, 256, 384), BF),
            jax.ShapeDtypeStruct((4, 256, 384), BF),
        ],
        compiler_params=pltpu.CompilerParams(vmem_limit_bytes=40 * MIB),
        cost_estimate=COST,
        name="attend_back_far",
    )(place, q, *do, o32, lse, *far)


def attend_back_near(place, q, do, lse, near, delta, dqt):
    keys = [whole((4, 256, 384)), whole((4, 256, 384))]
    return pl.pallas_call(
        grad_near_kernel,
        grid_spec=pltpu.PrefetchScalarGridSpec(
            num_scalar_prefetch=1,
            grid=(4,),
            in_specs=[of_slot((256, 192))] + [whole((256, 192))] * 4 + [of_slot((3, 256))] + keys + [of_slot((3, 256)), of_slot((3, HD, 256))],
            out_specs=[of_slot((256, 192))] + keys,
            scratch_shapes=GRAD_SCRATCH,
        ),
        out_shape=[
            jax.ShapeDtypeStruct((4, 256, 192), BF),
            jax.ShapeDtypeStruct((4, 256, 384), BF),
            jax.ShapeDtypeStruct((4, 256, 384), BF),
        ],
        compiler_params=pltpu.CompilerParams(vmem_limit_bytes=40 * MIB),
        cost_estimate=COST,
        name="attend_back_near",
    )(place, q, *do, lse, *near, delta, dqt)


def project(x_ref, w_ref, bias_ref, gain_ref, shift_ref):
    x = x_ref[...].astype(F32)
    center = x - jnp.mean(x, axis=-1, keepdims=True)
    spread = jnp.mean(center * center, axis=-1, keepdims=True)
    xhat = center * lax.rsqrt(spread + 1e-05)
    h1 = (xhat * gain_ref[...] + shift_ref[...]).astype(BF)
    qkv = jnp.dot(h1, w_ref[0], preferred_element_type=F32) + bias_ref[0]
    return xhat.astype(BF), qkv[:, :192].astype(BF) * jnp.asarray(0.125, BF), qkv[:, 192:].astype(BF)


def prep_own_kernel(place, x_ref, far_ref, w_ref, bias_ref, gain_ref, shift_ref, xhat_ref, q_ref, kv_ref, far_kv_ref):
    xhat_ref[0], q_ref[0], kv_ref[0] = project(x_ref, w_ref, bias_ref, gain_ref, shift_ref)
    far_kv_ref[...] = project(far_ref, w_ref, bias_ref, gain_ref, shift_ref)[2]


def prep_rest_kernel(place, x1_ref, x2_ref, x3_ref, w_ref, bias_ref, gain_ref, shift_ref, *refs):
    xhat_ref, q_ref, kv_ref = refs[-3:]
    for i, x_ref in enumerate((x1_ref, x2_ref, x3_ref)):
        @pl.when(pl.program_id(0) == i)
        def _():
            xhat_ref[0], q_ref[0], kv_ref[0] = project(x_ref, w_ref, bias_ref, gain_ref, shift_ref)


def prep_call(kernel, name, place, blocks, weights, slot_of, steps, extra, others=()):
    shapes = [(256, 768), (256, 192), (256, 384)]
    return pl.pallas_call(
        kernel,
        grid_spec=pltpu.PrefetchScalarGridSpec(
            num_scalar_prefetch=1,
            grid=(steps,),
            in_specs=[whole((256, 768))] * len(blocks)
            + [
                pl.BlockSpec((1, 768, 576), lambda i, place: (place[0], 0, 0)),
                pl.BlockSpec((1, 1, 576), lambda i, place: (place[0], 0, 0)),
                whole((1, 768)),
                whole((1, 768)),
            ]
            + [pl.BlockSpec(memory_space=pl.ANY)] * len(others),
            out_specs=[pl.BlockSpec((1,) + shape, lambda i, place: (slot_of(i), 0, 0)) for shape in shapes] + [whole((256, 384))] * extra,
        ),
        out_shape=[jax.ShapeDtypeStruct((4,) + shape, BF) for shape in shapes] + [jax.ShapeDtypeStruct((256, 384), BF)] * extra,
        input_output_aliases={5 + len(blocks) + i: i for i in range(len(others))},
        compiler_params=pltpu.CompilerParams(vmem_limit_bytes=24 * MIB),
        cost_estimate=COST,
        name=name,
    )(place, *blocks, *weights, *others)


FIRST = ("x", "y")
SECOND = ("y", "z")
REST = ("z", "x")
KEYS = ("x", "z")


def shift_pairs(axes, step, pairwise=False):
    pairs = []
    for s in range(16):
        for b in range(8):
            at = {"y": s // 4, "z": (s // 2 % 2) * 2 + b // 4, "c": s % 2, "x": b % 4}
            axis = axes[at["c"]]
            at[axis] = at[axis] ^ step if pairwise else (at[axis] + step) % (2 if axis == "c" else 4)
            source = (at["y"] * 4 + (at["z"] // 2) * 2 + at["c"]) * 8 + (at["z"] % 2) * 4 + at["x"]
            pairs.append((source, s * 8 + b))
    return pairs


def fetch(array, axes, step):
    if isinstance(axes, str):
        axes = (axes, axes)
    return lax.ppermute(array, ("seq", "batch"), shift_pairs(axes, step))


def fetch_all(array, axes):
    return [fetch(array, axes, step) for step in (1, 2, 3)]


def roll_slots(pieces, index):
    count = len(pieces)
    stacked = jnp.stack(pieces + pieces[:-1])
    return lax.dynamic_slice_in_dim(stacked, lax.rem(count - index, count), count, 0)


def sum_pairs(array, axes):
    for step in (2, 1):
        array = (array.astype(F32) + fetch_pair(array, axes, step).astype(F32)).astype(array.dtype)
    return array


def halve(array, axes, index):
    for step in (2, 1):
        parts = array.reshape(2, -1, *array.shape[1:])
        side = lax.rem(index // step, 2)
        kept = lax.dynamic_index_in_dim(parts, side, 0, keepdims=False)
        other = fetch_pair(lax.dynamic_index_in_dim(parts, 1 - side, 0, keepdims=False), axes, step)
        array = (kept.astype(F32) + other.astype(F32)).astype(array.dtype)
    return array


def fetch_sides(array, axes):
    return fetch(array, axes, 1), fetch(array, axes, 3)


def fetch_halves(side1, side3, axes):
    half = side1.shape[0] // 2
    return fetch(side1[:half], axes, 1), fetch(side3[half:], axes, 3)


def fetch_pair(array, axes, step):
    if isinstance(axes, str):
        axes = (axes, axes)
    return lax.ppermute(array, ("seq", "batch"), shift_pairs(axes, step, True))


def all_gather(array, axes, index):
    return roll_slots([array] + fetch_all(array, axes), index)


def feed_kernel(place, a0, a1, a2, a3, x_ref, dy_ref, w_out_ref, w_up_hbm, w_down_hbm, b_out_ref, gain_ref, shift_ref, b_up_ref, b_down_ref, result_ref, mid_grad_ref, d0, d1, d2, d3, g_ref, du_ref, h2_ref, da_ref, at_ref, send_ref, rows_ref, turned_ref, up_ref, down_ref, hidden, send_scr, up_sem, down_sem, own_sem, send_sem):
    core = place[2]
    copies = []
    for j in range(2):
        part = pl.ds(j * 1536, 1536)
        copies.append(pltpu.make_async_copy(w_up_hbm.at[:, part], up_ref.at[j], up_sem.at[j]))
        copies.append(pltpu.make_async_copy(w_down_hbm.at[part, :], down_ref.at[j], down_sem.at[j]))
    for copy in copies:
        copy.start()
    own, sent = [], []
    for k, ref in enumerate((g_ref, du_ref)):
        own.append(pltpu.make_async_copy(hidden.at[core, k], ref, own_sem.at[k]))
        sent.append(pltpu.make_async_copy(hidden.at[1 - core, k], send_ref.at[:, pl.ds(k * 1536, 1536)], send_sem.at[k]))
    sent.append(pltpu.make_async_copy(send_scr, send_ref.at[:, pl.ds(3072, 1920)], send_sem.at[2]))

    for e, ref in enumerate((a0, a1, a2, a3)):
        turned_ref[:, e * 192 : (e + 1) * 192] = ref[...]
        for group in range(4):
            @pl.when(lax.rem(place[0] + e, 4) == group)
            def _():
                at = group % 2 * 192

                @pl.when(core == group // 2)
                def _():
                    at_ref[:, at : at + 192] = ref[...]

                @pl.when(core != group // 2)
                def _():
                    send_scr[:, 1536 + at : 1728 + at] = ref[...]

    dy = dy_ref[...]
    mid = x_ref[...].astype(F32) + jnp.dot(turned_ref[...], w_out_ref[...], preferred_element_type=F32) + b_out_ref[...]
    center = mid - jnp.mean(mid, axis=-1, keepdims=True)
    norm = lax.rsqrt(jnp.mean(center * center, axis=-1, keepdims=True) + 1e-05)
    xhat = center * norm
    h2 = (xhat * gain_ref[...] + shift_ref[...]).astype(BF)
    h2_ref[...] = h2
    send_scr[:, 0:768] = h2
    rows_ref[...] = jnp.zeros(rows_ref.shape, F32)
    rows_ref[3:4, :] = jnp.sum(dy.astype(F32), axis=0, keepdims=True)

    out = mid + b_down_ref[...]
    dh2 = jnp.zeros((256, 768), F32)
    scale = 0.7978845608028654
    for j in range(2):
        copies[2 * j].wait()
        copies[2 * j + 1].wait()
        for i in range(2):
            k = 2 * j + i
            at = slice(i * 768, (i + 1) * 768)
            u = jnp.dot(h2, up_ref[j, :, at], preferred_element_type=F32) + b_up_ref[:, k * 768 : (k + 1) * 768]
            grad_act = nt(dy, down_ref[j, at, :])
            square = u * u
            t = jnp.tanh(u * (scale + scale * 0.044715 * square))
            half = 0.5 + 0.5 * t
            g = u * half
            slope = half + g * (1.0 - t) * (scale + 3 * scale * 0.044715 * square)
            g = g.astype(BF)
            du = (grad_act * slope).astype(BF)
            rows_ref[6 + k : 7 + k, :] = jnp.sum(du.astype(F32), axis=0, keepdims=True)
            out = out + jnp.dot(g, down_ref[j, at, :], preferred_element_type=F32)
            dh2 = dh2 + nt(du, up_ref[j, :, at])

            hidden[j, 0, :, at] = g
            hidden[j, 1, :, at] = du

    for copy in own + sent[:2]:
        copy.start()
    result_ref[...] = out.astype(BF)
    rows_ref[4:5, :] = jnp.sum(dh2 * xhat, axis=0, keepdims=True)
    rows_ref[5:6, :] = jnp.sum(dh2, axis=0, keepdims=True)
    grad = dh2 * gain_ref[...]
    inner = grad - jnp.mean(grad, axis=-1, keepdims=True) - xhat * jnp.mean(grad * xhat, axis=-1, keepdims=True)
    mid_grad = dy.astype(F32) + norm * inner
    mid_grad_ref[...] = mid_grad
    da = mid_grad.astype(BF)
    da_ref[...] = da
    send_scr[:, 768:1536] = da
    sent[2].start()
    rows_ref[2:3, :] = jnp.sum(da.astype(F32), axis=0, keepdims=True)
    do = nt(da, w_out_ref[...]).astype(BF)
    for e, ref in enumerate((d0, d1, d2, d3)):
        ref[...] = do[:, e * 192 : (e + 1) * 192]
    for copy in own + sent:
        copy.wait()


def feed(place, heads, x, dy, w_out, w_up, w_down, b_out, gain, shift, b_up, b_down):
    tile = whole((256, 768))
    row = whole((1, 768))
    part = whole((256, 192))
    return pl.pallas_call(
        feed_kernel,
        grid_spec=pltpu.PrefetchScalarGridSpec(
            num_scalar_prefetch=1,
            grid=(1,),
            in_specs=[part] * 4
            + [
                tile,
                tile,
                whole((768, 768)),
                pl.BlockSpec(memory_space=pl.ANY),
                pl.BlockSpec(memory_space=pl.ANY),
                row,
                row,
                row,
                whole((1, 3072)),
                row,
            ],
            out_specs=[tile, tile]
            + [part] * 4
            + [pl.BlockSpec(memory_space=pl.ANY)] * 2
            + [tile, tile, whole((256, 384)), pl.BlockSpec(memory_space=pl.ANY), whole((64, 768))],
            scratch_shapes=[
                pltpu.VMEM((256, 768), BF),
                pltpu.VMEM((2, 768, 1536), BF),
                pltpu.VMEM((2, 1536, 768), BF),
                pltpu.VMEM((2, 2, 256, 1536), BF),
                pltpu.VMEM((256, 1920), BF),
                pltpu.SemaphoreType.DMA((2,)),
                pltpu.SemaphoreType.DMA((2,)),
                pltpu.SemaphoreType.DMA((2,)),
                pltpu.SemaphoreType.DMA((3,)),
            ],
        ),
        out_shape=[
            jax.ShapeDtypeStruct((256, 768), BF),
            jax.ShapeDtypeStruct((256, 768), F32),
        ]
        + [jax.ShapeDtypeStruct((256, 192), BF)] * 4
        + [jax.ShapeDtypeStruct((256, width), BF) for width in (1536, 1536, 768, 768, 384, 4992)]
        + [jax.ShapeDtypeStruct((64, 768), F32)],
        compiler_params=pltpu.CompilerParams(vmem_limit_bytes=60 * MIB),
        cost_estimate=COST,
        name="feed",
    )(
        place,
        *heads,
        x,
        dy,
        w_out,
        w_up,
        w_down,
        b_out.reshape(1, 768),
        gain.reshape(1, 768),
        shift.reshape(1, 768),
        b_up.reshape(1, 3072),
        b_down.reshape(1, 768),
    )


def both(own, other):
    return jnp.concatenate([own, other], axis=0)


def weights_kernel(info, g, dy, du, h2, at, da, received, dy2, b0, b1, b2, b3, out_scr, slot_scr, sem):
    dy_both = both(dy[...], dy2[...])
    out_scr[...] = tn(both(at[...], received[:, 4608:4992]), both(da[...], received[:, 3840:4608]))
    zero = jnp.zeros((8, 768), F32)
    copies = []
    for i, ref in enumerate((b0, b1, b2, b3)):
        a1 = lax.rem(info[1] + i, 4)
        cut = pl.ds(pl.multiple_of(a1 * 384, 384), 384)
        down = tn(both(g[:, cut], received[:, cut]), dy_both).astype(BF)
        first = pl.multiple_of(lax.rem(a1, 2) * 384, 384)
        left = both(h2[:, pl.ds(first, 384)], received[:, pl.ds(pl.multiple_of(3072 + first, 384), 384)])
        second = pl.multiple_of(a1 // 2 * 768, 768)
        right = both(du[:, pl.ds(second, 768)], received[:, pl.ds(pl.multiple_of(1536 + second, 768), 768)])
        up = tn(left, right).astype(BF)
        for a2 in range(4):
            slot_scr[i, a2, 0:96, :] = down[a2 * 96 : (a2 + 1) * 96]
            slot_scr[i, a2, 96:192, :] = up[a2 * 96 : (a2 + 1) * 96]
            rest = out_scr[pl.ds(pl.multiple_of(a1 * 96 + a2 * 24, 8), 24), :]
            slot_scr[i, a2, 192:224, :] = jnp.concatenate([rest, zero], axis=0).astype(BF)
        copies.append(pltpu.make_async_copy(slot_scr.at[i], ref, sem.at[i]))
        copies[-1].start()
    for copy in copies:
        copy.wait()


def weights(info, g, dy, du, h2, at, da, received, dy_received):
    operands = (g, dy, du, h2, at, da, received, dy_received)
    return pl.pallas_call(
        weights_kernel,
        grid_spec=pltpu.PrefetchScalarGridSpec(
            num_scalar_prefetch=1,
            grid=(1,),
            in_specs=[whole(array.shape) for array in operands],
            out_specs=[pl.BlockSpec(memory_space=pl.ANY)] * 4,
            scratch_shapes=[
                pltpu.VMEM((384, 768), F32),
                pltpu.VMEM((4, 4, 224, 768), BF),
                pltpu.SemaphoreType.DMA((4,)),
            ],
        ),
        out_shape=[jax.ShapeDtypeStruct((4, 224, 768), BF)] * 4,
        compiler_params=pltpu.CompilerParams(vmem_limit_bytes=60 * MIB),
        cost_estimate=COST,
        name="weights",
    )(info, *operands)


def add_kernel(info, p0, p1, p2, p3, *outs):
    total = p0[0].astype(F32) + p1[0].astype(F32) + p2[0].astype(F32) + p3[0].astype(F32)
    for i, out in enumerate(outs):
        @pl.when(pl.program_id(0) == i)
        def _():
            out[...] = total.astype(BF)


def add_pieces(info, pieces):
    spec = pl.BlockSpec((1, 224, 768), lambda i, info: (lax.rem(info[2] + i, 4), 0, 0))
    return pl.pallas_call(
        add_kernel,
        grid_spec=pltpu.PrefetchScalarGridSpec(
            num_scalar_prefetch=1, grid=(4,), in_specs=[spec] * 4, out_specs=[whole((224, 768))] * 4
        ),
        out_shape=[jax.ShapeDtypeStruct((224, 768), BF)] * 4,
        compiler_params=pltpu.CompilerParams(vmem_limit_bytes=24 * MIB),
        cost_estimate=COST,
        name="add_pieces",
    )(info, *pieces)


def place_kernel(counts, info, *refs):
    down, up, out = refs[-3:]
    for i, count in enumerate(counts):
        @pl.when(pl.program_id(0) == i)
        def _():
            base = sum(counts[:i])
            for r2 in range(4):
                a2 = lax.rem(info[2] + r2, 4)
                rows = refs[base + r2 * count // 4][r2 % (4 // count)].astype(F32)
                at = pl.multiple_of(a2 * 96, 96)
                down[pl.ds(at, 96), :] = rows[0:96]
                up[pl.ds(at, 96), :] = rows[96:192]
                out[pl.ds(pl.multiple_of(a2 * 24, 8), 24), :] = rows[192:216]


def place_weights(info, slots, pieces, others=()):
    arrays = [array for piece in pieces for array in piece]

    def first(i, info):
        slot_at = slots[0]
        for j, other in enumerate(slots):
            slot_at = jnp.where(i == j, other, slot_at)
        return lax.rem(info[1] + slot_at, 4)

    def by_rows(i, info):
        return (info[0] * 4 + first(i, info), 0)

    def by_columns(i, info):
        return (lax.rem(first(i, info), 2), info[0] * 2 + first(i, info) // 2)

    return pl.pallas_call(
        functools.partial(place_kernel, [len(piece) for piece in pieces]),
        grid_spec=pltpu.PrefetchScalarGridSpec(
            num_scalar_prefetch=1,
            grid=(len(pieces),),
            in_specs=[whole(array.shape) for array in arrays] + [pl.BlockSpec(memory_space=pl.ANY)] * len(others),
            out_specs=[pl.BlockSpec((384, 768), by_rows), pl.BlockSpec((384, 768), by_columns), pl.BlockSpec((96, 768), by_rows)],
        ),
        out_shape=[
            jax.ShapeDtypeStruct((3072, 768), F32),
            jax.ShapeDtypeStruct((768, 3072), F32),
            jax.ShapeDtypeStruct((768, 768), F32),
        ],
        input_output_aliases={1 + len(arrays) + i: i for i in range(len(others))},
        compiler_params=pltpu.CompilerParams(vmem_limit_bytes=32 * MIB),
        cost_estimate=COST,
        name="place_weights",
    )(info, *arrays, *others)


def moment_kernel(place, xhat_ref, dq_ref, near0_ref, near1_ref, far_ref, w_ref, gain_ref, shift_ref, rows_ref, p0, p1, p2, p3, give_ref, keep_ref, dqkv_ref):
    step = pl.program_id(0)

    @pl.when(step == 0)
    def _():
        for i, piece in enumerate((p0, p1, p2, p3)):
            dkv = near0_ref[i].astype(F32) + near1_ref[i].astype(F32) + far_ref[i].astype(F32)
            piece[:, :192] = dq_ref[i]
            piece[:, 192:] = dkv.astype(BF)
            dqkv_ref[i * 256 : (i + 1) * 256, :] = piece[...]

    dqkv = dqkv_ref[...]
    moment = tn(xhat_ref[...], dqkv)
    total = jnp.sum(dqkv.astype(F32), axis=0, keepdims=True)
    w = w_ref[0].astype(F32)
    gain = jnp.sum(w * moment, axis=1, keepdims=True)
    shift = jnp.sum(w * total, axis=1, keepdims=True)
    gw = (gain_ref[...] * moment + shift_ref[...] * total).astype(BF)
    lane = lax.broadcasted_iota(jnp.int32, (384, 64), 1)
    here = lax.rem(place[2] + 1 + step, 2)
    ends = jnp.concatenate([total[:, 384:], jnp.zeros((1, 192), F32)], axis=1)
    total_here = jnp.where(here == 0, total[:, :384], ends)
    row = lax.broadcasted_iota(jnp.int32, (64, 384), 0)
    vectors = jnp.where(row == 10, total_here, rows_ref[...]).T
    vectors = jnp.where(lane == 0, gain, jnp.where(lane == 1, shift, vectors)).astype(BF)

    def put(ref):
        ref[:, :576] = gw
        ref[:, 576:640] = vectors

    @pl.when(step == 0)
    def _():
        put(give_ref)

    @pl.when(step == 1)
    def _():
        put(keep_ref)


def moments(place, xhat, dq, near0, near1, far, w_groups, gain, shift, rows):
    def half(i, place):
        return lax.rem(place[2] + 1 + i, 2)

    return pl.pallas_call(
        moment_kernel,
        grid_spec=pltpu.PrefetchScalarGridSpec(
            num_scalar_prefetch=1,
            grid=(2,),
            in_specs=[
                pl.BlockSpec((1024, 384), lambda i, place: (0, half(i, place))),
                whole((4, 256, 192)),
                whole((4, 256, 384)),
                whole((4, 256, 384)),
                whole((4, 256, 384)),
                pl.BlockSpec((1, 384, 576), lambda i, place: (place[0], half(i, place), 0)),
                pl.BlockSpec((384, 1), lambda i, place: (half(i, place), 0)),
                pl.BlockSpec((384, 1), lambda i, place: (half(i, place), 0)),
                pl.BlockSpec((64, 384), lambda i, place: (0, half(i, place))),
            ],
            out_specs=[whole((256, 576))] * 4 + [whole((384, 640))] * 2,
            scratch_shapes=[pltpu.VMEM((1024, 576), BF)],
        ),
        out_shape=[jax.ShapeDtypeStruct((256, 576), BF)] * 4 + [jax.ShapeDtypeStruct((384, 640), BF)] * 2,
        compiler_params=pltpu.CompilerParams(vmem_limit_bytes=40 * MIB),
        cost_estimate=COST,
        name="moments",
    )(place, xhat.reshape(1024, 768), dq, near0, near1, far, w_groups, gain.reshape(768, 1), shift.reshape(768, 1), rows)


def regroup_kernel(w_ref, out_ref):
    for group in range(4):
        @pl.when(pl.program_id(0) == group)
        def _():
            at = group * 192
            out_ref[0, :, :192] = w_ref[:, at : at + 192]
            for h in range(3):
                for t in range(2):
                    to = 192 + h * 128 + t * HD
                    first = 768 * (t + 1) + at + h * HD
                    out_ref[0, :, to : to + HD] = w_ref[:, first : first + HD]


def regroup(w):
    return pl.pallas_call(
        regroup_kernel,
        grid=(4,),
        in_specs=[pl.BlockSpec((768, 2304), lambda i: (0, 0))],
        out_specs=pl.BlockSpec((1, 768, 576), lambda i: (i, 0, 0)),
        out_shape=jax.ShapeDtypeStruct((4, 768, 576), BF),
        compiler_params=pltpu.CompilerParams(vmem_limit_bytes=24 * MIB),
        cost_estimate=COST,
        name="regroup",
    )(w)


def finish_kernel(place, p0, p1, p2, p3, w_ref, x_ref, gain_ref, mid_ref, out_ref, acc_ref):
    e = pl.program_id(0)
    for i, piece in enumerate((p0, p1, p2, p3)):
        @pl.when(e == i)
        def _():
            part = nt(piece[...], w_ref[0])
            acc_ref[...] = part if i == 0 else acc_ref[...] + part

    @pl.when(e == 3)
    def _():
        x = x_ref[...].astype(F32)
        center = x - jnp.mean(x, axis=-1, keepdims=True)
        scale = lax.rsqrt(jnp.mean(center * center, axis=-1, keepdims=True) + 1e-05)
        xhat = center * scale
        grad = acc_ref[...] * gain_ref[...]
        inner = grad - jnp.mean(grad, axis=-1, keepdims=True) - xhat * jnp.mean(grad * xhat, axis=-1, keepdims=True)
        out_ref[...] = mid_ref[...] + scale * inner


def finish(place, pieces, w_groups, x, gain, middle):
    return pl.pallas_call(
        finish_kernel,
        grid_spec=pltpu.PrefetchScalarGridSpec(
            num_scalar_prefetch=1,
            grid=(4,),
            in_specs=[whole((256, 576))] * 4
            + [
                pl.BlockSpec((1, 768, 576), lambda i, place: (lax.rem(place[0] + i, 4), 0, 0)),
                whole((256, 768)),
                whole((1, 768)),
                whole((256, 768)),
            ],
            out_specs=whole((256, 768)),
            scratch_shapes=[pltpu.VMEM((256, 768), F32)],
        ),
        out_shape=jax.ShapeDtypeStruct((256, 768), F32),
        compiler_params=pltpu.CompilerParams(vmem_limit_bytes=24 * MIB),
        cost_estimate=COST,
        name="finish",
    )(place, *pieces, w_groups, x, gain.reshape(1, 768), middle)


def join_kernel(info, p0, p1, p2, p3, *refs):
    out_ref, rows_ref, cols_ref = refs[-3:]

    def put(rows, part, group):
        to = pl.ds(pl.multiple_of(part * 96, 96), 96)
        rows = rows.astype(F32)
        out_ref[to, group * 192 : (group + 1) * 192] = rows[:, :192]
        for h in range(3):
            for t in range(2):
                start = 192 + h * 128 + t * HD
                column = 768 * (t + 1) + group * 192 + h * HD
                out_ref[to, column : column + HD] = rows[:, start : start + HD]
        cols_ref[group, to, :] = rows[:, 512:640]

    for r1, piece in enumerate((p0, p1, p2, p3)):
        first = lax.rem(info[1] + r1, 4)

        @pl.when(info[0] == 0)
        def _():
            for group in range(4):
                put(piece[lax.rem(group + 4 - info[2], 4)], first, group)

        for group in range(4):
            @pl.when(jnp.logical_and(info[0] == 1, first == group))
            def _():
                for r2 in range(4):
                    put(piece[r2], lax.rem(info[2] + r2, 4), group)

    turned = [cols_ref[group].T for group in range(4)]
    rows_ref[:16, :] = (turned[0] + turned[1] + turned[2] + turned[3])[64:80]
    for group in range(4):
        rows_ref[16 + group : 17 + group, :] = turned[group][74:75]
    rows_ref[20:, :] = jnp.zeros((4, 384), F32)


def join_qkv(info, pieces, others=()):
    return pl.pallas_call(
        join_kernel,
        grid_spec=pltpu.PrefetchScalarGridSpec(
            num_scalar_prefetch=1,
            grid=(1,),
            in_specs=[whole((4, 96, 640))] * 4 + [pl.BlockSpec(memory_space=pl.ANY)] * len(others),
            out_specs=[
                pl.BlockSpec((384, 2304), lambda i, info: (info[0], 0)),
                pl.BlockSpec((24, 384), lambda i, info: (0, info[0])),
            ],
            scratch_shapes=[pltpu.VMEM((4, 384, 128), F32)],
        ),
        out_shape=[jax.ShapeDtypeStruct((768, 2304), F32), jax.ShapeDtypeStruct((24, 768), F32)],
        input_output_aliases={5 + i: i for i in range(len(others))},
        compiler_params=pltpu.CompilerParams(vmem_limit_bytes=40 * MIB),
        cost_estimate=COST,
        name="join_qkv",
    )(info, *pieces, *others)


def region(always, work, *operands):
    shapes = jax.eval_shape(work, *operands)
    empty = jax.tree.map(lambda shape: jnp.zeros(shape.shape, shape.dtype), shapes)
    return lax.cond(always, work, lambda *args: empty, *operands)


def layer_norm(values, gain, shift):
    center = values - jnp.mean(values, axis=-1, keepdims=True)
    spread = jnp.mean(center * center, axis=-1, keepdims=True)
    return center * lax.rsqrt(spread + 1e-05) * gain + shift


def shards(
    tokens,
    cotangent,
    ln1_gain,
    ln1_shift,
    w_qkv,
    b_query,
    b_value,
    w_out,
    b_out,
    ln2_gain,
    ln2_shift,
    w_up,
    b_up,
    w_down,
    b_down,
):
    seq, batch = lax.axis_index("seq"), lax.axis_index("batch")
    y, zh, c = seq // 4, lax.rem(seq // 2, 2), lax.rem(seq, 2)
    z, x = zh * 2 + batch // 4, lax.rem(batch, 4)
    always = seq + batch >= 0
    place = jnp.stack([y, zh, c, x]).astype(jnp.int32)
    info = jnp.stack([c, jnp.where(c == 0, x, y), jnp.where(c == 0, y, z)]).astype(jnp.int32)
    other_info = jnp.stack([1 - c, jnp.where(c == 0, y, x), jnp.where(c == 0, z, y)]).astype(jnp.int32)

    tokens = tokens[0]
    dy_low = cotangent[0]
    columns = [tokens] + fetch_all(tokens, "y") + [fetch(tokens, "z", 2)]
    dy_other = fetch(dy_low, "c", 1)

    def by_group(array):
        parts = array.reshape(1, 3, 4, 3, HD)
        query = parts[:, 0].transpose(1, 0, 2, 3).reshape(4, 1, 192)
        keys = parts[:, 1:].transpose(2, 0, 3, 1, 4).reshape(4, 1, 384)
        return jnp.concatenate([query, keys], axis=2)

    w_groups = regroup(w_qkv)
    bias_groups = by_group(jnp.concatenate([b_query, jnp.zeros_like(b_query), b_value]))
    w_out_turned = lax.dynamic_slice_in_dim(jnp.concatenate([w_out, w_out]), y * 192, 768, 0)

    prep_weights = (w_groups, bias_groups, ln1_gain.reshape(1, 768), ln1_shift.reshape(1, 768))
    *own, far_first = prep_call(prep_own_kernel, "prep_own", place, (tokens, columns[4]), prep_weights, lambda i: 0, 1, 1)
    xhat, q, kv = prep_call(prep_rest_kernel, "prep_rest", place, columns[1:4], prep_weights, lambda i: i + 1, 3, 0, own)
    far_rest = fetch(kv[1:], "z", 2)
    near = (kv, fetch(kv, "c", 1))
    far_near = (far_first, fetch(far_first, "c", 1))
    far = []

    def far_of(state):
        rest, *state = lax.optimization_barrier((far_rest, *state))
        far.extend([*far_near, rest, fetch(rest, "c", 1)])
        return state, far[2:]

    o, o32, lse = attend(place, q, (*near, *far_near), far_of)

    heads = [o[0]] + [fetch(o[4 - e], "y", e) for e in (1, 2, 3)]
    fed = feed(place, heads, tokens, dy_low, w_out_turned, w_up, w_down, b_out, ln2_gain, ln2_shift, b_up, b_down)
    result, grad_middle, *do, g, du, h2, da, attended, send, vectors = fed

    do_mine = [do[0]] + [fetch(do[4 - e], "y", e) for e in (1, 2, 3)]
    received = fetch(send, "c", 1)
    pieces = weights(info, g, dy_low, du, h2, attended, da, received, dy_other)

    def back_far(*do_mine):
        delta, dqt, far0, far1 = attend_back_far(place, q, do_mine, o32, lse, far)
        return delta, dqt, (far0.astype(F32) + fetch(far1, "c", 1).astype(F32)).astype(BF)

    def back_near(delta, dqt, *do_mine):
        dq, near0, near1 = attend_back_near(place, q, do_mine, lse, near, delta, dqt)
        return dq, near0, fetch(near1, "c", 1)

    def scatter_beside(pieces, *do_mine):
        received = [fetch(pieces[d], FIRST, 4 - d) for d in (1, 2, 3)]
        delta, dqt, far_sum = region(always, back_far, *do_mine)
        far_received = fetch(far_sum, "z", 2)
        dq, near0, near1 = region(always, back_near, delta, dqt, *do_mine)
        dq, *received = lax.optimization_barrier((dq, *received))
        pieces = add_pieces(info, [pieces[0]] + received)
        moved = [fetch(pieces[d], SECOND, 4 - d) for d in (1, 2, 3)]
        moved = moments(place, xhat, dq, near0, near1, far_received, w_groups, ln1_gain, ln1_shift, vectors), pieces[0], moved
        return moved

    (dqkv0, dqkv1, dqkv2, dqkv3, given, gw), own, received = region(always, scatter_beside, pieces, *do_mine)
    pieces = [own] + received

    def sum_rest(pieces, given, gw):
        chunk = sum(p.astype(F32) for p in pieces).astype(BF)
        gw = (gw.astype(F32) + fetch(given, "c", 1).astype(F32)).astype(BF)
        return sum_pairs(chunk, REST), halve(gw, KEYS, jnp.where(c == 0, x, z))

    def rows_beside(dqkv1, dqkv2, dqkv3, *operands):
        rows = fetch(dqkv3, "y", 1), fetch(dqkv2, "y", 2), fetch(dqkv1, "y", 3)
        return *rows, *region(always, sum_rest, *operands)

    *parts, chunk, gw = region(always, rows_beside, dqkv1, dqkv2, dqkv3, pieces, given, gw)

    def sum_keys(gw):
        return (sum_pairs(gw, REST),)

    def gather_second(chunk, gw):
        return jnp.stack([chunk] + fetch_all(chunk, SECOND)), *region(always, sum_keys, gw)

    chunk, gw = region(always, gather_second, chunk, gw)

    def finish_keys_rows(gw, *parts):
        gw = jnp.stack([gw] + fetch_all(gw, SECOND))
        return gw, finish(place, parts, w_groups, tokens, ln1_gain, grad_middle)

    def place_first(chunk):
        other = fetch(chunk, "c", 1)
        placed = place_weights(info, (0,), [(chunk,)])
        return place_weights(other_info, (0,), [(other,)], placed)

    def place_after(chunk, *operands):
        gw, grad_inputs = region(always, finish_keys_rows, *operands)
        gw, chunk = lax.optimization_barrier((gw, chunk))
        return gw, grad_inputs, *region(always, place_first, chunk)

    def gather_sides(chunk, *operands):
        return *fetch_sides(chunk, FIRST), *region(always, place_after, chunk, *operands)

    side1, side3, gw, grad_inputs, *placed = region(always, gather_sides, chunk, gw, dqkv0, *parts)

    def place_near(placed, *near):
        return place_weights(info, (1, 3), [(piece,) for piece in near], placed)

    def gather_far(placed, *near):
        others = [fetch(piece, "c", 1) for piece in near]
        return *fetch_halves(*near, FIRST), *others, *region(always, place_near, placed, *near)

    low, high, other1, other3, *placed = region(always, gather_far, placed, side1, side3)

    def place_more(low, high, placed, *others):
        far = fetch(low, "c", 1), fetch(high, "c", 1)
        placed = place_weights(other_info, (1, 3), [(piece,) for piece in others], placed)
        placed = place_weights(info, (2,), [(low, high)], placed)
        return place_weights(other_info, (2,), [far], placed)

    def gather_keys(gw, *operands):
        return *fetch_all(gw, FIRST), *region(always, place_more, *operands)

    key1, key2, key3, gw_down, gw_up, gw_out = region(always, gather_keys, gw, low, high, placed, other1, other3)
    keys = (gw, key1, key2, key3)
    other_keys = [fetch(piece, "c", 1) for piece in keys]
    joined = join_qkv(info, keys)
    gw_qkv, sums = join_qkv(other_info, other_keys, joined)
    return (
        result[None],
        grad_inputs[None],
        sums[0],
        sums[1],
        gw_qkv,
        sums[16:20, :192].reshape(768),
        sums[16:20, 192:576].reshape(4, 3, 2, HD)[:, :, 1].reshape(768),
        gw_out,
        sums[2],
        sums[4],
        sums[5],
        gw_up,
        sums[6:10].reshape(3072),
        gw_down,
        sums[3],
    )


def solution(mesh):
    split = P("batch", "seq", None)
    return jax.shard_map(
        shards,
        mesh=mesh,
        in_specs=(split, split) + (P(),) * 13,
        out_specs=(split, split) + (P(),) * 13,
        check_vma=False,
    )
```

```python
import functools

import jax
import jax.numpy as jnp
from jax import lax
from jax.experimental import pallas as pl
from jax.experimental.pallas import tpu as pltpu
from jax.sharding import PartitionSpec as P

HD = 64
LOG2E = 1.4426950408889634
BF = jnp.bfloat16
F32 = jnp.float32
MIB = 2**20
COST = pl.CostEstimate(flops=1000, bytes_accessed=1000, transcendentals=0)


def nt(left, right):
    return lax.dot_general(left, right, (((1,), (1,)), ((), ())), preferred_element_type=F32)


def tn(left, right):
    return lax.dot_general(left, right, (((0,), (0,)), ((), ())), preferred_element_type=F32)


def whole(shape):
    return pl.BlockSpec(shape, lambda i, *_: (0,) * len(shape))


def of_slot(shape):
    return pl.BlockSpec((1,) + shape, lambda i, *_: (i,) + (0,) * len(shape))


def causal(scores, other):
    keys = lax.broadcasted_iota(jnp.int32, scores.shape, 0)
    queries = lax.broadcasted_iota(jnp.int32, scores.shape, 1)
    return jnp.where(keys <= queries, scores, other)


def query_y(place):
    return lax.rem(place[0] + pl.program_id(0), 4)


def slot(place, y):
    return lax.rem(y + 4 - place[0], 4)


def softmax_step(q_ref, m_ref, l_ref, acc_ref, blocks, masks):
    scores = []
    for h in range(3):
        q = q_ref[0, :, h * HD : (h + 1) * HD]
        row = [nt(block[:, h * 128 : h * 128 + HD], q) * LOG2E for block in blocks]
        scores.append([mask(s, -1e30) if mask else s for s, mask in zip(row, masks)])
    probs = []
    for h in range(3):
        old = m_ref[0, h : h + 1, :]
        new = old
        for s in scores[h]:
            new = jnp.maximum(new, jnp.max(s, axis=0, keepdims=True))
        factor = jnp.exp2(old - new)
        m_ref[0, h : h + 1, :] = new
        row = [jnp.exp2(s - new) for s in scores[h]]
        l_ref[0, h : h + 1, :] = l_ref[0, h : h + 1, :] * factor + sum(jnp.sum(p, axis=0, keepdims=True) for p in row)
        probs.append((row, factor))
    for h in range(3):
        row, factor = probs[h]
        acc = acc_ref[0, h] * factor
        for block, p in zip(blocks, row):
            acc = acc + tn(block[:, h * 128 + HD : (h + 1) * 128], p.astype(BF))
        acc_ref[0, h] = acc


def attend_near_kernel(place, q_ref, kv0_ref, kv1_ref, first0_ref, first1_ref, m_ref, l_ref, acc_ref):
    own = pl.program_id(0)
    m_ref[...] = jnp.full(m_ref.shape, -1e30, F32)
    l_ref[...] = jnp.zeros(l_ref.shape, F32)
    acc_ref[...] = jnp.zeros(acc_ref.shape, F32)

    def beside(scores, other):
        return jnp.where(place[2] == 1, scores, other)

    softmax_step(q_ref, m_ref, l_ref, acc_ref, [kv0_ref[own], kv1_ref[own]], [causal, beside])

    @pl.when(place[0] < query_y(place) + place[1])
    def _():
        softmax_step(q_ref, m_ref, l_ref, acc_ref, [first0_ref[...], first1_ref[...]], [None, None])

    def body(y, carry):
        at = slot(place, y)
        softmax_step(q_ref, m_ref, l_ref, acc_ref, [kv0_ref[at], kv1_ref[at]], [None, None])
        return carry

    lax.fori_loop(0, query_y(place), body, 0)


def attend_far_kernel(place, q_ref, kv0_ref, kv1_ref, m_in, l_in, acc_in, o0, o1, o2, o3, o32_ref, lse_ref, m_ref, l_ref, acc_ref):
    m_ref[...] = m_in[...]
    l_ref[...] = l_in[...]
    acc_ref[...] = acc_in[...]

    def body(y, carry):
        @pl.when(y != place[0])
        def _():
            at = slot(place, y) - 1
            softmax_step(q_ref, m_ref, l_ref, acc_ref, [kv0_ref[at], kv1_ref[at]], [None, None])

        return carry

    lax.fori_loop(0, query_y(place) + place[1], body, 0)
    for h in range(3):
        o = (acc_ref[0, h] / l_ref[0, h : h + 1, :]).T
        o32_ref[0, :, h * HD : (h + 1) * HD] = o
        for i, ref in enumerate((o0, o1, o2, o3)):
            @pl.when(pl.program_id(0) == i)
            def _():
                ref[:, h * HD : (h + 1) * HD] = o.astype(BF)
    lse_ref[...] = m_ref[...] + jnp.log2(l_ref[...])


def attend(place, q, near, far_of):
    stats = [of_slot((3, 256)), of_slot((3, 256)), of_slot((3, HD, 256))]
    stat_shapes = [
        jax.ShapeDtypeStruct((4, 3, 256), F32),
        jax.ShapeDtypeStruct((4, 3, 256), F32),
        jax.ShapeDtypeStruct((4, 3, HD, 256), F32),
    ]
    keys = [whole((4, 256, 384)), whole((4, 256, 384)), whole((256, 384)), whole((256, 384))]
    far_keys = [whole((3, 256, 384)), whole((3, 256, 384))]
    state = pl.pallas_call(
        attend_near_kernel,
        grid_spec=pltpu.PrefetchScalarGridSpec(
            num_scalar_prefetch=1, grid=(4,), in_specs=[of_slot((256, 192))] + keys, out_specs=stats
        ),
        out_shape=stat_shapes,
        compiler_params=pltpu.CompilerParams(vmem_limit_bytes=32 * MIB),
        cost_estimate=COST,
        name="attend_near",
    )(place, q, *near)
    state, far = far_of(state)
    return pl.pallas_call(
        attend_far_kernel,
        grid_spec=pltpu.PrefetchScalarGridSpec(
            num_scalar_prefetch=1,
            grid=(4,),
            in_specs=[of_slot((256, 192))] + far_keys + stats,
            out_specs=[whole((256, 192))] * 4 + [of_slot((256, 192)), of_slot((3, 256))],
            scratch_shapes=[pltpu.VMEM((1, 3, 256), F32), pltpu.VMEM((1, 3, 256), F32), pltpu.VMEM((1, 3, HD, 256), F32)],
        ),
        out_shape=[jax.ShapeDtypeStruct((256, 192), BF)] * 4
        + [
            jax.ShapeDtypeStruct((4, 256, 192), F32),
            jax.ShapeDtypeStruct((4, 3, 256), F32),
        ],
        compiler_params=pltpu.CompilerParams(vmem_limit_bytes=32 * MIB),
        cost_estimate=COST,
        name="attend_far",
    )(place, q, *far, *state)


def grad_step(lse_ref, qdo_ref, delta_ref, dqt_ref, sums, blocks, at, masks):
    both = {}
    for h in range(3):
        for i, block in enumerate(blocks):
            both[h, i] = nt(block[:, h * 128 : (h + 1) * 128], qdo_ref[h])
    weights = {}
    for h in range(3):
        for i, mask in enumerate(masks):
            p = jnp.exp2(both[h, i][:, :256] * LOG2E - lse_ref[0, h : h + 1, :])
            if mask:
                p = mask(p, 0.0)
            ds = (p * (both[h, i][:, 256:] - delta_ref[h])).astype(BF)
            weights[h, i] = (ds, p.astype(BF))
    for h in range(3):
        dqt = dqt_ref[h]
        for i, block in enumerate(blocks):
            ds, p = weights[h, i]
            sums[i][at, :, h * 128 : (h + 1) * 128] += jnp.dot(
                jnp.concatenate([ds, p], axis=1), qdo_ref[h], preferred_element_type=F32
            )
            dqt = dqt + tn(block[:, h * 128 : h * 128 + HD], ds)
        dqt_ref[h] = dqt


def grad_start(q_ref, do_refs, delta_of, qdo_ref, delta_ref, sums):
    @pl.when(pl.program_id(0) == 0)
    def _():
        for total in sums:
            total[...] = jnp.zeros(total.shape, F32)

    zero = jnp.zeros((256, HD), BF)
    for i, do_ref in enumerate(do_refs):
        @pl.when(pl.program_id(0) == i)
        def _():
            for h in range(3):
                do = do_ref[:, h * HD : (h + 1) * HD]
                qdo_ref[h, :256, :] = jnp.concatenate([q_ref[0, :, h * HD : (h + 1) * HD], zero], axis=1)
                qdo_ref[h, 256:, :] = jnp.concatenate([zero, do], axis=1)
                delta_ref[h] = delta_of(h, do)


def grad_end(sums, outs):
    @pl.when(pl.program_id(0) == 3)
    def _():
        for total, out in zip(sums, outs):
            out[...] = total[...].astype(BF)


def grad_far_kernel(place, q_ref, do0, do1, do2, do3, o32_ref, lse_ref, first0_ref, first1_ref, kv0_ref, kv1_ref, delta_out, dqt_out, g0_ref, g1_ref, qdo_ref, delta_ref, dqt_ref, sum0_ref, sum1_ref):
    sums = [sum0_ref, sum1_ref]

    def delta_of(h, do):
        prod = do.astype(F32) * o32_ref[0, :, h * HD : (h + 1) * HD]
        return jnp.sum(prod.T, axis=0, keepdims=True)

    grad_start(q_ref, (do0, do1, do2, do3), delta_of, qdo_ref, delta_ref, sums)
    dqt_ref[...] = jnp.zeros(dqt_ref.shape, F32)

    @pl.when(place[0] < query_y(place) + place[1])
    def _():
        grad_step(lse_ref, qdo_ref, delta_ref, dqt_ref, sums, [first0_ref[...], first1_ref[...]], 0, [None, None])

    def body(y, carry):
        @pl.when(y != place[0])
        def _():
            at = slot(place, y)
            grad_step(lse_ref, qdo_ref, delta_ref, dqt_ref, sums, [kv0_ref[at - 1], kv1_ref[at - 1]], at, [None, None])

        return carry

    lax.fori_loop(0, query_y(place) + place[1], body, 0)
    for h in range(3):
        delta_out[0, h : h + 1, :] = delta_ref[h]
        dqt_out[0, h] = dqt_ref[h]
    grad_end(sums, [g0_ref, g1_ref])


def grad_near_kernel(place, q_ref, do0, do1, do2, do3, lse_ref, kv0_ref, kv1_ref, delta_in, dqt_in, dq_ref, g0_ref, g1_ref, qdo_ref, delta_ref, dqt_ref, sum0_ref, sum1_ref):
    own = pl.program_id(0)
    sums = [sum0_ref, sum1_ref]
    grad_start(q_ref, (do0, do1, do2, do3), lambda h, do: delta_in[0, h : h + 1, :], qdo_ref, delta_ref, sums)
    dqt_ref[...] = dqt_in[0]

    def beside(probs, other):
        return jnp.where(place[2] == 1, probs, other)

    grad_step(lse_ref, qdo_ref, delta_ref, dqt_ref, sums, [kv0_ref[own], kv1_ref[own]], own, [causal, beside])

    def body(y, carry):
        at = slot(place, y)
        grad_step(lse_ref, qdo_ref, delta_ref, dqt_ref, sums, [kv0_ref[at], kv1_ref[at]], at, [None, None])
        return carry

    lax.fori_loop(0, query_y(place), body, 0)
    for h in range(3):
        dq_ref[0, :, h * HD : (h + 1) * HD] = (dqt_ref[h].T * 0.125).astype(BF)
    grad_end(sums, [g0_ref, g1_ref])


GRAD_SCRATCH = [
    pltpu.VMEM((3, 512, 128), BF),
    pltpu.VMEM((3, 1, 256), F32),
    pltpu.VMEM((3, HD, 256), F32),
    pltpu.VMEM((4, 256, 384), F32),
    pltpu.VMEM((4, 256, 384), F32),
]


def attend_back_far(place, q, do, o32, lse, far):
    keys = [whole((4, 256, 384)), whole((4, 256, 384))]
    return pl.pallas_call(
        grad_far_kernel,
        grid_spec=pltpu.PrefetchScalarGridSpec(
            num_scalar_prefetch=1,
            grid=(4,),
            in_specs=[of_slot((256, 192))] + [whole((256, 192))] * 4 + [of_slot((256, 192)), of_slot((3, 256))] + [whole((256, 384))] * 2 + [whole((3, 256, 384))] * 2,
            out_specs=[of_slot((3, 256)), of_slot((3, HD, 256))] + keys,
            scratch_shapes=GRAD_SCRATCH,
        ),
        out_shape=[
            jax.ShapeDtypeStruct((4, 3, 256), F32),
            jax.ShapeDtypeStruct((4, 3, HD, 256), F32),
            jax.ShapeDtypeStruct((4, 256, 384), BF),
            jax.ShapeDtypeStruct((4, 256, 384), BF),
        ],
        compiler_params=pltpu.CompilerParams(vmem_limit_bytes=40 * MIB),
        cost_estimate=COST,
        name="attend_back_far",
    )(place, q, *do, o32, lse, *far)


def attend_back_near(place, q, do, lse, near, delta, dqt):
    keys = [whole((4, 256, 384)), whole((4, 256, 384))]
    return pl.pallas_call(
        grad_near_kernel,
        grid_spec=pltpu.PrefetchScalarGridSpec(
            num_scalar_prefetch=1,
            grid=(4,),
            in_specs=[of_slot((256, 192))] + [whole((256, 192))] * 4 + [of_slot((3, 256))] + keys + [of_slot((3, 256)), of_slot((3, HD, 256))],
            out_specs=[of_slot((256, 192))] + keys,
            scratch_shapes=GRAD_SCRATCH,
        ),
        out_shape=[
            jax.ShapeDtypeStruct((4, 256, 192), BF),
            jax.ShapeDtypeStruct((4, 256, 384), BF),
            jax.ShapeDtypeStruct((4, 256, 384), BF),
        ],
        compiler_params=pltpu.CompilerParams(vmem_limit_bytes=40 * MIB),
        cost_estimate=COST,
        name="attend_back_near",
    )(place, q, *do, lse, *near, delta, dqt)


def project(x_ref, w_ref, bias_ref, gain_ref, shift_ref):
    x = x_ref[...].astype(F32)
    center = x - jnp.mean(x, axis=-1, keepdims=True)
    spread = jnp.mean(center * center, axis=-1, keepdims=True)
    xhat = center * lax.rsqrt(spread + 1e-05)
    h1 = (xhat * gain_ref[...] + shift_ref[...]).astype(BF)
    qkv = jnp.dot(h1, w_ref[0], preferred_element_type=F32) + bias_ref[0]
    return xhat.astype(BF), qkv[:, :192].astype(BF) * jnp.asarray(0.125, BF), qkv[:, 192:].astype(BF)


def prep_own_kernel(place, x_ref, far_ref, w_ref, bias_ref, gain_ref, shift_ref, xhat_ref, q_ref, kv_ref, far_kv_ref):
    xhat_ref[0], q_ref[0], kv_ref[0] = project(x_ref, w_ref, bias_ref, gain_ref, shift_ref)
    far_kv_ref[...] = project(far_ref, w_ref, bias_ref, gain_ref, shift_ref)[2]


def prep_rest_kernel(place, x1_ref, x2_ref, x3_ref, w_ref, bias_ref, gain_ref, shift_ref, *refs):
    xhat_ref, q_ref, kv_ref = refs[-3:]
    for i, x_ref in enumerate((x1_ref, x2_ref, x3_ref)):
        @pl.when(pl.program_id(0) == i)
        def _():
            xhat_ref[0], q_ref[0], kv_ref[0] = project(x_ref, w_ref, bias_ref, gain_ref, shift_ref)


def prep_call(kernel, name, place, blocks, weights, slot_of, steps, extra, others=()):
    shapes = [(256, 768), (256, 192), (256, 384)]
    return pl.pallas_call(
        kernel,
        grid_spec=pltpu.PrefetchScalarGridSpec(
            num_scalar_prefetch=1,
            grid=(steps,),
            in_specs=[whole((256, 768))] * len(blocks)
            + [
                pl.BlockSpec((1, 768, 576), lambda i, place: (place[0], 0, 0)),
                pl.BlockSpec((1, 1, 576), lambda i, place: (place[0], 0, 0)),
                whole((1, 768)),
                whole((1, 768)),
            ]
            + [pl.BlockSpec(memory_space=pl.ANY)] * len(others),
            out_specs=[pl.BlockSpec((1,) + shape, lambda i, place: (slot_of(i), 0, 0)) for shape in shapes] + [whole((256, 384))] * extra,
        ),
        out_shape=[jax.ShapeDtypeStruct((4,) + shape, BF) for shape in shapes] + [jax.ShapeDtypeStruct((256, 384), BF)] * extra,
        input_output_aliases={5 + len(blocks) + i: i for i in range(len(others))},
        compiler_params=pltpu.CompilerParams(vmem_limit_bytes=24 * MIB),
        cost_estimate=COST,
        name=name,
    )(place, *blocks, *weights, *others)


FIRST = ("x", "y")
SECOND = ("y", "z")
REST = ("z", "x")
KEYS = ("x", "z")


def shift_pairs(axes, step, pairwise=False):
    pairs = []
    for s in range(16):
        for b in range(8):
            at = {"y": s // 4, "z": (s // 2 % 2) * 2 + b // 4, "c": s % 2, "x": b % 4}
            axis = axes[at["c"]]
            at[axis] = at[axis] ^ step if pairwise else (at[axis] + step) % (2 if axis == "c" else 4)
            source = (at["y"] * 4 + (at["z"] // 2) * 2 + at["c"]) * 8 + (at["z"] % 2) * 4 + at["x"]
            pairs.append((source, s * 8 + b))
    return pairs


def fetch(array, axes, step):
    if isinstance(axes, str):
        axes = (axes, axes)
    return lax.ppermute(array, ("seq", "batch"), shift_pairs(axes, step))


def fetch_all(array, axes):
    return [fetch(array, axes, step) for step in (1, 2, 3)]


def roll_slots(pieces, index):
    count = len(pieces)
    stacked = jnp.stack(pieces + pieces[:-1])
    return lax.dynamic_slice_in_dim(stacked, lax.rem(count - index, count), count, 0)


def sum_pairs(array, axes):
    for step in (2, 1):
        array = (array.astype(F32) + fetch_pair(array, axes, step).astype(F32)).astype(array.dtype)
    return array


def halve(array, axes, index):
    for step in (2, 1):
        parts = array.reshape(2, -1, *array.shape[1:])
        side = lax.rem(index // step, 2)
        kept = lax.dynamic_index_in_dim(parts, side, 0, keepdims=False)
        other = fetch_pair(lax.dynamic_index_in_dim(parts, 1 - side, 0, keepdims=False), axes, step)
        array = (kept.astype(F32) + other.astype(F32)).astype(array.dtype)
    return array


def fetch_sides(array, axes):
    return fetch(array, axes, 1), fetch(array, axes, 3)


def fetch_halves(side1, side3, axes):
    half = side1.shape[0] // 2
    return fetch(side1[:half], axes, 1), fetch(side3[half:], axes, 3)


def fetch_pair(array, axes, step):
    if isinstance(axes, str):
        axes = (axes, axes)
    return lax.ppermute(array, ("seq", "batch"), shift_pairs(axes, step, True))


def all_gather(array, axes, index):
    return roll_slots([array] + fetch_all(array, axes), index)


def feed_kernel(place, a0, a1, a2, a3, x_ref, dy_ref, w_out_ref, w_up_hbm, w_down_hbm, b_out_ref, gain_ref, shift_ref, b_up_ref, b_down_ref, result_ref, mid_grad_ref, d0, d1, d2, d3, g_ref, du_ref, h2_ref, da_ref, at_ref, send_ref, rows_ref, turned_ref, up_ref, down_ref, hidden, send_scr, up_sem, down_sem, own_sem, send_sem):
    core = place[2]
    copies = []
    for j in range(2):
        part = pl.ds(j * 1536, 1536)
        copies.append(pltpu.make_async_copy(w_up_hbm.at[:, part], up_ref.at[j], up_sem.at[j]))
        copies.append(pltpu.make_async_copy(w_down_hbm.at[part, :], down_ref.at[j], down_sem.at[j]))
    for copy in copies:
        copy.start()
    own, sent = [], []
    for k, ref in enumerate((g_ref, du_ref)):
        own.append(pltpu.make_async_copy(hidden.at[core, k], ref, own_sem.at[k]))
        sent.append(pltpu.make_async_copy(hidden.at[1 - core, k], send_ref.at[:, pl.ds(k * 1536, 1536)], send_sem.at[k]))
    sent.append(pltpu.make_async_copy(send_scr, send_ref.at[:, pl.ds(3072, 1920)], send_sem.at[2]))

    for e, ref in enumerate((a0, a1, a2, a3)):
        turned_ref[:, e * 192 : (e + 1) * 192] = ref[...]
        for group in range(4):
            @pl.when(lax.rem(place[0] + e, 4) == group)
            def _():
                at = group % 2 * 192

                @pl.when(core == group // 2)
                def _():
                    at_ref[:, at : at + 192] = ref[...]

                @pl.when(core != group // 2)
                def _():
                    send_scr[:, 1536 + at : 1728 + at] = ref[...]

    dy = dy_ref[...]
    mid = x_ref[...].astype(F32) + jnp.dot(turned_ref[...], w_out_ref[...], preferred_element_type=F32) + b_out_ref[...]
    center = mid - jnp.mean(mid, axis=-1, keepdims=True)
    norm = lax.rsqrt(jnp.mean(center * center, axis=-1, keepdims=True) + 1e-05)
    xhat = center * norm
    h2 = (xhat * gain_ref[...] + shift_ref[...]).astype(BF)
    h2_ref[...] = h2
    send_scr[:, 0:768] = h2
    rows_ref[...] = jnp.zeros(rows_ref.shape, F32)
    rows_ref[3:4, :] = jnp.sum(dy.astype(F32), axis=0, keepdims=True)

    out = mid + b_down_ref[...]
    dh2 = jnp.zeros((256, 768), F32)
    scale = 0.7978845608028654
    for j in range(2):
        copies[2 * j].wait()
        copies[2 * j + 1].wait()
        for i in range(2):
            k = 2 * j + i
            at = slice(i * 768, (i + 1) * 768)
            u = jnp.dot(h2, up_ref[j, :, at], preferred_element_type=F32) + b_up_ref[:, k * 768 : (k + 1) * 768]
            grad_act = nt(dy, down_ref[j, at, :])
            square = u * u
            t = jnp.tanh(u * (scale + scale * 0.044715 * square))
            half = 0.5 + 0.5 * t
            g = u * half
            slope = half + g * (1.0 - t) * (scale + 3 * scale * 0.044715 * square)
            g = g.astype(BF)
            du = (grad_act * slope).astype(BF)
            rows_ref[6 + k : 7 + k, :] = jnp.sum(du.astype(F32), axis=0, keepdims=True)
            out = out + jnp.dot(g, down_ref[j, at, :], preferred_element_type=F32)
            dh2 = dh2 + nt(du, up_ref[j, :, at])

            hidden[j, 0, :, at] = g
            hidden[j, 1, :, at] = du

    for copy in own + sent[:2]:
        copy.start()
    result_ref[...] = out.astype(BF)
    rows_ref[4:5, :] = jnp.sum(dh2 * xhat, axis=0, keepdims=True)
    rows_ref[5:6, :] = jnp.sum(dh2, axis=0, keepdims=True)
    grad = dh2 * gain_ref[...]
    inner = grad - jnp.mean(grad, axis=-1, keepdims=True) - xhat * jnp.mean(grad * xhat, axis=-1, keepdims=True)
    mid_grad = dy.astype(F32) + norm * inner
    mid_grad_ref[...] = mid_grad
    da = mid_grad.astype(BF)
    da_ref[...] = da
    send_scr[:, 768:1536] = da
    sent[2].start()
    rows_ref[2:3, :] = jnp.sum(da.astype(F32), axis=0, keepdims=True)
    do = nt(da, w_out_ref[...]).astype(BF)
    for e, ref in enumerate((d0, d1, d2, d3)):
        ref[...] = do[:, e * 192 : (e + 1) * 192]
    for copy in own + sent:
        copy.wait()


def feed(place, heads, x, dy, w_out, w_up, w_down, b_out, gain, shift, b_up, b_down):
    tile = whole((256, 768))
    row = whole((1, 768))
    part = whole((256, 192))
    return pl.pallas_call(
        feed_kernel,
        grid_spec=pltpu.PrefetchScalarGridSpec(
            num_scalar_prefetch=1,
            grid=(1,),
            in_specs=[part] * 4
            + [
                tile,
                tile,
                whole((768, 768)),
                pl.BlockSpec(memory_space=pl.ANY),
                pl.BlockSpec(memory_space=pl.ANY),
                row,
                row,
                row,
                whole((1, 3072)),
                row,
            ],
            out_specs=[tile, tile]
            + [part] * 4
            + [pl.BlockSpec(memory_space=pl.ANY)] * 2
            + [tile, tile, whole((256, 384)), pl.BlockSpec(memory_space=pl.ANY), whole((64, 768))],
            scratch_shapes=[
                pltpu.VMEM((256, 768), BF),
                pltpu.VMEM((2, 768, 1536), BF),
                pltpu.VMEM((2, 1536, 768), BF),
                pltpu.VMEM((2, 2, 256, 1536), BF),
                pltpu.VMEM((256, 1920), BF),
                pltpu.SemaphoreType.DMA((2,)),
                pltpu.SemaphoreType.DMA((2,)),
                pltpu.SemaphoreType.DMA((2,)),
                pltpu.SemaphoreType.DMA((3,)),
            ],
        ),
        out_shape=[
            jax.ShapeDtypeStruct((256, 768), BF),
            jax.ShapeDtypeStruct((256, 768), F32),
        ]
        + [jax.ShapeDtypeStruct((256, 192), BF)] * 4
        + [jax.ShapeDtypeStruct((256, width), BF) for width in (1536, 1536, 768, 768, 384, 4992)]
        + [jax.ShapeDtypeStruct((64, 768), F32)],
        compiler_params=pltpu.CompilerParams(vmem_limit_bytes=60 * MIB),
        cost_estimate=COST,
        name="feed",
    )(
        place,
        *heads,
        x,
        dy,
        w_out,
        w_up,
        w_down,
        b_out.reshape(1, 768),
        gain.reshape(1, 768),
        shift.reshape(1, 768),
        b_up.reshape(1, 3072),
        b_down.reshape(1, 768),
    )


def both(own, other):
    return jnp.concatenate([own, other], axis=0)


def weights_kernel(info, g, dy, du, h2, at, da, received, dy2, b0, b1, b2, b3, out_scr, slot_scr, sem):
    dy_both = both(dy[...], dy2[...])
    out_scr[...] = tn(both(at[...], received[:, 4608:4992]), both(da[...], received[:, 3840:4608]))
    zero = jnp.zeros((8, 768), F32)
    copies = []
    for i, ref in enumerate((b0, b1, b2, b3)):
        a1 = lax.rem(info[1] + i, 4)
        cut = pl.ds(pl.multiple_of(a1 * 384, 384), 384)
        down = tn(both(g[:, cut], received[:, cut]), dy_both).astype(BF)
        first = pl.multiple_of(lax.rem(a1, 2) * 384, 384)
        left = both(h2[:, pl.ds(first, 384)], received[:, pl.ds(pl.multiple_of(3072 + first, 384), 384)])
        second = pl.multiple_of(a1 // 2 * 768, 768)
        right = both(du[:, pl.ds(second, 768)], received[:, pl.ds(pl.multiple_of(1536 + second, 768), 768)])
        up = tn(left, right).astype(BF)
        for a2 in range(4):
            slot_scr[i, a2, 0:96, :] = down[a2 * 96 : (a2 + 1) * 96]
            slot_scr[i, a2, 96:192, :] = up[a2 * 96 : (a2 + 1) * 96]
            rest = out_scr[pl.ds(pl.multiple_of(a1 * 96 + a2 * 24, 8), 24), :]
            slot_scr[i, a2, 192:224, :] = jnp.concatenate([rest, zero], axis=0).astype(BF)
        copies.append(pltpu.make_async_copy(slot_scr.at[i], ref, sem.at[i]))
        copies[-1].start()
    for copy in copies:
        copy.wait()


def weights(info, g, dy, du, h2, at, da, received, dy_received):
    operands = (g, dy, du, h2, at, da, received, dy_received)
    return pl.pallas_call(
        weights_kernel,
        grid_spec=pltpu.PrefetchScalarGridSpec(
            num_scalar_prefetch=1,
            grid=(1,),
            in_specs=[whole(array.shape) for array in operands],
            out_specs=[pl.BlockSpec(memory_space=pl.ANY)] * 4,
            scratch_shapes=[
                pltpu.VMEM((384, 768), F32),
                pltpu.VMEM((4, 4, 224, 768), BF),
                pltpu.SemaphoreType.DMA((4,)),
            ],
        ),
        out_shape=[jax.ShapeDtypeStruct((4, 224, 768), BF)] * 4,
        compiler_params=pltpu.CompilerParams(vmem_limit_bytes=60 * MIB),
        cost_estimate=COST,
        name="weights",
    )(info, *operands)


def add_kernel(info, p0, p1, p2, p3, *outs):
    total = p0[0].astype(F32) + p1[0].astype(F32) + p2[0].astype(F32) + p3[0].astype(F32)
    for i, out in enumerate(outs):
        @pl.when(pl.program_id(0) == i)
        def _():
            out[...] = total.astype(BF)


def add_pieces(info, pieces):
    spec = pl.BlockSpec((1, 224, 768), lambda i, info: (lax.rem(info[2] + i, 4), 0, 0))
    return pl.pallas_call(
        add_kernel,
        grid_spec=pltpu.PrefetchScalarGridSpec(
            num_scalar_prefetch=1, grid=(4,), in_specs=[spec] * 4, out_specs=[whole((224, 768))] * 4
        ),
        out_shape=[jax.ShapeDtypeStruct((224, 768), BF)] * 4,
        compiler_params=pltpu.CompilerParams(vmem_limit_bytes=24 * MIB),
        cost_estimate=COST,
        name="add_pieces",
    )(info, *pieces)


def place_kernel(counts, info, *refs):
    down, up, out = refs[-3:]
    for i, count in enumerate(counts):
        @pl.when(pl.program_id(0) == i)
        def _():
            base = sum(counts[:i])
            for r2 in range(4):
                a2 = lax.rem(info[2] + r2, 4)
                rows = refs[base + r2 * count // 4][r2 % (4 // count)].astype(F32)
                at = pl.multiple_of(a2 * 96, 96)
                down[pl.ds(at, 96), :] = rows[0:96]
                up[pl.ds(at, 96), :] = rows[96:192]
                out[pl.ds(pl.multiple_of(a2 * 24, 8), 24), :] = rows[192:216]


def place_weights(info, slots, pieces, others=()):
    arrays = [array for piece in pieces for array in piece]

    def first(i, info):
        slot_at = slots[0]
        for j, other in enumerate(slots):
            slot_at = jnp.where(i == j, other, slot_at)
        return lax.rem(info[1] + slot_at, 4)

    def by_rows(i, info):
        return (info[0] * 4 + first(i, info), 0)

    def by_columns(i, info):
        return (lax.rem(first(i, info), 2), info[0] * 2 + first(i, info) // 2)

    return pl.pallas_call(
        functools.partial(place_kernel, [len(piece) for piece in pieces]),
        grid_spec=pltpu.PrefetchScalarGridSpec(
            num_scalar_prefetch=1,
            grid=(len(pieces),),
            in_specs=[whole(array.shape) for array in arrays] + [pl.BlockSpec(memory_space=pl.ANY)] * len(others),
            out_specs=[pl.BlockSpec((384, 768), by_rows), pl.BlockSpec((384, 768), by_columns), pl.BlockSpec((96, 768), by_rows)],
        ),
        out_shape=[
            jax.ShapeDtypeStruct((3072, 768), F32),
            jax.ShapeDtypeStruct((768, 3072), F32),
            jax.ShapeDtypeStruct((768, 768), F32),
        ],
        input_output_aliases={1 + len(arrays) + i: i for i in range(len(others))},
        compiler_params=pltpu.CompilerParams(vmem_limit_bytes=32 * MIB),
        cost_estimate=COST,
        name="place_weights",
    )(info, *arrays, *others)


def moment_kernel(place, xhat_ref, dq_ref, near0_ref, near1_ref, far_ref, w_ref, gain_ref, shift_ref, rows_ref, p0, p1, p2, p3, give_ref, keep_ref, dqkv_ref):
    step = pl.program_id(0)

    @pl.when(step == 0)
    def _():
        for i, piece in enumerate((p0, p1, p2, p3)):
            dkv = near0_ref[i].astype(F32) + near1_ref[i].astype(F32) + far_ref[i].astype(F32)
            piece[:, :192] = dq_ref[i]
            piece[:, 192:] = dkv.astype(BF)
            dqkv_ref[i * 256 : (i + 1) * 256, :] = piece[...]

    dqkv = dqkv_ref[...]
    moment = tn(xhat_ref[...], dqkv)
    total = jnp.sum(dqkv.astype(F32), axis=0, keepdims=True)
    w = w_ref[0].astype(F32)
    gain = jnp.sum(w * moment, axis=1, keepdims=True)
    shift = jnp.sum(w * total, axis=1, keepdims=True)
    gw = (gain_ref[...] * moment + shift_ref[...] * total).astype(BF)
    lane = lax.broadcasted_iota(jnp.int32, (384, 64), 1)
    here = lax.rem(place[2] + 1 + step, 2)
    ends = jnp.concatenate([total[:, 384:], jnp.zeros((1, 192), F32)], axis=1)
    total_here = jnp.where(here == 0, total[:, :384], ends)
    row = lax.broadcasted_iota(jnp.int32, (64, 384), 0)
    vectors = jnp.where(row == 10, total_here, rows_ref[...]).T
    vectors = jnp.where(lane == 0, gain, jnp.where(lane == 1, shift, vectors)).astype(BF)

    def put(ref):
        ref[:, :576] = gw
        ref[:, 576:640] = vectors

    @pl.when(step == 0)
    def _():
        put(give_ref)

    @pl.when(step == 1)
    def _():
        put(keep_ref)


def moments(place, xhat, dq, near0, near1, far, w_groups, gain, shift, rows):
    def half(i, place):
        return lax.rem(place[2] + 1 + i, 2)

    return pl.pallas_call(
        moment_kernel,
        grid_spec=pltpu.PrefetchScalarGridSpec(
            num_scalar_prefetch=1,
            grid=(2,),
            in_specs=[
                pl.BlockSpec((1024, 384), lambda i, place: (0, half(i, place))),
                whole((4, 256, 192)),
                whole((4, 256, 384)),
                whole((4, 256, 384)),
                whole((4, 256, 384)),
                pl.BlockSpec((1, 384, 576), lambda i, place: (place[0], half(i, place), 0)),
                pl.BlockSpec((384, 1), lambda i, place: (half(i, place), 0)),
                pl.BlockSpec((384, 1), lambda i, place: (half(i, place), 0)),
                pl.BlockSpec((64, 384), lambda i, place: (0, half(i, place))),
            ],
            out_specs=[whole((256, 576))] * 4 + [whole((384, 640))] * 2,
            scratch_shapes=[pltpu.VMEM((1024, 576), BF)],
        ),
        out_shape=[jax.ShapeDtypeStruct((256, 576), BF)] * 4 + [jax.ShapeDtypeStruct((384, 640), BF)] * 2,
        compiler_params=pltpu.CompilerParams(vmem_limit_bytes=40 * MIB),
        cost_estimate=COST,
        name="moments",
    )(place, xhat.reshape(1024, 768), dq, near0, near1, far, w_groups, gain.reshape(768, 1), shift.reshape(768, 1), rows)


def regroup_kernel(w_ref, out_ref):
    for group in range(4):
        @pl.when(pl.program_id(0) == group)
        def _():
            at = group * 192
            out_ref[0, :, :192] = w_ref[:, at : at + 192]
            for h in range(3):
                for t in range(2):
                    to = 192 + h * 128 + t * HD
                    first = 768 * (t + 1) + at + h * HD
                    out_ref[0, :, to : to + HD] = w_ref[:, first : first + HD]


def regroup(w):
    return pl.pallas_call(
        regroup_kernel,
        grid=(4,),
        in_specs=[pl.BlockSpec((768, 2304), lambda i: (0, 0))],
        out_specs=pl.BlockSpec((1, 768, 576), lambda i: (i, 0, 0)),
        out_shape=jax.ShapeDtypeStruct((4, 768, 576), BF),
        compiler_params=pltpu.CompilerParams(vmem_limit_bytes=24 * MIB),
        cost_estimate=COST,
        name="regroup",
    )(w)


def finish_kernel(place, p0, p1, p2, p3, w_ref, x_ref, gain_ref, mid_ref, out_ref, acc_ref):
    e = pl.program_id(0)
    for i, piece in enumerate((p0, p1, p2, p3)):
        @pl.when(e == i)
        def _():
            part = nt(piece[...], w_ref[0])
            acc_ref[...] = part if i == 0 else acc_ref[...] + part

    @pl.when(e == 3)
    def _():
        x = x_ref[...].astype(F32)
        center = x - jnp.mean(x, axis=-1, keepdims=True)
        scale = lax.rsqrt(jnp.mean(center * center, axis=-1, keepdims=True) + 1e-05)
        xhat = center * scale
        grad = acc_ref[...] * gain_ref[...]
        inner = grad - jnp.mean(grad, axis=-1, keepdims=True) - xhat * jnp.mean(grad * xhat, axis=-1, keepdims=True)
        out_ref[...] = mid_ref[...] + scale * inner


def finish(place, pieces, w_groups, x, gain, middle):
    return pl.pallas_call(
        finish_kernel,
        grid_spec=pltpu.PrefetchScalarGridSpec(
            num_scalar_prefetch=1,
            grid=(4,),
            in_specs=[whole((256, 576))] * 4
            + [
                pl.BlockSpec((1, 768, 576), lambda i, place: (lax.rem(place[0] + i, 4), 0, 0)),
                whole((256, 768)),
                whole((1, 768)),
                whole((256, 768)),
            ],
            out_specs=whole((256, 768)),
            scratch_shapes=[pltpu.VMEM((256, 768), F32)],
        ),
        out_shape=jax.ShapeDtypeStruct((256, 768), F32),
        compiler_params=pltpu.CompilerParams(vmem_limit_bytes=24 * MIB),
        cost_estimate=COST,
        name="finish",
    )(place, *pieces, w_groups, x, gain.reshape(1, 768), middle)


def join_kernel(info, p0, p1, p2, p3, *refs):
    out_ref, rows_ref, cols_ref = refs[-3:]

    def put(rows, part, group):
        to = pl.ds(pl.multiple_of(part * 96, 96), 96)
        rows = rows.astype(F32)
        out_ref[to, group * 192 : (group + 1) * 192] = rows[:, :192]
        for h in range(3):
            for t in range(2):
                start = 192 + h * 128 + t * HD
                column = 768 * (t + 1) + group * 192 + h * HD
                out_ref[to, column : column + HD] = rows[:, start : start + HD]
        cols_ref[group, to, :] = rows[:, 512:640]

    for r1, piece in enumerate((p0, p1, p2, p3)):
        first = lax.rem(info[1] + r1, 4)

        @pl.when(info[0] == 0)
        def _():
            for group in range(4):
                put(piece[lax.rem(group + 4 - info[2], 4)], first, group)

        for group in range(4):
            @pl.when(jnp.logical_and(info[0] == 1, first == group))
            def _():
                for r2 in range(4):
                    put(piece[r2], lax.rem(info[2] + r2, 4), group)

    turned = [cols_ref[group].T for group in range(4)]
    rows_ref[:16, :] = (turned[0] + turned[1] + turned[2] + turned[3])[64:80]
    for group in range(4):
        rows_ref[16 + group : 17 + group, :] = turned[group][74:75]
    rows_ref[20:, :] = jnp.zeros((4, 384), F32)


def join_qkv(info, pieces, others=()):
    return pl.pallas_call(
        join_kernel,
        grid_spec=pltpu.PrefetchScalarGridSpec(
            num_scalar_prefetch=1,
            grid=(1,),
            in_specs=[whole((4, 96, 640))] * 4 + [pl.BlockSpec(memory_space=pl.ANY)] * len(others),
            out_specs=[
                pl.BlockSpec((384, 2304), lambda i, info: (info[0], 0)),
                pl.BlockSpec((24, 384), lambda i, info: (0, info[0])),
            ],
            scratch_shapes=[pltpu.VMEM((4, 384, 128), F32)],
        ),
        out_shape=[jax.ShapeDtypeStruct((768, 2304), F32), jax.ShapeDtypeStruct((24, 768), F32)],
        input_output_aliases={5 + i: i for i in range(len(others))},
        compiler_params=pltpu.CompilerParams(vmem_limit_bytes=40 * MIB),
        cost_estimate=COST,
        name="join_qkv",
    )(info, *pieces, *others)


def region(always, work, *operands):
    shapes = jax.eval_shape(work, *operands)
    empty = jax.tree.map(lambda shape: jnp.zeros(shape.shape, shape.dtype), shapes)
    return lax.cond(always, work, lambda *args: empty, *operands)


def layer_norm(values, gain, shift):
    center = values - jnp.mean(values, axis=-1, keepdims=True)
    spread = jnp.mean(center * center, axis=-1, keepdims=True)
    return center * lax.rsqrt(spread + 1e-05) * gain + shift


def shards(
    tokens,
    cotangent,
    ln1_gain,
    ln1_shift,
    w_qkv,
    b_query,
    b_value,
    w_out,
    b_out,
    ln2_gain,
    ln2_shift,
    w_up,
    b_up,
    w_down,
    b_down,
):
    seq, batch = lax.axis_index("seq"), lax.axis_index("batch")
    y, zh, c = seq // 4, lax.rem(seq // 2, 2), lax.rem(seq, 2)
    z, x = zh * 2 + batch // 4, lax.rem(batch, 4)
    always = seq + batch >= 0
    place = jnp.stack([y, zh, c, x]).astype(jnp.int32)
    info = jnp.stack([c, jnp.where(c == 0, x, y), jnp.where(c == 0, y, z)]).astype(jnp.int32)
    other_info = jnp.stack([1 - c, jnp.where(c == 0, y, x), jnp.where(c == 0, z, y)]).astype(jnp.int32)

    tokens = tokens[0]
    dy_low = cotangent[0]
    columns = [tokens] + fetch_all(tokens, "y") + [fetch(tokens, "z", 2)]
    dy_other = fetch(dy_low, "c", 1)

    def by_group(array):
        parts = array.reshape(1, 3, 4, 3, HD)
        query = parts[:, 0].transpose(1, 0, 2, 3).reshape(4, 1, 192)
        keys = parts[:, 1:].transpose(2, 0, 3, 1, 4).reshape(4, 1, 384)
        return jnp.concatenate([query, keys], axis=2)

    w_groups = regroup(w_qkv)
    bias_groups = by_group(jnp.concatenate([b_query, jnp.zeros_like(b_query), b_value]))
    w_out_turned = lax.dynamic_slice_in_dim(jnp.concatenate([w_out, w_out]), y * 192, 768, 0)

    prep_weights = (w_groups, bias_groups, ln1_gain.reshape(1, 768), ln1_shift.reshape(1, 768))
    *own, far_first = prep_call(prep_own_kernel, "prep_own", place, (tokens, columns[4]), prep_weights, lambda i: 0, 1, 1)
    xhat, q, kv = prep_call(prep_rest_kernel, "prep_rest", place, columns[1:4], prep_weights, lambda i: i + 1, 3, 0, own)
    far_rest = fetch(kv[1:], "z", 2)
    near = (kv, fetch(kv, "c", 1))
    far_near = (far_first, fetch(far_first, "c", 1))
    far = []

    def far_of(state):
        rest, *state = lax.optimization_barrier((far_rest, *state))
        far.extend([*far_near, rest, fetch(rest, "c", 1)])
        return state, far[2:]

    *o, o32, lse = attend(place, q, (*near, *far_near), far_of)

    heads = [o[0]] + [fetch(o[4 - e], "y", e) for e in (1, 2, 3)]
    fed = feed(place, heads, tokens, dy_low, w_out_turned, w_up, w_down, b_out, ln2_gain, ln2_shift, b_up, b_down)
    result, grad_middle, *do, g, du, h2, da, attended, send, vectors = fed

    do_mine = [do[0]] + [fetch(do[4 - e], "y", e) for e in (1, 2, 3)]
    received = fetch(send, "c", 1)
    pieces = weights(info, g, dy_low, du, h2, attended, da, received, dy_other)

    def back_far(*do_mine):
        delta, dqt, far0, far1 = attend_back_far(place, q, do_mine, o32, lse, far)
        return delta, dqt, (far0.astype(F32) + fetch(far1, "c", 1).astype(F32)).astype(BF)

    def back_near(delta, dqt, *do_mine):
        dq, near0, near1 = attend_back_near(place, q, do_mine, lse, near, delta, dqt)
        return dq, near0, fetch(near1, "c", 1)

    def scatter_beside(pieces, *do_mine):
        received = [fetch(pieces[d], FIRST, 4 - d) for d in (1, 2, 3)]
        delta, dqt, far_sum = region(always, back_far, *do_mine)
        far_received = fetch(far_sum, "z", 2)
        dq, near0, near1 = region(always, back_near, delta, dqt, *do_mine)
        dq, *received = lax.optimization_barrier((dq, *received))
        pieces = add_pieces(info, [pieces[0]] + received)
        moved = [fetch(pieces[d], SECOND, 4 - d) for d in (1, 2, 3)]
        moved = moments(place, xhat, dq, near0, near1, far_received, w_groups, ln1_gain, ln1_shift, vectors), pieces[0], moved
        return moved

    (dqkv0, dqkv1, dqkv2, dqkv3, given, gw), own, received = region(always, scatter_beside, pieces, *do_mine)
    pieces = [own] + received

    def sum_rest(pieces, given, gw):
        chunk = sum(p.astype(F32) for p in pieces).astype(BF)
        gw = (gw.astype(F32) + fetch(given, "c", 1).astype(F32)).astype(BF)
        return sum_pairs(chunk, REST), halve(gw, KEYS, jnp.where(c == 0, x, z))

    def rows_beside(dqkv1, dqkv2, dqkv3, *operands):
        rows = fetch(dqkv3, "y", 1), fetch(dqkv2, "y", 2), fetch(dqkv1, "y", 3)
        return *rows, *region(always, sum_rest, *operands)

    *parts, chunk, gw = region(always, rows_beside, dqkv1, dqkv2, dqkv3, pieces, given, gw)

    def sum_keys(gw):
        return (sum_pairs(gw, REST),)

    def gather_second(chunk, gw):
        return jnp.stack([chunk] + fetch_all(chunk, SECOND)), *region(always, sum_keys, gw)

    chunk, gw = region(always, gather_second, chunk, gw)

    def finish_keys_rows(gw, *parts):
        gw = jnp.stack([gw] + fetch_all(gw, SECOND))
        return gw, finish(place, parts, w_groups, tokens, ln1_gain, grad_middle)

    def place_first(chunk):
        other = fetch(chunk, "c", 1)
        placed = place_weights(info, (0,), [(chunk,)])
        return place_weights(other_info, (0,), [(other,)], placed)

    def place_after(chunk, *operands):
        gw, grad_inputs = region(always, finish_keys_rows, *operands)
        gw, chunk = lax.optimization_barrier((gw, chunk))
        return gw, grad_inputs, *region(always, place_first, chunk)

    def gather_sides(chunk, *operands):
        return *fetch_sides(chunk, FIRST), *region(always, place_after, chunk, *operands)

    side1, side3, gw, grad_inputs, *placed = region(always, gather_sides, chunk, gw, dqkv0, *parts)

    def place_near(placed, *near):
        return place_weights(info, (1, 3), [(piece,) for piece in near], placed)

    def gather_far(placed, *near):
        others = [fetch(piece, "c", 1) for piece in near]
        return *fetch_halves(*near, FIRST), *others, *region(always, place_near, placed, *near)

    low, high, other1, other3, *placed = region(always, gather_far, placed, side1, side3)

    def place_more(low, high, placed, *others):
        far = fetch(low, "c", 1), fetch(high, "c", 1)
        placed = place_weights(other_info, (1, 3), [(piece,) for piece in others], placed)
        placed = place_weights(info, (2,), [(low, high)], placed)
        return place_weights(other_info, (2,), [far], placed)

    def gather_keys(gw, *operands):
        return *fetch_all(gw, FIRST), *region(always, place_more, *operands)

    key1, key2, key3, gw_down, gw_up, gw_out = region(always, gather_keys, gw, low, high, placed, other1, other3)
    keys = (gw, key1, key2, key3)
    other_keys = [fetch(piece, "c", 1) for piece in keys]
    joined = join_qkv(info, keys)
    gw_qkv, sums = join_qkv(other_info, other_keys, joined)
    return (
        result[None],
        grad_inputs[None],
        sums[0],
        sums[1],
        gw_qkv,
        sums[16:20, :192].reshape(768),
        sums[16:20, 192:576].reshape(4, 3, 2, HD)[:, :, 1].reshape(768),
        gw_out,
        sums[2],
        sums[4],
        sums[5],
        gw_up,
        sums[6:10].reshape(3072),
        gw_down,
        sums[3],
    )


def solution(mesh):
    split = P("batch", "seq", None)
    return jax.shard_map(
        shards,
        mesh=mesh,
        in_specs=(split, split) + (P(),) * 13,
        out_specs=(split, split) + (P(),) * 13,
        check_vma=False,
    )
```
